128 devices in a mesh: wide: 16 (over x_hi, z, core), node: 8 (over x_lo, y).
Axes of the slice: x: 4 (x_hi: 2, x_lo: 2; x = x_hi * 2 + x_lo), y: 4, z: 4, core: 2. Of those that a mesh axis runs over, the one named last changes fastest.
Arguments:
- tokens: bfloat16 [12288, 3072], P('wide', 'node'), may hold values from -6 to 6
- target: bfloat16 [12288, 3072], P('wide', 'node'), may hold values from -6 to 6
- mod_table: bfloat16 [32, 3072], P(None, 'node'), may hold values from -1.5 to 1.5
- adv_table: float32 [32, 16], replicated, may hold values from 0.25 to 4
- w_up: bfloat16 [3072, 7168], P('wide', 'node'), may hold values from -0.109375 to 0.109375
- w_down_t: bfloat16 [3072, 7168], P('wide', 'node'), may hold values from -0.0625 to 0.0625
- bins: int32 [48], P('wide'), may hold values from 0 to 31
- groups: int32 [48], P('wide'), may hold values from 0 to 15
Outputs:
- grad_tokens: float32 [12288, 3072], P('wide', 'node')
- grad_up: float32 [3072, 7168], P('wide', 'node')
- grad_down: float32 [3072, 7168], P('wide', 'node')
The draws below stay inside these ranges and needn't reach their ends.
All inputs are finite; a program needn't handle non-finite values.
Results may differ from the reference program's by a relative error of at most 0.02.
Values may be sent and summed in bfloat16 or wider, within the bound.
A program may use at most 128 MiB of HBM per device.

```python
import math
import jax
import jax.numpy as jnp
from jax import lax

D = 3072
FF = 7168
SEQ = 256
MICRO = 3
BINS = 32
GROUPS = 16
SAMPLES = 48
TOKENS = 12288
N_WIDE = 16
N_NODE = 8


def set_ends(array, key, smallest, largest):
    longest = array.shape.index(max(array.shape))
    spots = []
    for shift in (0, 1):
        where = [jax.random.randint(jax.random.fold_in(key, axis), (), 0, length) for axis, length in enumerate(array.shape)]
        where[longest] = (where[longest] + shift) % array.shape[longest]
        spots.append(tuple(where))
    return array.at[spots[0]].set(smallest).at[spots[1]].set(largest)


def with_spikes(values, key, source, target, blocks, factor):
    owner, partner = [(jnp.arange(values.shape[position]) // (values.shape[position] // blocks)).reshape([-1 if axis == position else 1 for axis in range(values.ndim)]) for position in (source, target)]
    chosen = jax.random.permutation(key, blocks)[partner]
    strong = (owner == chosen) | (owner == (partner + blocks // 2) % blocks)
    return jnp.where(strong, factor * values, values)


def levels(rng, dims, shards, low, top_value):
    factor_of = 1.0
    for position, parts in shards:
        draws = jax.random.uniform(jax.random.fold_in(jax.random.fold_in(rng, 6), position), (parts,), jnp.float32, low / len(shards), top_value / len(shards))
        factor_of = factor_of * jnp.repeat(jnp.exp(draws), dims[position] // parts).reshape((-1,) + (1,) * (len(dims) - 1 - position))
    return factor_of


def noise(key, shape, deviation, most, split=(), held_as=jnp.bfloat16):
    level = levels(key, shape, split, -0.22, 0.18) if split else 1.0
    array = jax.random.normal(key, shape, jnp.float32) * deviation * level
    return jnp.minimum(jnp.maximum(array, -most), most).astype(held_as)


def bell_draw_with(own_key, extent, spread, reach, shards, heavy, kind=jnp.bfloat16):
    result = spread * jax.random.normal(own_key, extent, jnp.float32)
    if shards:
        result = result * levels(own_key, extent, shards, -0.22, 0.18)
    return jnp.clip(with_spikes(result, jax.random.fold_in(own_key, 3), *heavy), -reach, reach).astype(kind)


def setup_inputs(seed: int = 0) -> dict:
    key_list = jax.random.split(jax.random.key(seed), 9)
    return {
        "tokens": bell_draw_with(key_list[0], (TOKENS, D), 1.0, 6.0, ((0, 16), (1, 8)), (0, 1, 16, 2.0)),
        "target": noise(key_list[1], (TOKENS, D), 1.0, 6.0, ((0, 16), (1, 8))),
        "mod_table": noise(key_list[2], (BINS, D), 0.3, 1.5, ((1, 8),)),
        "adv_table": jnp.clip(jnp.exp(jax.random.uniform(key_list[3], (BINS, GROUPS), jnp.float32, math.log(0.25), math.log(4.0))), 0.25, 4.0),
        "w_up": noise(key_list[4], (D, FF), D ** -0.5, 0.109375, ((0, 16), (1, 8))),
        "w_down_t": noise(key_list[5], (D, FF), FF ** -0.5, 0.0625, ((0, 16), (1, 8))),
        "bins": set_ends(jax.random.randint(key_list[6], (SAMPLES,), 0, BINS), jax.random.fold_in(key_list[6], 1), 0, BINS - 1).astype(jnp.int32),
        "groups": set_ends(jax.random.randint(key_list[7], (SAMPLES,), 0, GROUPS), jax.random.fold_in(key_list[7], 1), 0, GROUPS - 1).astype(jnp.int32),
    }


def gelu_tanh(value):
    return jax.nn.gelu(value, approximate=True)

def reference(tokens, target, mod_table, adv_table, w_up, w_down_t, bins, groups):
    bin_tok = jnp.repeat(bins, SEQ)
    grp_tok = jnp.repeat(groups, SEQ)
    gain = 1.0 + mod_table.astype(jnp.float32)[bin_tok]
    modulated = (tokens.astype(jnp.float32) * gain).astype(jnp.bfloat16)
    pre = jnp.dot(modulated, w_up, preferred_element_type=jnp.float32)
    hidden = gelu_tanh(pre).astype(jnp.bfloat16)
    block = FF // N_NODE
    delta = jnp.zeros(tokens.shape, jnp.float32)
    for index in range(N_NODE):
        part = jnp.dot(hidden[:, index * block:(index + 1) * block], w_down_t[:, index * block:(index + 1) * block].T, preferred_element_type=jnp.float32)
        delta = delta + lax.optimization_barrier(part.astype(jnp.bfloat16)).astype(jnp.float32)
    weight = adv_table[bin_tok, grp_tok]
    err = tokens.astype(jnp.float32) + delta - target.astype(jnp.float32)
    dpred = weight[:, None] * err
    dy = dpred.astype(jnp.bfloat16)
    dh = jnp.dot(dy, w_down_t, preferred_element_type=jnp.float32)
    pull = jax.vjp(gelu_tanh, pre)[1]
    dpre = pull(dh)[0].astype(jnp.bfloat16)
    dmod = jnp.zeros(tokens.shape, jnp.float32)
    for index in range(N_NODE):
        part = jnp.dot(dpre[:, index * block:(index + 1) * block], w_up[:, index * block:(index + 1) * block].T, preferred_element_type=jnp.float32)
        dmod = dmod + lax.optimization_barrier(part.astype(jnp.bfloat16)).astype(jnp.float32)
    grad_tokens = dpred + gain * dmod
    scale = float(TOKENS) ** (-0.5)
    rows = SEQ * MICRO
    grad_up = jnp.zeros(w_up.shape, jnp.float32)
    grad_down = jnp.zeros(w_up.shape, jnp.float32)
    for index in range(N_WIDE):
        low = index * rows
        term_up = jnp.dot(modulated[low:low + rows].T, dpre[low:low + rows], preferred_element_type=jnp.float32) * scale
        term_down = jnp.dot(dy[low:low + rows].T, hidden[low:low + rows], preferred_element_type=jnp.float32) * scale
        grad_up = grad_up + lax.optimization_barrier(term_up.astype(jnp.bfloat16)).astype(jnp.float32)
        grad_down = grad_down + lax.optimization_barrier(term_down.astype(jnp.bfloat16)).astype(jnp.float32)
    return (grad_tokens, grad_up, grad_down)
```

```python
import jax
import jax.numpy as jnp
from jax import lax
from jax.experimental import pallas as pl
from jax.experimental.pallas import tpu as pltpu
from jax.sharding import PartitionSpec as P

F32 = jnp.float32
BF16 = jnp.bfloat16
MESH = pl.DeviceIdType.MESH
COEF = 0.7978845608028654


def dot_nn(a, b):
    return jnp.dot(a, b, preferred_element_type=F32)


def dot_nt(a, b):
    return lax.dot_general(a, b, (((1,), (1,)), ((), ())), preferred_element_type=F32)


def dot_tn(a, b):
    return lax.dot_general(a, b, (((0,), (0,)), ((), ())), preferred_element_type=F32)


def gelu_slope(v):
    th = jnp.tanh(COEF * (v + 0.044715 * v * v * v))
    return 0.5 * (1.0 + th) + 0.5 * v * (1.0 - th * th) * COEF * (1.0 + 3 * 0.044715 * v * v)


def tiles(rows, size, body):
    @pl.loop(0, rows // size)
    def _(t):
        body(pl.ds(pl.multiple_of(t * size, size), size))


def make_kernel(rows, feat, depth, hidden, micro, scale):
    seq = rows // micro

    def kernel(
        tok, tgt, mod, adv, bins, grps, wu_in, wd_in,
        gt_out, gu_out, gd_out,
        X, Y, Wu, Wd, pre, dh, hid, dpre, SB, RB1, RB2, SGD, SIBD, SIBU, RGD, RGU, gain,
        ss, rs, ls,
    ):
        SGU = Wd
        wi, ni = lax.axis_index("wide"), lax.axis_index("node")
        xh, z, c = wi // 8, (wi // 2) % 4, wi % 2
        xl, y = ni // 4, ni % 4

        def nd(dx, dy):
            return ((xl + dx) % 2) * 4 + (y + dy + 4) % 4

        def wm(dx, dz):
            return ((xh + dx) % 2) * 4 + (z + dz + 4) % 4

        def dnode(dx, dy):
            return (wi, nd(dx, dy))

        def dwide(dx, dz):
            return (wm(dx, dz) * 2 + c, ni)

        sib = (wm(0, 0) * 2 + 1 - c, ni)

        table = {}
        count = [0]

        def add(name, src, dst, got, dev):
            table[name] = (count[0], src, dst, got, dev)
            count[0] += 1

        def desc(name, received):
            i, src, dst, got, dev = table[name]
            return pltpu.make_async_remote_copy(
                src_ref=got if received else src,
                dst_ref=got if received else dst,
                send_sem=ss.at[i],
                recv_sem=rs.at[i],
                device_id=dev,
                device_id_type=MESH,
            )

        def start(*names):
            for name in names:
                desc(name, False).start()

        def recv(*names):
            for name in names:
                desc(name, True).wait_recv()

        def sent(*names):
            for name in names:
                desc(name, False).wait_send()

        half = rows // 2
        H1, H2 = pl.ds(0, half), pl.ds(half, half)

        def add_ag(p, B):
            def one(name, blk, r, got, dev):
                add(p + name, B.at[blk, r], B.at[blk, r], B.at[got, r], dev)

            R = pl.ds(0, rows)
            one("x", nd(0, 0), R, nd(1, 0), dnode(1, 0))
            one("yp", nd(0, 0), R, nd(0, -1), dnode(0, 1))
            one("ym", nd(0, 0), R, nd(0, 1), dnode(0, -1))
            one("cp", nd(0, -1), H1, nd(0, 2), dnode(0, 1))
            one("cm", nd(0, 1), H2, nd(0, 2), dnode(0, -1))
            one("bp", nd(1, 0), R, nd(1, -1), dnode(0, 1))
            one("bm", nd(1, 0), R, nd(1, 1), dnode(0, -1))
            one("d1", nd(0, 2), H1, nd(1, 2), dnode(1, 0))
            one("d2", nd(0, 2), H2, nd(1, 2), dnode(1, 0))

        AGN = ("x", "yp", "ym", "cp", "cm", "bp", "bm", "d1", "d2")
        part = depth // 16
        mine, other = pl.multiple_of(c * part, part), pl.multiple_of((1 - c) * part, part)
        PC, PS = pl.ds(mine, part), pl.ds(other, part)
        Q1 = pl.ds(mine, part // 2)
        Q2 = pl.ds(pl.multiple_of(mine + part // 2, part // 2), part // 2)
        SIBS = ((0, 0), (0, -1), (0, 1), (1, 0), (0, 2), (1, -1), (1, 1), (1, 2))

        def add_wag(p, B):
            def one(name, blk, r, got, dev):
                add(p + name, B.at[blk, r], B.at[blk, r], B.at[got, r], dev)

            one("x", wm(0, 0), PC, wm(1, 0), dwide(1, 0))
            one("zp", wm(0, 0), PC, wm(0, -1), dwide(0, 1))
            one("zm", wm(0, 0), PC, wm(0, 1), dwide(0, -1))
            one("cp", wm(0, -1), Q1, wm(0, 2), dwide(0, 1))
            one("cm", wm(0, 1), Q2, wm(0, 2), dwide(0, -1))
            one("bp", wm(1, 0), PC, wm(1, -1), dwide(0, 1))
            one("bm", wm(1, 0), PC, wm(1, 1), dwide(0, -1))
            one("ep", wm(1, -1), Q1, wm(1, 2), dwide(0, 1))
            one("em", wm(1, 1), Q2, wm(1, 2), dwide(0, -1))
            for dx, dz in SIBS:
                b = wm(dx, dz)
                add(f"{p}s{dx}{dz}", B.at[b, PC], B.at[b, PC], B.at[b, PS], sib)

        WAG = ("x", "zp", "zm", "cp", "cm", "bp", "bm", "ep", "em") + tuple(f"s{a}{b}" for a, b in SIBS)

        def add_rs(p, R):
            def one(name, blk, r, slot, dev):
                add(p + name, SB.at[blk, r], R.at[slot, r], R.at[slot, r], dev)

            W = pl.ds(0, rows)
            one("x0", nd(1, 2), W, 0, dnode(1, 0))
            one("bp", nd(1, 1), W, 2, dnode(0, 1))
            one("bm", nd(1, -1), W, 3, dnode(0, -1))
            one("cp", nd(0, 2), H1, 1, dnode(0, 1))
            one("cm", nd(0, 2), H2, 1, dnode(0, -1))
            one("ax", nd(1, 0), W, 4, dnode(1, 0))
            one("ap", nd(0, 1), W, 5, dnode(0, 1))
            one("am", nd(0, -1), W, 6, dnode(0, -1))

        RSN = ("x0", "bp", "bm", "cp", "cm", "ax", "ap", "am")
        A1, A2 = pl.ds(0, part // 2), pl.ds(part // 2, part // 2)
        AW = pl.ds(0, part)

        def add_wrs(p, S, R, B):
            def one(name, blk, r, slot, rr, dev):
                add(p + name, S.at[blk, r], R.at[slot, rr], R.at[slot, rr], dev)

            one("cp0", wm(0, 2), Q1, 0, A1, dwide(0, 1))
            one("cm0", wm(0, 2), Q2, 0, A2, dwide(0, -1))
            one("cp1", wm(1, 2), Q1, 1, A1, dwide(0, 1))
            one("cm1", wm(1, 2), Q2, 1, A2, dwide(0, -1))
            one("bp", wm(1, 1), PC, 2, AW, dwide(0, 1))
            one("bm", wm(1, -1), PC, 3, AW, dwide(0, -1))
            one("ap", wm(0, 1), PC, 4, AW, dwide(0, 1))
            one("am", wm(0, -1), PC, 5, AW, dwide(0, -1))
            one("ax", wm(1, 0), PC, 6, AW, dwide(1, 0))
            base = count[0]
            count[0] += 8

            def sibling(b):
                return pltpu.make_async_remote_copy(
                    src_ref=S.at[b, PS],
                    dst_ref=B.at[b],
                    send_sem=ss.at[base + b],
                    recv_sem=rs.at[base + b],
                    device_id=sib,
                    device_id_type=MESH,
                )

            return sibling

        RSW = ("cp0", "cm0", "cp1", "cm1", "bp", "bm", "ap", "am", "ax")
        add_ag("X", X)
        add_ag("Y", Y)
        add_wag("U", Wu)
        add_wag("D", Wd)
        add_rs("P", RB1)
        add_rs("M", RB2)
        sib_d = add_wrs("G", SGD, RGD, SIBD)
        sib_u = add_wrs("H", SGU, RGU, SIBU)

        barrier = pltpu.get_barrier_semaphore()
        for dev in (dnode(1, 0), dnode(0, 1), dnode(0, -1), dwide(1, 0), dwide(0, 1), dwide(0, -1), sib):
            pl.semaphore_signal(barrier, inc=1, device_id=dev, device_id_type=MESH)
        lu = pltpu.make_async_copy(wu_in, Wu.at[wm(0, 0), PC], ls.at[0])
        ld = pltpu.make_async_copy(wd_in, Wd.at[wm(0, 0), PC], ls.at[1])
        lu.start()
        ld.start()
        nb, ng = adv.shape
        row_i = lax.broadcasted_iota(jnp.int32, (nb, feat), 0)
        for s in range(micro):
            picked = jnp.sum(jnp.where(row_i == bins[s], mod[...].astype(F32), 0.0), axis=0, keepdims=True)
            gain[s : s + 1, :] = 1.0 + picked

            def modulate(r, s=s):
                q = pl.ds(pl.multiple_of(r.start + s * seq, 32), r.size)
                X[nd(0, 0), q, :] = (tok[q, :].astype(F32) * gain[s : s + 1, :]).astype(BF16)

            tiles(seq, 32, modulate)
        lu.wait()
        ld.wait()
        pl.semaphore_wait(barrier, 7)

        start("Xyp", "Xym", "Xx", "Ux", "Uzp", "Uzm", "Us00")

        def zero(r):
            pre[r, :] = jnp.zeros((r.size, hidden), F32)
            dh[r, :] = jnp.zeros((r.size, hidden), F32)

        tiles(rows, 32, zero)
        recv("Uzp")
        start("Ucp", "Us0-1")
        recv("Uzm")
        start("Ucm", "Us01")
        recv("Ux")
        start("Ubp", "Ubm", "Us10")
        start("Dx", "Dzp", "Dzm", "Ds00")
        recv("Xyp")
        start("Xcp")
        recv("Xym")
        start("Xcm")
        recv("Xx")
        start("Xbp", "Xbm")
        recv("Ucp", "Ucm")
        start("Us02")
        recv("Ubp")
        start("Uep", "Us1-1")
        recv("Ubm")
        start("Uem", "Us11")
        recv("Xcp")
        start("Xd1")
        recv("Xcm")
        start("Xd2")
        recv("Dzp")
        start("Dcp", "Ds0-1")
        recv("Dzm")
        start("Dcm", "Ds01")
        recv("Dx")
        start("Dbp", "Dbm", "Ds10")
        recv("Uep", "Uem")
        start("Us12")
        recv(*[f"Us{a}{b}" for a, b in SIBS])

        def arrival(k):
            dx = jnp.where((k == 3) | (k >= 5), 1, 0)
            dy = jnp.where((k == 1) | (k == 5), 1, jnp.where((k == 2) | (k == 6), 3, jnp.where((k == 4) | (k == 7), 2, 0)))
            return ((xl + dx) % 2) * 4 + (y + dy) % 4

        @pl.loop(0, 8)
        def _(k):
            @pl.when(k == 5)
            def _():
                recv("Dcp", "Dcm")
                start("Ds02")
                recv("Dbp")
                start("Dep", "Ds1-1")
                recv("Dbm")
                start("Dem", "Ds11")
                recv("Xbp", "Xbm", "Xd1", "Xd2")

            n = arrival(k)
            pre[...] += dot_nn(X[n], Wu[n])

        def activate(r):
            hid[r, :] = jax.nn.gelu(pre[r, :], approximate=True).astype(BF16)

        tiles(rows, 32, activate)
        recv("Dep", "Dem")
        start("Ds12")
        recv(*[f"Ds{a}{b}" for a, b in SIBS])

        def departure(k):
            dx = jnp.where((k <= 2) | (k == 4), 1, 0)
            dy = jnp.where((k == 0) | (k == 3), 2, jnp.where((k == 1) | (k == 5), 1, jnp.where((k == 2) | (k == 6), 3, 0)))
            return ((xl + dx) % 2) * 4 + (y + dy) % 4

        def products(p, left, weight):
            @pl.loop(0, 8)
            def _(k):
                n = departure(k)
                SB[n] = dot_nt(left[...], weight[n]).astype(BF16)

                @pl.when(k == 0)
                def _():
                    start(p + "x0")

                @pl.when(k == 1)
                def _():
                    start(p + "bp")

                @pl.when(k == 2)
                def _():
                    start(p + "bm")

        def plus(blk, r0, size, R, *slots):
            def body(r):
                q = pl.ds(pl.multiple_of(r.start + r0, 32), r.size)
                v = SB[blk, q, :].astype(F32)
                for slot in slots:
                    v = v + R[slot, q, :].astype(F32)
                SB[blk, q, :] = v.astype(BF16)

            tiles(size, 32, body)

        def rs_first(p, R):
            recv(p + "x0")
            plus(nd(0, 2), 0, rows, R, 0)
            start(p + "cp", p + "cm")

        def rs_second(p, R):
            recv(p + "bp", p + "bm")
            plus(nd(1, 0), 0, rows, R, 2, 3)
            start(p + "ax")

        def rs_third(p, R):
            recv(p + "cp")
            plus(nd(0, 1), 0, half, R, 1)
            start(p + "ap")
            recv(p + "cm")
            plus(nd(0, -1), half, half, R, 1)
            start(p + "am")

        products("P", hid, Wd)
        rs_first("P", RB1)
        rs_second("P", RB1)
        rs_third("P", RB1)
        recv("Pax", "Pap", "Pam")

        def total(R, q):
            v = SB[nd(0, 0), q, :].astype(F32) + R[4, q, :].astype(F32)
            return v + R[5, q, :].astype(F32) + R[6, q, :].astype(F32)

        bin_i = lax.broadcasted_iota(jnp.int32, (nb, ng), 0)
        grp_i = lax.broadcasted_iota(jnp.int32, (nb, ng), 1)
        for s in range(micro):
            chosen = jnp.where((bin_i == bins[s]) & (grp_i == grps[s]), adv[...], 0.0)
            weight = jnp.sum(jnp.sum(chosen, axis=1, keepdims=True), axis=0, keepdims=True)

            def error(r, s=s, weight=weight):
                q = pl.ds(pl.multiple_of(r.start + s * seq, 32), r.size)
                d = weight * (tok[q, :].astype(F32) + total(RB1, q) - tgt[q, :].astype(F32))
                gt_out[q, :] = d
                Y[nd(0, 0), q, :] = d.astype(BF16)

            tiles(seq, 32, error)

        start("Yyp", "Yym", "Yx")
        sent(*["P" + n for n in RSN])

        @pl.loop(0, 8)
        def _(k):
            @pl.when(k == 1)
            def _():
                recv("Yyp")
                start("Ycp")
                recv("Yym")
                start("Ycm")
                recv("Yx")
                start("Ybp", "Ybm")

            @pl.when(k == 4)
            def _():
                recv("Ycp")
                start("Yd1")
                recv("Ycm")
                start("Yd2")

            @pl.when(k == 5)
            def _():
                recv("Ybp", "Ybm", "Yd1", "Yd2")

            n = arrival(k)
            SGD[n] = (dot_tn(Y[n], hid[...]) * scale).astype(BF16)
            sib_d(n).start()
            dh[...] += dot_nn(Y[n], Wd[n])

        def wide_plus(S, blk, slots, r0, size):
            def body(r):
                a = pl.ds(pl.multiple_of(r.start + r0, 32), r.size)
                q = pl.ds(pl.multiple_of(mine + r.start + r0, 32), r.size)
                v = S[blk, q, :].astype(F32)
                for ref, slot in slots:
                    v = v + ref[slot, a, :].astype(F32)
                S[blk, q, :] = v.astype(BF16)

            tiles(size, 32, body)

        def wide_first(p, S, B, sibling):
            for d in ((0, 2), (1, 2)):
                b = wm(*d)
                sibling(b).wait_recv()
                wide_plus(S, b, ((B, b),), 0, part)
            start(p + "cp0", p + "cm0", p + "cp1", p + "cm1")

        def wide_rest(p, S, B, sibling):
            for d in ((1, 1), (1, -1), (0, 1), (0, -1), (1, 0), (0, 0)):
                sibling(wm(*d)).wait_recv()

        quarter = part // 2

        def wide_second(p, S, B, R):
            for dx, cc, kind in ((1, "1", "b"), (0, "0", "a")):
                recv(p + "cp" + cc)
                b = wm(dx, 1)
                wide_plus(S, b, ((B, b), (R, dx)), 0, quarter)
                wide_plus(S, b, ((B, b),), quarter, quarter)
                start(p + kind + "p")
                recv(p + "cm" + cc)
                b = wm(dx, -1)
                wide_plus(S, b, ((B, b),), 0, quarter)
                wide_plus(S, b, ((B, b), (R, dx)), quarter, quarter)
                start(p + kind + "m")

        def wide_third(p, S, B, R):
            recv(p + "bp", p + "bm")
            b = wm(1, 0)
            wide_plus(S, b, ((B, b), (R, 2), (R, 3)), 0, part)
            start(p + "ax")

        def wide_last(p, S, B, R, out):
            recv(p + "ap", p + "am", p + "ax")
            b = wm(0, 0)

            def body(r):
                q = pl.ds(pl.multiple_of(mine + r.start, 32), r.size)
                v = S[b, q, :].astype(F32) + B[b, r, :].astype(F32)
                for slot in (4, 5, 6):
                    v = v + R[slot, r, :].astype(F32)
                out[r, :] = v

            tiles(part, 32, body)

        wide_first("G", SGD, SIBD, sib_d)

        def slope(r):
            dpre[r, :] = (dh[r, :] * gelu_slope(pre[r, :])).astype(BF16)

        tiles(rows, 32, slope)

        products("M", dpre, Wu)
        wide_rest("G", SGD, SIBD, sib_d)
        wide_second("G", SGD, SIBD, RGD)
        sent(*["D" + n for n in WAG])

        def outward(k):
            dx = jnp.where((k == 1) | (k == 2) | (k == 3) | (k == 6), 1, 0)
            dz = jnp.where(k <= 1, 2, jnp.where((k == 2) | (k == 4), 1, jnp.where((k == 3) | (k == 5), 3, 0)))
            return ((xh + dx) % 2) * 4 + (z + dz) % 4

        @pl.loop(0, 8)
        def _(k):
            m = outward(k)
            SGU[m] = (dot_tn(X[m], dpre[...]) * scale).astype(BF16)
            sib_u(m).start()

            @pl.when(k == 3)
            def _():
                wide_first("H", SGU, SIBU, sib_u)

        rs_first("M", RB2)
        wide_third("G", SGD, SIBD, RGD)
        rs_second("M", RB2)
        rs_third("M", RB2)
        wide_rest("H", SGU, SIBU, sib_u)
        wide_second("H", SGU, SIBU, RGU)
        wide_last("G", SGD, SIBD, RGD, gd_out)
        recv("Max", "Map", "Mam")
        for s in range(micro):

            def finish(r, s=s):
                q = pl.ds(pl.multiple_of(r.start + s * seq, 32), r.size)
                gt_out[q, :] = gt_out[q, :] + gain[s : s + 1, :] * total(RB2, q)

            tiles(seq, 32, finish)
        wide_third("H", SGU, SIBU, RGU)
        wide_last("H", SGU, SIBU, RGU, gu_out)

        sent(*["X" + n for n in AGN], *["Y" + n for n in AGN], *["U" + n for n in WAG], *["M" + n for n in RSN])
        sent(*["G" + n for n in RSW], *["H" + n for n in RSW])

        @pl.loop(0, 8)
        def _(b):
            sib_d(b).wait_send()
            sib_u(b).wait_send()

    return kernel


TRANSFERS = 9 * 2 + 17 * 2 + 8 * 2 + 17 * 2


def on_device(tokens, target, mod_table, adv_table, w_up, w_down_t, bins, groups):
    rows, feat = tokens.shape
    part, hidden = w_up.shape
    depth = part * 16
    micro = bins.shape[0]
    scale = float(16 * rows) ** (-0.5)
    vmem = pl.BlockSpec(memory_space=pltpu.VMEM)
    smem = pl.BlockSpec(memory_space=pltpu.SMEM)
    anys = pl.BlockSpec(memory_space=pl.ANY)
    block = (8, rows, feat)
    wblock = (8, depth // 8, hidden)
    V = pltpu.VMEM
    flops = 6 * 2 * rows * depth * hidden
    return pl.pallas_call(
        make_kernel(rows, feat, depth, hidden, micro, scale),
        out_shape=(
            jax.ShapeDtypeStruct((rows, feat), F32),
            jax.ShapeDtypeStruct((part, hidden), F32),
            jax.ShapeDtypeStruct((part, hidden), F32),
        ),
        in_specs=[vmem, vmem, vmem, vmem, smem, smem, anys, anys],
        out_specs=(vmem, vmem, vmem),
        scratch_shapes=[
            V(block, BF16), V(block, BF16), V(wblock, BF16), V(wblock, BF16),
            V((rows, hidden), F32), V((rows, hidden), F32), V((rows, hidden), BF16), V((rows, hidden), BF16),
            V(block, BF16), V((7, rows, feat), BF16), V((7, rows, feat), BF16),
            V(wblock, BF16), V((8, part, hidden), BF16), V((8, part, hidden), BF16),
            V((7, part, hidden), BF16), V((7, part, hidden), BF16),
            V((8, feat), F32),
            pltpu.SemaphoreType.DMA((TRANSFERS,)),
            pltpu.SemaphoreType.DMA((TRANSFERS,)),
            pltpu.SemaphoreType.DMA((2,)),
        ],
        compiler_params=pltpu.CompilerParams(
            collective_id=0, has_side_effects=True, vmem_limit_bytes=63 * 2**20
        ),
        cost_estimate=pl.CostEstimate(flops=flops, bytes_accessed=8 * 2**20, transcendentals=2 * rows * hidden),
        name="block_gradient",
    )(tokens, target, mod_table, adv_table, bins, groups, w_up, w_down_t)


def solution(mesh):
    return jax.shard_map(
        on_device,
        mesh=mesh,
        in_specs=(
            P("wide", "node"),
            P("wide", "node"),
            P(None, "node"),
            P(),
            P("wide", "node"),
            P("wide", "node"),
            P("wide"),
            P("wide"),
        ),
        out_specs=(P("wide", "node"), P("wide", "node"), P("wide", "node")),
        check_vma=False,
    )
```

```python
import jax
import jax.numpy as jnp
from jax import lax
from jax.experimental import pallas as pl
from jax.experimental.pallas import tpu as pltpu
from jax.sharding import PartitionSpec as P

F32 = jnp.float32
BF16 = jnp.bfloat16
MESH = pl.DeviceIdType.MESH
COEF = 0.7978845608028654


def dot_nn(a, b):
    return jnp.dot(a, b, preferred_element_type=F32)


def dot_nt(a, b):
    return lax.dot_general(a, b, (((1,), (1,)), ((), ())), preferred_element_type=F32)


def dot_tn(a, b):
    return lax.dot_general(a, b, (((0,), (0,)), ((), ())), preferred_element_type=F32)


def gelu_slope(v):
    th = jnp.tanh(COEF * (v + 0.044715 * v * v * v))
    return 0.5 * (1.0 + th) + 0.5 * v * (1.0 - th * th) * COEF * (1.0 + 3 * 0.044715 * v * v)


def tiles(rows, size, body):
    @pl.loop(0, rows // size)
    def _(t):
        body(pl.ds(pl.multiple_of(t * size, size), size))


def make_kernel(rows, feat, depth, hidden, micro, scale):
    seq = rows // micro

    def kernel(
        tok, tgt_in, mod, adv, bins, grps, wu_in, wd_in,
        gt_out, gu_out, gd_out,
        X, Y, Wu, Wd, pre, dh, hid, dpre, SB, RB, SGD, SIBD, SIBU, RGD, RGU, gain,
        tgt, dpred, gt, gu, gd, ss, rs, ls,
    ):
        SGU = Wd
        wi, ni = lax.axis_index("wide"), lax.axis_index("node")
        xh, z, c = wi // 8, (wi // 2) % 4, wi % 2
        xl, y = ni // 4, ni % 4

        def nd(dx, dy):
            return ((xl + dx) % 2) * 4 + (y + dy + 4) % 4

        def wm(dx, dz):
            return ((xh + dx) % 2) * 4 + (z + dz + 4) % 4

        def dnode(dx, dy):
            return (wi, nd(dx, dy))

        def dwide(dx, dz):
            return (wm(dx, dz) * 2 + c, ni)

        sib = (wm(0, 0) * 2 + 1 - c, ni)

        table = {}
        count = [0]

        def add(name, src, dst, got, dev):
            table[name] = (count[0], src, dst, got, dev)
            count[0] += 1

        def desc(name, received):
            i, src, dst, got, dev = table[name]
            return pltpu.make_async_remote_copy(
                src_ref=got if received else src,
                dst_ref=got if received else dst,
                send_sem=ss.at[i],
                recv_sem=rs.at[i],
                device_id=dev,
                device_id_type=MESH,
            )

        def start(*names):
            for name in names:
                desc(name, False).start()

        def recv(*names):
            for name in names:
                desc(name, True).wait_recv()

        def sent(*names):
            for name in names:
                desc(name, False).wait_send()

        part = depth // 16
        mine, other = pl.multiple_of(c * part, part), pl.multiple_of((1 - c) * part, part)
        PC, PS = pl.ds(mine, part), pl.ds(other, part)
        Q1 = pl.ds(mine, part // 2)
        Q2 = pl.ds(pl.multiple_of(mine + part // 2, part // 2), part // 2)
        W = pl.ds(0, rows)
        half = rows // 2
        H1, H2 = pl.ds(0, half), pl.ds(half, half)
        K = [pl.ds(i * (half // 2), half // 2) for i in range(4)]

        def add_ag(p, B, fewer):
            def one(name, blk, r, got, dev):
                add(p + name, B.at[blk, r], B.at[blk, r], B.at[got, r], dev)

            one("yp1", nd(0, 0), H1, nd(0, -1), dnode(0, 1))
            one("yp2", nd(0, 0), H2, nd(0, -1), dnode(0, 1))
            one("ym1", nd(0, 0), H1, nd(0, 1), dnode(0, -1))
            one("ym2", nd(0, 0), H2, nd(0, 1), dnode(0, -1))
            for i, r in (("1", H1), ("2", H2)):
                one("x" + i, nd(0, 0), r, nd(1, 0), dnode(1, 0))
                one("bp" + i, nd(1, 0), r, nd(1, -1), dnode(0, 1))
                one("bm" + i, nd(1, 0), r, nd(1, 1), dnode(0, -1))
            for i, rp, rm in (("1", K[0], K[2]), ("2", K[1], K[3])):
                one("cp" + i, nd(0, -1), rp, nd(0, 2), dnode(0, 1))
                one("cm" + i, nd(0, 1), rm, nd(0, 2), dnode(0, -1))
                one("dp" + i, nd(0, 2), rp, nd(1, 2), dnode(1, 0))
                if not fewer:
                    one("dm" + i, nd(0, 2), rm, nd(1, 2), dnode(1, 0))
            if fewer:
                one("ep", nd(1, -1), K[2], nd(1, 2), dnode(0, 1))
                one("em", nd(1, 1), K[3], nd(1, 2), dnode(0, -1))

        def ag_names(p, fewer):
            names = ["yp", "ym", "x", "bp", "bm", "cp", "cm", "dp"] + ([] if fewer else ["dm"])
            last = ["ep", "em"] if fewer else []
            return [p + n + i for n in names for i in "12"] + [p + n for n in last]

        def add_wag(p, B, b0):
            def one(name, blk, r, got, dev):
                add(p + name, B.at[blk, r], B.at[blk, r], B.at[got, r], dev)

            one("x", wm(0, 0), PC, wm(1, 0), dwide(1, 0))
            for i, b in ((0, b0), (1, 1 - b0)):
                here, up, down, far = (b * 4 + (z + d) % 4 for d in (0, 1, 3, 2))
                one(f"zp{i}", here, Q1, down, dwide(0, 1))
                one(f"zm{i}", here, Q2, up, dwide(0, -1))
                one(f"yp{i}", here, Q2, down, dwide(0, 1))
                one(f"ym{i}", here, Q1, up, dwide(0, -1))
                one(f"cp{i}", down, Q1, far, dwide(0, 1))
                one(f"cm{i}", up, Q2, far, dwide(0, -1))
            base = count[0]
            count[0] += 8

            def share(b, received=False):
                r = PS if received else PC
                return pltpu.make_async_remote_copy(
                    src_ref=B.at[b, r],
                    dst_ref=B.at[b, r],
                    send_sem=ss.at[base + b],
                    recv_sem=rs.at[base + b],
                    device_id=sib,
                    device_id_type=MESH,
                )

            return share

        WAG = ("x",) + tuple(f"{n}{i}" for i in (0, 1) for n in ("zp", "zm", "yp", "ym", "cp", "cm"))

        def add_rs(p, R):
            def one(name, blk, r, slot, dev):
                add(p + name, SB.at[blk, r], R.at[slot, r], R.at[slot, r], dev)

            one("x0", nd(1, 2), W, 0, dnode(1, 0))
            one("bp", nd(1, 1), W, 2, dnode(0, 1))
            one("bm", nd(1, -1), W, 3, dnode(0, -1))
            one("cp", nd(0, 2), H1, 1, dnode(0, 1))
            one("cm", nd(0, 2), H2, 1, dnode(0, -1))
            one("ax", nd(1, 0), W, 4, dnode(1, 0))
            one("ap1", nd(0, 1), H1, 5, dnode(0, 1))
            one("ap2", nd(0, 1), H2, 5, dnode(0, 1))
            one("am1", nd(0, -1), H1, 6, dnode(0, -1))
            one("am2", nd(0, -1), H2, 6, dnode(0, -1))

        RSN = ("x0", "bp", "bm", "cp", "cm", "ax", "ap1", "ap2", "am1", "am2")
        A1, A2 = pl.ds(0, part // 2), pl.ds(part // 2, part // 2)
        AW = pl.ds(0, part)

        def add_wrs(p, S, R, B, b0):
            def one(name, blk, r, slot, rr, dev):
                add(p + name, S.at[blk, r], R.at[slot, rr], R.at[slot, rr], dev)

            one("x", wm(1, 0), PC, 6, AW, dwide(1, 0))
            for i, b in ((0, b0), (1, 1 - b0)):
                up, down, far = (b * 4 + (z + d) % 4 for d in (1, 3, 2))
                one(f"cp{i}", far, Q1, i, A1, dwide(0, 1))
                one(f"cm{i}", far, Q2, i, A2, dwide(0, -1))
                one(f"ap{i}", up, PC, 2 + 2 * i, AW, dwide(0, 1))
                one(f"am{i}", down, PC, 3 + 2 * i, AW, dwide(0, -1))
            base = count[0]
            count[0] += 8

            def share(b):
                return pltpu.make_async_remote_copy(
                    src_ref=S.at[b, PS],
                    dst_ref=B.at[b],
                    send_sem=ss.at[base + b],
                    recv_sem=rs.at[base + b],
                    device_id=sib,
                    device_id_type=MESH,
                )

            return share

        RSW = ("x",) + tuple(f"{n}{i}" for i in (0, 1) for n in ("cp", "cm", "ap", "am"))
        add_ag("X", X, True)
        add_ag("Y", Y, False)
        share_u = add_wag("U", Wu, xh)
        share_d = add_wag("D", Wd, 1 - xl)
        add_rs("P", RB)
        add_rs("M", RB)
        sib_d = add_wrs("G", SGD, RGD, SIBD, xl)
        sib_u = add_wrs("H", SGU, RGU, SIBU, xl)

        barrier = pltpu.get_barrier_semaphore()
        for dev in (dnode(1, 0), dnode(0, 1), dnode(0, -1), dwide(1, 0), dwide(0, 1), dwide(0, -1), sib):
            pl.semaphore_signal(barrier, inc=1, device_id=dev, device_id_type=MESH)
        lu = pltpu.make_async_copy(wu_in, Wu.at[wm(0, 0), PC], ls.at[0])
        ld = pltpu.make_async_copy(wd_in, Wd.at[wm(0, 0), PC], ls.at[1])
        lt = pltpu.make_async_copy(tgt_in, tgt, ls.at[2])
        lu.start()
        ld.start()
        lt.start()

        def back(src, dst, i):
            return pltpu.make_async_copy(src, dst, ls.at[3 + i])

        ng, nb = adv.shape
        row_i = lax.broadcasted_iota(jnp.int32, (nb, feat), 0)
        for s in range(micro):
            picked = jnp.sum(jnp.where(row_i == bins[s], mod[...].astype(F32), 0.0), axis=0, keepdims=True)
            gain[s : s + 1, :] = 1.0 + picked

            def modulate(r, s=s):
                q = pl.ds(pl.multiple_of(r.start + s * seq, 32), r.size)
                X[nd(0, 0), q, :] = (tok[q, :].astype(F32) * gain[s : s + 1, :]).astype(BF16)

            tiles(seq, 32, modulate)
        lu.wait()
        ld.wait()
        pl.semaphore_wait(barrier, 7)

        def ring_start(p, i):
            start(f"{p}zp{i}", f"{p}zm{i}", f"{p}yp{i}", f"{p}ym{i}")

        def ring_relay(p, i):
            recv(f"{p}zp{i}")
            start(f"{p}cp{i}")
            recv(f"{p}zm{i}")
            start(f"{p}cm{i}")

        def ring_share(p, i, b, share):
            recv(f"{p}yp{i}")
            share(b * 4 + (z + 3) % 4).start()
            recv(f"{p}ym{i}")
            share(b * 4 + (z + 1) % 4).start()

        def ring_end(p, i, b, share):
            recv(f"{p}cp{i}", f"{p}cm{i}")
            share(b * 4 + (z + 2) % 4).start()

        same = xh == xl
        start("Xyp1", "Xym2", "Ux")
        ring_start("U", 0)
        start("Xyp2", "Xym1", "Xx2")
        share_u(wm(0, 0)).start()
        share_d(wm(0, 0)).start()

        @pl.when(~same)
        def _():
            start("Dx")

        start("Xx1")

        def zero(r):
            pre[r, :] = jnp.zeros((r.size, hidden), F32)
            dh[r, :] = jnp.zeros((r.size, hidden), F32)

        tiles(rows, 32, zero)
        ring_relay("U", 0)
        recv("Xyp1")
        start("Xcp1", "Xcp2")
        recv("Xym2")
        start("Xcm1", "Xcm2")
        recv("Ux")
        ring_start("U", 1)
        share_u(wm(1, 0)).start()
        ring_share("U", 0, xh, share_u)
        ring_end("U", 0, xh, share_u)
        ring_relay("U", 1)

        @pl.when(~same)
        def _():
            ring_start("D", 0)

        recv("Xx2")
        start("Xbp2", "Xbm2")
        recv("Xcp1", "Xcp2")
        start("Xdp1", "Xdp2")
        recv("Xcm1", "Xcm2")

        @pl.when(same)
        def _():
            start("Dx")
            recv("Dx")
            ring_start("D", 0)
            share_d(wm(1, 0)).start()

        ring_share("U", 1, 1 - xh, share_u)
        ring_end("U", 1, 1 - xh, share_u)
        recv("Xyp2", "Xym1")

        @pl.loop(0, 8)
        def _(b):
            share_u(b, True).wait_recv()

        def arrival(k):
            dx = jnp.where((k == 3) | (k >= 5), 1, 0)
            dy = jnp.where((k == 1) | (k == 5), 1, jnp.where((k == 2) | (k == 6), 3, jnp.where((k == 4) | (k == 7), 2, 0)))
            return ((xl + dx) % 2) * 4 + (y + dy) % 4

        @pl.loop(0, 8)
        def _(k):
            @pl.when(k == 1)
            def _():
                recv("Xx1")
                start("Xbp1", "Xbm1")

            @pl.when(k == 2)
            def _():
                recv("Xbp2")
                start("Xep")
                recv("Xbm2")
                start("Xem")

            @pl.when(k == 5)
            def _():
                ring_relay("D", 0)
                recv("Xbp1", "Xbm1")

            @pl.when(k == 7)
            def _():
                ring_share("D", 0, 1 - xl, share_d)

                @pl.when(~same)
                def _():
                    recv("Dx")
                    share_d(wm(1, 0)).start()

                ring_start("D", 1)
                recv("Xdp1", "Xdp2", "Xep", "Xem")

            n = arrival(k)
            pre[...] += dot_nn(X[n], Wu[n])

        def activate(r):
            hid[r, :] = jax.nn.gelu(pre[r, :], approximate=True).astype(BF16)

        tiles(rows, 32, activate)
        ring_end("D", 0, 1 - xl, share_d)

        def departure(k):
            dx = jnp.where(k <= 3, 1, 0)
            dy = jnp.where((k == 0) | (k == 4), 2, jnp.where((k == 1) | (k == 5), 1, jnp.where((k == 2) | (k == 6), 3, 0)))
            return ((xl + dx) % 2) * 4 + (y + dy) % 4

        def products(p, left, weight, first, last):
            @pl.loop(first, last)
            def _(k):
                n = departure(k)
                SB[n] = dot_nt(left[...], weight[n]).astype(BF16)
                for at, name in ((0, "x0"), (1, "bp"), (2, "bm"), (5, "ap2"), (6, "am1")):
                    if first <= at < last:

                        @pl.when(k == at)
                        def _(name=name):
                            start(p + name)

        def plus(blk, r0, size, R, *slots):
            def body(r):
                q = pl.ds(pl.multiple_of(r.start + r0, 32), r.size)
                v = SB[blk, q, :].astype(F32)
                for slot in slots:
                    v = v + R[slot, q, :].astype(F32)
                SB[blk, q, :] = v.astype(BF16)

            tiles(size, 32, body)

        def rs_first(p, R):
            recv(p + "x0")
            plus(nd(0, 2), 0, rows, R, 0)
            start(p + "cp", p + "cm")

        def rs_second(p, R):
            recv(p + "bp", p + "bm")
            plus(nd(1, 0), 0, rows, R, 2, 3)
            start(p + "ax")

        def rs_third(p, R):
            recv(p + "cp")
            plus(nd(0, 1), 0, half, R, 1)
            start(p + "ap1")
            recv(p + "cm")
            plus(nd(0, -1), half, half, R, 1)
            start(p + "am2")

        def rs_end(p):
            recv(*[p + n for n in ("ax", "ap1", "ap2", "am1", "am2")])

        def wait_column(b, share):
            for d in range(4):
                share(b * 4 + d, True).wait_recv()

        wait_column(1 - xl, share_d)
        products("P", hid, Wd, 0, 4)
        ring_relay("D", 1)
        ring_share("D", 1, xl, share_d)
        ring_end("D", 1, xl, share_d)
        wait_column(xl, share_d)
        products("P", hid, Wd, 4, 5)
        rs_first("P", RB)
        products("P", hid, Wd, 5, 8)
        rs_second("P", RB)
        rs_third("P", RB)
        rs_end("P")
        lt.wait()

        def total(R, q):
            v = SB[nd(0, 0), q, :].astype(F32) + R[4, q, :].astype(F32)
            return v + R[5, q, :].astype(F32) + R[6, q, :].astype(F32)

        bin_i = lax.broadcasted_iota(jnp.int32, (ng, nb), 1)
        grp_i = lax.broadcasted_iota(jnp.int32, (ng, nb), 0)
        for s in range(micro):
            chosen = jnp.where((bin_i == bins[s]) & (grp_i == grps[s]), adv[...], 0.0)
            weight = jnp.sum(jnp.sum(chosen, axis=1, keepdims=True), axis=0, keepdims=True)

            def error(r, s=s, weight=weight):
                q = pl.ds(pl.multiple_of(r.start + s * seq, 32), r.size)
                d = weight * (tok[q, :].astype(F32) + total(RB, q) - tgt[q, :].astype(F32))
                dpred[q, :] = d
                Y[nd(0, 0), q, :] = d.astype(BF16)

            tiles(seq, 32, error)

        start("Yyp1", "Yym2", "Yx1", "Yx2", "Yyp2", "Yym1")
        sent(*["P" + n for n in RSN])

        def stage_down(m):
            SGD[m] = (dot_tn(Y[m], hid[...]) * scale).astype(BF16)
            sib_d(m).start()

        def stage_up(m):
            SGU[m] = (dot_tn(X[m], dpre[...]) * scale).astype(BF16)
            sib_u(m).start()

        def wide_plus(S, blk, slots, r0, size):
            def body(r):
                a = pl.ds(pl.multiple_of(r.start + r0, 32), r.size)
                q = pl.ds(pl.multiple_of(mine + r.start + r0, 32), r.size)
                v = S[blk, q, :].astype(F32)
                for ref, slot in slots:
                    v = v + ref[slot, a, :].astype(F32)
                S[blk, q, :] = v.astype(BF16)

            tiles(size, 32, body)

        quarter = part // 2

        def wide_first(p, i, b, S, B, share):
            m = b * 4 + (z + 2) % 4
            share(m).wait_recv()
            wide_plus(S, m, ((B, m),), 0, part)
            start(f"{p}cp{i}", f"{p}cm{i}")

        def wide_second(p, i, b, S, B, R, share):
            for d in (1, 3, 0):
                share(b * 4 + (z + d) % 4).wait_recv()
            m = b * 4 + (z + 1) % 4
            wide_plus(S, m, ((B, m),), quarter, quarter)
            recv(f"{p}cp{i}")
            wide_plus(S, m, ((B, m), (R, i)), 0, quarter)
            start(f"{p}ap{i}")
            m = b * 4 + (z + 3) % 4
            wide_plus(S, m, ((B, m),), 0, quarter)
            recv(f"{p}cm{i}")
            wide_plus(S, m, ((B, m), (R, i)), quarter, quarter)
            start(f"{p}am{i}")

        def wide_third(p, i, b, S, B, R):
            recv(f"{p}ap{i}", f"{p}am{i}")

            @pl.when(xh != b)
            def _():
                m = b * 4 + z
                wide_plus(S, m, ((B, m), (R, 2 + 2 * i), (R, 3 + 2 * i)), 0, part)
                start(p + "x")

        def wide_last(p, b0, S, B, R, out):
            recv(p + "x")
            m = wm(0, 0)
            slot = jnp.where(xh == b0, 2, 4)

            def body(r):
                q = pl.ds(pl.multiple_of(mine + r.start, 32), r.size)
                v = S[m, q, :].astype(F32) + B[m, r, :].astype(F32)
                v = v + R[slot, r, :].astype(F32) + R[slot + 1, r, :].astype(F32)
                out[r, :] = (v + R[6, r, :].astype(F32)).astype(BF16)

            tiles(part, 32, body)

        G0 = ("G", 0, xl, SGD, SIBD)
        G1 = ("G", 1, 1 - xl, SGD, SIBD)
        U0 = ("H", 0, xl, SGU, SIBU)
        U1 = ("H", 1, 1 - xl, SGU, SIBU)

        @pl.loop(0, 5)
        def _(k):
            @pl.when(k == 1)
            def _():
                recv("Yyp1")
                start("Ycp1", "Ycp2")
                recv("Yym2")
                start("Ycm1", "Ycm2")
                recv("Yx1")
                start("Ybp1", "Ybm1")
                recv("Yx2")
                start("Ybp2", "Ybm2")
                recv("Yyp2", "Yym1")

            @pl.when(k == 4)
            def _():
                for i in "12":
                    recv("Ycp" + i)
                    start("Ydp" + i)
                    recv("Ycm" + i)
                    start("Ydm" + i)

            n = arrival(k)

            @pl.when(k != 3)
            def _():
                stage_down(n)

            dh[...] += dot_nn(Y[n], Wd[n])

        wide_first(*G0, sib_d)
        wide_second(*G0, RGD, sib_d)
        recv(*["Y" + n + i for n in ("bp", "bm", "dp", "dm") for i in "12"])
        stage_down((1 - xl) * 4 + (z + 2) % 4)

        @pl.loop(5, 8)
        def _(k):
            n = arrival(k)
            dh[...] += dot_nn(Y[n], Wd[n])

        wide_first(*G1, sib_d)

        def slope(r):
            dpre[r, :] = (dh[r, :] * gelu_slope(pre[r, :])).astype(BF16)

        tiles(rows, 32, slope)

        products("M", dpre, Wu, 0, 3)
        sent(*["D" + n for n in WAG])

        @pl.loop(0, 8)
        def _(b):
            share_d(b).wait_send()

        @pl.loop(0, 2)
        def _(k):
            stage_up(((xl + k) % 2) * 4 + (z + 2) % 4)

        wide_first(*U0, sib_u)
        wide_first(*U1, sib_u)

        @pl.loop(0, 3)
        def _(k):
            stage_down((1 - xl) * 4 + (z + 3 + k) % 4)

        wide_second(*G1, RGD, sib_d)
        wide_third("G", 0, xl, SGD, SIBD, RGD)
        products("M", dpre, Wu, 3, 5)

        @pl.loop(0, 3)
        def _(k):
            stage_up(xl * 4 + (z + 3 + k) % 4)

        rs_first("M", RB)
        rs_second("M", RB)
        wide_second(*U0, RGU, sib_u)
        products("M", dpre, Wu, 5, 8)

        @pl.loop(0, 3)
        def _(k):
            stage_up((1 - xl) * 4 + (z + 3 + k) % 4)

        rs_third("M", RB)
        wide_second(*U1, RGU, sib_u)
        wide_third("G", 1, 1 - xl, SGD, SIBD, RGD)
        wide_third("H", 0, xl, SGU, SIBU, RGU)
        rs_end("M")
        for s in range(micro):

            def finish(r, s=s):
                q = pl.ds(pl.multiple_of(r.start + s * seq, 32), r.size)
                gt[q, :] = (dpred[q, :] + gain[s : s + 1, :] * total(RB, q)).astype(BF16)

            tiles(seq, 32, finish)
        back(gt, gt_out, 1).start()
        wide_last("G", xl, SGD, SIBD, RGD, gd)
        back(gd, gd_out, 0).start()
        wide_third("H", 1, 1 - xl, SGU, SIBU, RGU)
        wide_last("H", xl, SGU, SIBU, RGU, gu)
        back(gu, gu_out, 2).start()

        sent(*ag_names("X", True), *ag_names("Y", False), *["U" + n for n in WAG], *["M" + n for n in RSN])
        sent(*["G" + n for n in RSW], *["H" + n for n in RSW])

        @pl.loop(0, 8)
        def _(b):
            share_u(b).wait_send()
            sib_d(b).wait_send()
            sib_u(b).wait_send()

        back(gd, gd_out, 0).wait()
        back(gt, gt_out, 1).wait()
        back(gu, gu_out, 2).wait()

    return kernel


TRANSFERS = 18 + 18 + 21 * 2 + 10 * 2 + 17 * 2


def on_device(tokens, target, mod_table, adv_table, w_up, w_down_t, bins, groups):
    rows, feat = tokens.shape
    part, hidden = w_up.shape
    depth = part * 16
    micro = bins.shape[0]
    scale = float(16 * rows) ** (-0.5)
    vmem = pl.BlockSpec(memory_space=pltpu.VMEM)
    smem = pl.BlockSpec(memory_space=pltpu.SMEM)
    anys = pl.BlockSpec(memory_space=pl.ANY)
    block = (8, rows, feat)
    wblock = (8, depth // 8, hidden)
    V = pltpu.VMEM
    flops = 6 * 2 * rows * depth * hidden
    grads = pl.pallas_call(
        make_kernel(rows, feat, depth, hidden, micro, scale),
        out_shape=(
            jax.ShapeDtypeStruct((rows, feat), BF16),
            jax.ShapeDtypeStruct((part, hidden), BF16),
            jax.ShapeDtypeStruct((part, hidden), BF16),
        ),
        in_specs=[vmem, anys, vmem, vmem, smem, smem, anys, anys],
        out_specs=(anys, anys, anys),
        scratch_shapes=[
            V(block, BF16), V(block, BF16), V(wblock, BF16), V(wblock, BF16),
            V((rows, hidden), F32), V((rows, hidden), F32), V((rows, hidden), BF16), V((rows, hidden), BF16),
            V(block, BF16), V((7, rows, feat), BF16),
            V(wblock, BF16), V((8, part, hidden), BF16), V((8, part, hidden), BF16),
            V((7, part, hidden), BF16), V((7, part, hidden), BF16),
            V((8, feat), F32),
            V((rows, feat), BF16), V((rows, feat), F32), V((rows, feat), BF16), V((part, hidden), BF16), V((part, hidden), BF16),
            pltpu.SemaphoreType.DMA((TRANSFERS,)),
            pltpu.SemaphoreType.DMA((TRANSFERS,)),
            pltpu.SemaphoreType.DMA((6,)),
        ],
        compiler_params=pltpu.CompilerParams(
            collective_id=0, has_side_effects=True, vmem_limit_bytes=63 * 2**20
        ),
        cost_estimate=pl.CostEstimate(flops=flops, bytes_accessed=8 * 2**20, transcendentals=2 * rows * hidden),
        name="block_gradient",
    )(tokens, target, mod_table, adv_table.T, bins, groups, w_up, w_down_t)
    return tuple(g.astype(F32) for g in grads)


def solution(mesh):
    return jax.shard_map(
        on_device,
        mesh=mesh,
        in_specs=(
            P("wide", "node"),
            P("wide", "node"),
            P(None, "node"),
            P(),
            P("wide", "node"),
            P("wide", "node"),
            P("wide"),
            P("wide"),
        ),
        out_specs=(P("wide", "node"), P("wide", "node"), P("wide", "node")),
        check_vma=False,
    )
```

```python
import jax
import jax.numpy as jnp
from jax import lax
from jax.experimental import pallas as pl
from jax.experimental.pallas import tpu as pltpu
from jax.sharding import PartitionSpec as P

F32 = jnp.float32
BF16 = jnp.bfloat16
MESH = pl.DeviceIdType.MESH
COEF = 0.7978845608028654


def dot_nn(a, b):
    return jnp.dot(a, b, preferred_element_type=F32)


def dot_nt(a, b):
    return lax.dot_general(a, b, (((1,), (1,)), ((), ())), preferred_element_type=F32)


def dot_tn(a, b):
    return lax.dot_general(a, b, (((0,), (0,)), ((), ())), preferred_element_type=F32)


def gelu_slope(v):
    th = jnp.tanh(COEF * (v + 0.044715 * v * v * v))
    return 0.5 * (1.0 + th) + 0.5 * v * (1.0 - th * th) * COEF * (1.0 + 3 * 0.044715 * v * v)


def tiles(rows, size, body):
    @pl.loop(0, rows // size)
    def _(t):
        body(pl.ds(pl.multiple_of(t * size, size), size))


def make_kernel(rows, feat, depth, hidden, micro, scale):
    seq = rows // micro

    def kernel(
        tok_in, tgt_in, mod_in, adv_in, bins_in, grps_in, wu_in, wd_in,
        gt_out, gu_out, gd_out,
        X, Y, Wu, Wd, pre, dh, hid, dpre, SB, RB, SGD, SIBD, SIBU, RGD, RGU, gain,
        bins, grps, tok, mod, adv, tgt, dpred, gt, gu, gd, ss, rs, ls,
    ):
        SGU = Wd
        wi, ni = lax.axis_index("wide"), lax.axis_index("node")
        xh, z, c = wi // 8, (wi // 2) % 4, wi % 2
        xl, y = ni // 4, ni % 4

        def nd(dx, dy):
            return ((xl + dx) % 2) * 4 + (y + dy + 4) % 4

        def wm(dx, dz):
            return ((xh + dx) % 2) * 4 + (z + dz + 4) % 4

        def dnode(dx, dy):
            return (wi, nd(dx, dy))

        def dwide(dx, dz):
            return (wm(dx, dz) * 2 + c, ni)

        sib = (wm(0, 0) * 2 + 1 - c, ni)

        table = {}
        count = [0]

        def add(name, src, dst, got, dev):
            table[name] = (count[0], src, dst, got, dev)
            count[0] += 1

        def desc(name, received):
            i, src, dst, got, dev = table[name]
            return pltpu.make_async_remote_copy(
                src_ref=got if received else src,
                dst_ref=got if received else dst,
                send_sem=ss.at[i],
                recv_sem=rs.at[i],
                device_id=dev,
                device_id_type=MESH,
            )

        def start(*names):
            for name in names:
                desc(name, False).start()

        def recv(*names):
            for name in names:
                desc(name, True).wait_recv()

        def sent(*names):
            for name in names:
                desc(name, False).wait_send()

        part = depth // 16
        mine, other = pl.multiple_of(c * part, part), pl.multiple_of((1 - c) * part, part)
        PC, PS = pl.ds(mine, part), pl.ds(other, part)
        Q1 = pl.ds(mine, part // 2)
        Q2 = pl.ds(pl.multiple_of(mine + part // 2, part // 2), part // 2)
        W = pl.ds(0, rows)
        half = rows // 2
        H1, H2 = pl.ds(0, half), pl.ds(half, half)
        K = [pl.ds(i * (half // 2), half // 2) for i in range(4)]

        def add_ag(p, B, fewer):
            def one(name, blk, r, got, dev):
                add(p + name, B.at[blk, r], B.at[blk, r], B.at[got, r], dev)

            for i, rp, rm in (("1", K[0], K[2]), ("2", K[1], K[3]), ("3", H2, H1)):
                one("yp" + i, nd(0, 0), rp, nd(0, -1), dnode(0, 1))
                one("ym" + i, nd(0, 0), rm, nd(0, 1), dnode(0, -1))
            for i, r in (("1", H1), ("2", H2)):
                one("x" + i, nd(0, 0), r, nd(1, 0), dnode(1, 0))
                one("bp" + i, nd(1, 0), r, nd(1, -1), dnode(0, 1))
                one("bm" + i, nd(1, 0), r, nd(1, 1), dnode(0, -1))
            for i, rp, rm in (("1", K[0], K[2]), ("2", K[1], K[3])):
                one("cp" + i, nd(0, -1), rp, nd(0, 2), dnode(0, 1))
                one("cm" + i, nd(0, 1), rm, nd(0, 2), dnode(0, -1))
                one("dp" + i, nd(0, 2), rp, nd(1, 2), dnode(1, 0))
                if not fewer:
                    one("dm" + i, nd(0, 2), rm, nd(1, 2), dnode(1, 0))
            if fewer:
                one("ep", nd(1, -1), K[2], nd(1, 2), dnode(0, 1))
                one("em", nd(1, 1), K[3], nd(1, 2), dnode(0, -1))

        def ag_names(p, fewer):
            names = ["yp", "ym", "x", "bp", "bm", "cp", "cm", "dp"] + ([] if fewer else ["dm"])
            last = ["yp3", "ym3"] + (["ep", "em"] if fewer else [])
            return [p + n + i for n in names for i in "12"] + [p + n for n in last]

        def add_wag(p, B, b0):
            def one(name, blk, r, got, dev):
                add(p + name, B.at[blk, r], B.at[blk, r], B.at[got, r], dev)

            one("x", wm(0, 0), PC, wm(1, 0), dwide(1, 0))
            for i, b in ((0, b0), (1, 1 - b0)):
                here, up, down, far = (b * 4 + (z + d) % 4 for d in (0, 1, 3, 2))
                one(f"zp{i}", here, Q1, down, dwide(0, 1))
                one(f"zm{i}", here, Q2, up, dwide(0, -1))
                one(f"yp{i}", here, Q2, down, dwide(0, 1))
                one(f"ym{i}", here, Q1, up, dwide(0, -1))
                one(f"cp{i}", down, Q1, far, dwide(0, 1))
                one(f"cm{i}", up, Q2, far, dwide(0, -1))
            base = count[0]
            count[0] += 8

            def share(b, received=False):
                r = PS if received else PC
                return pltpu.make_async_remote_copy(
                    src_ref=B.at[b, r],
                    dst_ref=B.at[b, r],
                    send_sem=ss.at[base + b],
                    recv_sem=rs.at[base + b],
                    device_id=sib,
                    device_id_type=MESH,
                )

            return share

        WAG = ("x",) + tuple(f"{n}{i}" for i in (0, 1) for n in ("zp", "zm", "yp", "ym", "cp", "cm"))

        def add_rs(p, R):
            def one(name, blk, r, slot, dev):
                add(p + name, SB.at[blk, r], R.at[slot, r], R.at[slot, r], dev)

            for i, r in (("1", H1), ("2", H2)):
                one("x" + i, nd(1, 2), r, 0, dnode(1, 0))
                one("bp" + i, nd(1, 1), r, 2, dnode(0, 1))
                one("bm" + i, nd(1, -1), r, 3, dnode(0, -1))
            one("ax", nd(1, 0), W, 4, dnode(1, 0))
            for i, rp, rm in (("1", K[0], K[2]), ("2", K[1], K[3])):
                one("cp" + i, nd(0, 2), rp, 1, dnode(0, 1))
                one("cm" + i, nd(0, 2), rm, 1, dnode(0, -1))
            for i, rp, rm in (("1", K[0], K[2]), ("2", K[1], K[3]), ("3", H2, H1)):
                one("ap" + i, nd(0, 1), rp, 5, dnode(0, 1))
                one("am" + i, nd(0, -1), rm, 6, dnode(0, -1))

        RSN = ["ax"] + [n + i for n in ("x", "bp", "bm", "cp", "cm", "ap", "am") for i in "12"] + ["ap3", "am3"]
        A1, A2 = pl.ds(0, part // 2), pl.ds(part // 2, part // 2)
        AW = pl.ds(0, part)

        def add_wrs(p, S, R, B, b0):
            def one(name, blk, r, slot, rr, dev):
                add(p + name, S.at[blk, r], R.at[slot, rr], R.at[slot, rr], dev)

            one("xa", wm(1, 0), Q1, 6, A1, dwide(1, 0))
            one("xb", wm(1, 0), Q2, 6, A2, dwide(1, 0))
            for i, b in ((0, b0), (1, 1 - b0)):
                up, down, far = (b * 4 + (z + d) % 4 for d in (1, 3, 2))
                one(f"cp{i}", far, Q1, i, A1, dwide(0, 1))
                one(f"cm{i}", far, Q2, i, A2, dwide(0, -1))
                for h, r, a in (("a", Q1, A1), ("b", Q2, A2)):
                    one(f"ap{i}{h}", up, r, 2 + 2 * i, a, dwide(0, 1))
                    one(f"am{i}{h}", down, r, 3 + 2 * i, a, dwide(0, -1))
            base = count[0]
            count[0] += 8

            def share(b):
                return pltpu.make_async_remote_copy(
                    src_ref=S.at[b, PS],
                    dst_ref=B.at[b],
                    send_sem=ss.at[base + b],
                    recv_sem=rs.at[base + b],
                    device_id=sib,
                    device_id_type=MESH,
                )

            return share

        RSW = ("xa", "xb") + tuple(n.format(i) for i in (0, 1) for n in ("cp{}", "cm{}", "ap{}a", "ap{}b", "am{}a", "am{}b"))
        add_ag("X", X, True)
        add_ag("Y", Y, False)
        share_u = add_wag("U", Wu, xh)
        share_d = add_wag("D", Wd, 1 - xl)
        add_rs("P", RB)
        add_rs("M", RB)
        sib_d = add_wrs("G", SGD, RGD, SIBD, xl)
        sib_u = add_wrs("H", SGU, RGU, SIBU, xl)

        barrier = pltpu.get_barrier_semaphore()
        for dev in (dnode(1, 0), dnode(0, 1), dnode(0, -1), dwide(1, 0), dwide(0, 1), dwide(0, -1), sib):
            pl.semaphore_signal(barrier, inc=1, device_id=dev, device_id_type=MESH)
        lu = pltpu.make_async_copy(wu_in, Wu.at[wm(0, 0), PC], ls.at[0])
        ld = pltpu.make_async_copy(wd_in, Wd.at[wm(0, 0), PC], ls.at[1])
        lt = pltpu.make_async_copy(tgt_in, tgt, ls.at[2])
        lk = pltpu.make_async_copy(tok_in, tok, ls.at[6])
        lm = pltpu.make_async_copy(mod_in, mod, ls.at[7])
        la = pltpu.make_async_copy(adv_in, adv, ls.at[8])
        lb = pltpu.make_async_copy(bins_in, bins, ls.at[9])
        lg = pltpu.make_async_copy(grps_in, grps, ls.at[10])
        lb.start()
        lg.start()
        lm.start()
        lk.start()
        la.start()
        lu.start()
        ld.start()
        lt.start()

        def back(src, dst, i):
            return pltpu.make_async_copy(src, dst, ls.at[3 + i])

        ng, nb = adv.shape
        lb.wait()
        lg.wait()
        lm.wait()
        lk.wait()
        row_i = lax.broadcasted_iota(jnp.int32, (nb, feat), 0)
        for s in range(micro):
            picked = jnp.sum(jnp.where(row_i == bins[s], mod[...].astype(F32), 0.0), axis=0, keepdims=True)
            gain[s : s + 1, :] = 1.0 + picked

            def modulate(r, s=s):
                q = pl.ds(pl.multiple_of(r.start + s * seq, 32), r.size)
                X[nd(0, 0), q, :] = (tok[q, :].astype(F32) * gain[s : s + 1, :]).astype(BF16)

            tiles(seq, 32, modulate)
        lu.wait()
        ld.wait()
        pl.semaphore_wait(barrier, 7)

        def ring_start(p, i):
            start(f"{p}zp{i}", f"{p}zm{i}", f"{p}yp{i}", f"{p}ym{i}")

        def ring_relay(p, i):
            recv(f"{p}zp{i}")
            start(f"{p}cp{i}")
            recv(f"{p}zm{i}")
            start(f"{p}cm{i}")

        def ring_share(p, i, b, share):
            recv(f"{p}yp{i}")
            share(b * 4 + (z + 3) % 4).start()
            recv(f"{p}ym{i}")
            share(b * 4 + (z + 1) % 4).start()

        def ring_end(p, i, b, share):
            recv(f"{p}cp{i}", f"{p}cm{i}")
            share(b * 4 + (z + 2) % 4).start()

        same = xh == xl
        start("Xyp1", "Xym1", "Xyp2", "Xym2", "Ux")
        ring_start("U", 0)
        start("Xyp3", "Xym3")
        share_u(wm(0, 0)).start()
        share_d(wm(0, 0)).start()

        @pl.when(~same)
        def _():
            start("Dx")

        start("Xx2", "Xx1")

        def zero(r):
            pre[r, :] = jnp.zeros((r.size, hidden), F32)
            dh[r, :] = jnp.zeros((r.size, hidden), F32)

        tiles(rows, 32, zero)
        ring_relay("U", 0)
        def far_relay(p):
            for d in ("p1", "m1", "p2", "m2"):
                recv(p + "y" + d)
                start(p + "c" + d)

        far_relay("X")
        recv("Ux")
        ring_start("U", 1)
        share_u(wm(1, 0)).start()
        ring_share("U", 0, xh, share_u)
        ring_end("U", 0, xh, share_u)
        ring_relay("U", 1)

        @pl.when(same)
        def _():
            recv("Dx")
            share_d(wm(1, 0)).start()

        ring_start("D", 0)
        recv("Xx2")
        start("Xbp2", "Xbm2")
        recv("Xcp1", "Xcp2")
        start("Xdp1", "Xdp2")
        recv("Xcm1", "Xcm2")

        @pl.when(same)
        def _():
            start("Dx")

        ring_share("U", 1, 1 - xh, share_u)
        ring_end("U", 1, 1 - xh, share_u)
        recv("Xyp3", "Xym3")

        @pl.loop(0, 8)
        def _(b):
            share_u(b, True).wait_recv()

        def arrival(k):
            dx = jnp.where((k == 3) | (k >= 5), 1, 0)
            dy = jnp.where((k == 1) | (k == 5), 1, jnp.where((k == 2) | (k == 6), 3, jnp.where((k == 4) | (k == 7), 2, 0)))
            return ((xl + dx) % 2) * 4 + (y + dy) % 4

        @pl.loop(0, 5)
        def _(k):
            @pl.when(k == 1)
            def _():
                recv("Xx1")
                start("Xbp1", "Xbm1")

            @pl.when(k == 2)
            def _():
                recv("Xbp2")
                start("Xep")
                recv("Xbm2")
                start("Xem")

            n = arrival(k)
            pre[...] += dot_nn(X[n], Wu[n])

        ring_relay("D", 0)
        ring_share("D", 0, 1 - xl, share_d)

        @pl.when(same)
        def _():
            ring_start("D", 1)

        def forward(i, r):
            if i == "1":
                recv("Xbp1", "Xbm1", "Xdp1", "Xdp2")
            else:
                recv("Xep", "Xem")

            @pl.loop(5, 8)
            def _(k):
                n = arrival(k)
                pre[r] += dot_nn(X[n, r], Wu[n])

            def activate(t):
                q = pl.ds(pl.multiple_of(t.start + r.start, 32), t.size)
                hid[q, :] = jax.nn.gelu(pre[q, :], approximate=True).astype(BF16)

            if i == "1":
                ring_end("D", 0, 1 - xl, share_d)
            tiles(r.size, 32, activate)
            if i == "1":
                wait_column(1 - xl, share_d)
            products("P", hid, Wd, 0, 3, r)

        def departure(k):
            dx = jnp.where(k <= 3, 1, 0)
            dy = jnp.where((k == 0) | (k == 4), 2, jnp.where((k == 1) | (k == 5), 1, jnp.where((k == 2) | (k == 6), 3, 0)))
            return ((xl + dx) % 2) * 4 + (y + dy) % 4

        def products(p, left, weight, first, last, r=W):
            @pl.loop(first, last)
            def _(k):
                n = departure(k)
                SB[n, r] = dot_nt(left[r], weight[n]).astype(BF16)
                for at, name in ((0, "x"), (1, "bp"), (2, "bm")):
                    if first <= at < last:

                        @pl.when(k == at)
                        def _(name=name):
                            if r.start == 0:
                                start(p + name + "1")
                            if r.start + r.size == rows:
                                start(p + name + "2")

                for at, name in ((5, "ap3"), (6, "am3")):
                    if first <= at < last:

                        @pl.when(k == at)
                        def _(name=name):
                            start(p + name)

        def plus(blk, r0, size, R, *slots):
            def body(r):
                q = pl.ds(pl.multiple_of(r.start + r0, 32), r.size)
                v = SB[blk, q, :].astype(F32)
                for slot in slots:
                    v = v + R[slot, q, :].astype(F32)
                SB[blk, q, :] = v.astype(BF16)

            tiles(size, 32, body)

        def rs_first(p, R):
            recv(p + "x1")
            plus(nd(0, 2), 0, half, R, 0)
            start(p + "cp1", p + "cp2")
            recv(p + "x2")
            plus(nd(0, 2), half, half, R, 0)
            start(p + "cm1", p + "cm2")

        def rs_second(p, R):
            recv(*[p + n + i for i in "12" for n in ("bp", "bm")])
            plus(nd(1, 0), 0, rows, R, 2, 3)
            start(p + "ax")

        def rs_third(p, R):
            for i, r in ((1, 0), (2, 1)):
                recv(f"{p}cp{i}")
                plus(nd(0, 1), K[r].start, half // 2, R, 1)
                start(f"{p}ap{i}")
                recv(f"{p}cm{i}")
                plus(nd(0, -1), K[r + 2].start, half // 2, R, 1)
                start(f"{p}am{i}")

        def rs_end(p, i):
            if i == 1:
                recv(p + "ax", p + "ap3", p + "am3")
            recv(f"{p}ap{i}", f"{p}am{i}")

        def wait_column(b, share):
            for d in range(4):
                share(b * 4 + d, True).wait_recv()

        forward("1", H1)

        @pl.when(~same)
        def _():
            recv("Dx")
            share_d(wm(1, 0)).start()
            ring_start("D", 1)

        forward("2", H2)
        products("P", hid, Wd, 3, 4)
        ring_relay("D", 1)
        ring_share("D", 1, xl, share_d)
        ring_end("D", 1, xl, share_d)
        wait_column(xl, share_d)
        products("P", hid, Wd, 4, 5)
        rs_first("P", RB)
        products("P", hid, Wd, 5, 8)
        rs_second("P", RB)
        rs_third("P", RB)
        rs_end("P", 1)
        lt.wait()
        la.wait()

        def total(R, q):
            v = SB[nd(0, 0), q, :].astype(F32) + R[4, q, :].astype(F32)
            return v + R[5, q, :].astype(F32) + R[6, q, :].astype(F32)

        bin_i = lax.broadcasted_iota(jnp.int32, (ng, nb), 1)
        grp_i = lax.broadcasted_iota(jnp.int32, (ng, nb), 0)
        weight = []
        for s in range(micro):
            chosen = jnp.where((bin_i == bins[s]) & (grp_i == grps[s]), adv[...], 0.0)
            weight.append(jnp.sum(jnp.sum(chosen, axis=1, keepdims=True), axis=0, keepdims=True))

        def error(k):
            begin, end = K[k].start, K[k].start + K[k].size
            for s in range(micro):
                lo, hi = max(begin, s * seq), min(end, (s + 1) * seq)

                def body(r, s=s, lo=lo):
                    q = pl.ds(pl.multiple_of(r.start + lo, 32), r.size)
                    d = weight[s] * (tok[q, :].astype(F32) + total(RB, q) - tgt[q, :].astype(F32))
                    dpred[q, :] = d
                    Y[nd(0, 0), q, :] = d.astype(BF16)

                if lo < hi:
                    tiles(hi - lo, 32, body)

        error(0)
        error(2)
        start("Yyp1", "Yym1")
        rs_end("P", 2)
        error(1)
        error(3)
        start("Yyp2", "Yym2", "Yx1", "Yx2", "Yyp3", "Yym3")
        sent(*["P" + n for n in RSN])

        def stage_down(m):
            SGD[m] = (dot_tn(Y[m], hid[...]) * scale).astype(BF16)
            sib_d(m).start()

        def stage_up(m):
            SGU[m] = (dot_tn(X[m], dpre[...]) * scale).astype(BF16)
            sib_u(m).start()

        def wide_plus(S, blk, slots, r0, size):
            def body(r):
                a = pl.ds(pl.multiple_of(r.start + r0, 32), r.size)
                q = pl.ds(pl.multiple_of(mine + r.start + r0, 32), r.size)
                v = S[blk, q, :].astype(F32)
                for ref, slot in slots:
                    v = v + ref[slot, a, :].astype(F32)
                S[blk, q, :] = v.astype(BF16)

            tiles(size, 32, body)

        quarter = part // 2

        def wide_first(p, i, b, S, B, share):
            m = b * 4 + (z + 2) % 4
            share(m).wait_recv()
            wide_plus(S, m, ((B, m),), 0, part)
            start(f"{p}cp{i}", f"{p}cm{i}")

        def wide_early(p, i, b, S, B, share):
            up, down = b * 4 + (z + 1) % 4, b * 4 + (z + 3) % 4
            share(up).wait_recv()
            wide_plus(S, up, ((B, up),), quarter, quarter)
            start(f"{p}ap{i}b")
            share(down).wait_recv()
            wide_plus(S, down, ((B, down),), 0, quarter)
            start(f"{p}am{i}a")

        def wide_second(p, i, b, S, B, R, share):
            up, down = b * 4 + (z + 1) % 4, b * 4 + (z + 3) % 4
            recv(f"{p}cp{i}")
            wide_plus(S, up, ((B, up), (R, i)), 0, quarter)
            start(f"{p}ap{i}a")
            recv(f"{p}cm{i}")
            wide_plus(S, down, ((B, down), (R, i)), quarter, quarter)
            start(f"{p}am{i}b")
            share(b * 4 + z).wait_recv()

        def wide_step(p, i, b, S, B, R, share):
            up, down = b * 4 + (z + 1) % 4, b * 4 + (z + 3) % 4
            recv(f"{p}cp{i}", f"{p}cm{i}")
            share(up).wait_recv()
            wide_plus(S, up, ((B, up), (R, i)), 0, quarter)
            start(f"{p}ap{i}a")
            share(down).wait_recv()
            wide_plus(S, down, ((B, down),), 0, quarter)
            start(f"{p}am{i}a")
            wide_plus(S, up, ((B, up),), quarter, quarter)
            start(f"{p}ap{i}b")
            wide_plus(S, down, ((B, down), (R, i)), quarter, quarter)
            start(f"{p}am{i}b")
            share(b * 4 + z).wait_recv()

        def wide_third(p, i, b, S, B, R):
            m = b * 4 + z
            for h, r0 in (("a", 0), ("b", quarter)):
                recv(f"{p}ap{i}{h}", f"{p}am{i}{h}")

                @pl.when(xh != b)
                def _(h=h, r0=r0):
                    wide_plus(S, m, ((B, m), (R, 2 + 2 * i), (R, 3 + 2 * i)), r0, quarter)
                    start(p + "x" + h)

        def wide_last(p, b0, S, B, R, out):
            recv(p + "xa", p + "xb")
            m = wm(0, 0)
            slot = jnp.where(xh == b0, 2, 4)

            def body(r):
                q = pl.ds(pl.multiple_of(mine + r.start, 32), r.size)
                v = S[m, q, :].astype(F32) + B[m, r, :].astype(F32)
                v = v + R[slot, r, :].astype(F32) + R[slot + 1, r, :].astype(F32)
                out[r, :] = (v + R[6, r, :].astype(F32)).astype(BF16)

            tiles(part, 32, body)

        G0 = ("G", 0, xl, SGD, SIBD)
        G1 = ("G", 1, 1 - xl, SGD, SIBD)
        U0 = ("H", 0, xl, SGU, SIBU)
        U1 = ("H", 1, 1 - xl, SGU, SIBU)

        @pl.loop(0, 5)
        def _(k):
            @pl.when(k == 1)
            def _():
                far_relay("Y")
                recv("Yx1")
                start("Ybp1", "Ybm1")
                recv("Yx2")
                start("Ybp2", "Ybm2")
                recv("Yyp3", "Yym3")

            @pl.when(k == 4)
            def _():
                for d in ("p1", "p2", "m1", "m2"):
                    recv("Yc" + d)
                    start("Yd" + d)

            n = arrival(k)

            @pl.when(k != 3)
            def _():
                stage_down(n)

            @pl.when(k != 4)
            def _():
                dh[...] += dot_nn(Y[n], Wd[n])

        wide_first(*G0, sib_d)
        wide_early(*G0, sib_d)
        last = arrival(4)
        dh[...] += dot_nn(Y[last], Wd[last])
        wide_second(*G0, RGD, sib_d)
        def backward(i, r):
            recv(*["Y" + n + i for n in ("bp", "bm")], *["Yd" + "pm"[int(i) - 1] + j for j in "12"])
            if i == "2":
                stage_down((1 - xl) * 4 + (z + 2) % 4)

            def more(first, last):
                @pl.loop(first, last)
                def _(k):
                    n = arrival(k)
                    dh[r] += dot_nn(Y[n, r], Wd[n])

            more(5, 7)
            if i == "2":
                wide_first(*G1, sib_d)
            more(7, 8)

            def slope(t):
                q = pl.ds(pl.multiple_of(t.start + r.start, 32), t.size)
                dpre[q, :] = (dh[q, :] * gelu_slope(pre[q, :])).astype(BF16)

            tiles(r.size, 32, slope)
            if i == "2":

                @pl.loop(0, 2)
                def _(k):
                    stage_up(((xl + k) % 2) * 4 + (z + 2) % 4)

            products("M", dpre, Wu, 0, 3, r)
            if i == "2":
                wide_third("G", 0, xl, SGD, SIBD, RGD)

        backward("1", H1)
        sent(*["D" + n for n in WAG])

        @pl.loop(0, 8)
        def _(b):
            share_d(b).wait_send()

        backward("2", H2)
        wide_first(*U0, sib_u)
        wide_first(*U1, sib_u)
        products("M", dpre, Wu, 4, 5)

        @pl.loop(0, 3)
        def _(k):
            stage_down((1 - xl) * 4 + (z + 3 + k) % 4)

        rs_first("M", RB)
        wide_early(*G1, sib_d)
        wide_second(*G1, RGD, sib_d)
        products("M", dpre, Wu, 3, 4)
        rs_second("M", RB)
        products("M", dpre, Wu, 5, 8)

        @pl.loop(0, 3)
        def _(k):
            stage_up(xl * 4 + (z + 3 + k) % 4)

        wide_early(*U0, sib_u)
        wide_second(*U0, RGU, sib_u)
        rs_third("M", RB)

        @pl.loop(0, 3)
        def _(k):
            stage_up((1 - xl) * 4 + (z + 3 + k) % 4)

        wide_step(*U1, RGU, sib_u)
        wide_third("G", 1, 1 - xl, SGD, SIBD, RGD)
        wide_third("H", 0, xl, SGU, SIBU, RGU)
        rs_end("M", 1)
        rs_end("M", 2)
        for s in range(micro):

            def finish(r, s=s):
                q = pl.ds(pl.multiple_of(r.start + s * seq, 32), r.size)
                gt[q, :] = (dpred[q, :] + gain[s : s + 1, :] * total(RB, q)).astype(BF16)

            tiles(seq, 32, finish)
        back(gt, gt_out, 1).start()
        wide_third("H", 1, 1 - xl, SGU, SIBU, RGU)
        wide_last("G", xl, SGD, SIBD, RGD, gd)
        back(gd, gd_out, 0).start()
        wide_last("H", xl, SGU, SIBU, RGU, gu)
        back(gu, gu_out, 2).start()

        sent(*ag_names("X", True), *ag_names("Y", False), *["U" + n for n in WAG], *["M" + n for n in RSN])
        sent(*["G" + n for n in RSW], *["H" + n for n in RSW])

        @pl.loop(0, 8)
        def _(b):
            share_u(b).wait_send()
            sib_d(b).wait_send()
            sib_u(b).wait_send()

        back(gd, gd_out, 0).wait()
        back(gt, gt_out, 1).wait()
        back(gu, gu_out, 2).wait()

    return kernel


TRANSFERS = 160


def widen(*arrays):
    pieces = 2

    def kernel(*refs):
        n = len(arrays)
        src, dst, inner, outer, sems = refs[:n], refs[n : 2 * n], refs[2 * n : 3 * n], refs[3 * n : 4 * n], refs[4 * n]

        def copies(i, j):
            size = arrays[i].shape[0] // pieces
            r = pl.ds(j * size, size)
            return (
                pltpu.make_async_copy(src[i].at[r], inner[i].at[r], sems.at[0, i, j]),
                pltpu.make_async_copy(outer[i].at[r], dst[i].at[r], sems.at[1, i, j]),
                r,
            )

        every = [copies(i, j) for i in range(n) for j in range(pieces)]
        for read, _, _ in every:
            read.start()
        for k, (read, write, r) in enumerate(every):
            i = k // pieces
            read.wait()

            def body(t, i=i, r=r):
                q = pl.ds(pl.multiple_of(t.start + r.start, 32), t.size)
                outer[i][q, :] = inner[i][q, :].astype(F32)

            tiles(r.size, 32, body)
            write.start()
        for _, write, _ in every:
            write.wait()

    anys = pl.BlockSpec(memory_space=pl.ANY)
    return pl.pallas_call(
        kernel,
        out_shape=tuple(jax.ShapeDtypeStruct(a.shape, F32) for a in arrays),
        in_specs=[anys] * len(arrays),
        out_specs=(anys,) * len(arrays),
        scratch_shapes=[pltpu.VMEM(a.shape, BF16) for a in arrays]
        + [pltpu.VMEM(a.shape, F32) for a in arrays]
        + [pltpu.SemaphoreType.DMA((2, len(arrays), pieces))],
        compiler_params=pltpu.CompilerParams(vmem_limit_bytes=63 * 2**20),
        cost_estimate=pl.CostEstimate(flops=0, bytes_accessed=6 * sum(a.size for a in arrays), transcendentals=0),
        name="widen",
    )(*arrays)


def on_device(tokens, target, mod_table, adv_table, w_up, w_down_t, bins, groups):
    rows, feat = tokens.shape
    part, hidden = w_up.shape
    depth = part * 16
    micro = bins.shape[0]
    scale = float(16 * rows) ** (-0.5)
    anys = pl.BlockSpec(memory_space=pl.ANY)
    block = (8, rows, feat)
    wblock = (8, depth // 8, hidden)
    V = pltpu.VMEM
    flops = 6 * 2 * rows * depth * hidden
    grads = pl.pallas_call(
        make_kernel(rows, feat, depth, hidden, micro, scale),
        out_shape=(
            jax.ShapeDtypeStruct((rows, feat), BF16),
            jax.ShapeDtypeStruct((part, hidden), BF16),
            jax.ShapeDtypeStruct((part, hidden), BF16),
        ),
        in_specs=[anys] * 8,
        out_specs=(anys, anys, anys),
        scratch_shapes=[
            V(block, BF16), V(block, BF16), V(wblock, BF16), V(wblock, BF16),
            V((rows, hidden), F32), V((rows, hidden), F32), V((rows, hidden), BF16), V((rows, hidden), BF16),
            V(block, BF16), V((7, rows, feat), BF16),
            V(wblock, BF16), V((8, part, hidden), BF16), V((8, part, hidden), BF16),
            V((7, part, hidden), BF16), V((7, part, hidden), BF16),
            V((8, feat), F32),
            pltpu.SMEM(bins.shape, jnp.int32), pltpu.SMEM(groups.shape, jnp.int32),
            V((rows, feat), BF16), V(mod_table.shape, BF16), V(adv_table.shape[::-1], F32),
            V((rows, feat), BF16), V((rows, feat), F32), V((rows, feat), BF16), V((part, hidden), BF16), V((part, hidden), BF16),
            pltpu.SemaphoreType.DMA((TRANSFERS,)),
            pltpu.SemaphoreType.DMA((TRANSFERS,)),
            pltpu.SemaphoreType.DMA((11,)),
        ],
        compiler_params=pltpu.CompilerParams(
            collective_id=0, has_side_effects=True, vmem_limit_bytes=63 * 2**20
        ),
        cost_estimate=pl.CostEstimate(flops=flops, bytes_accessed=8 * 2**20, transcendentals=2 * rows * hidden),
        name="block_gradient",
    )(tokens, target, mod_table, adv_table.T, bins, groups, w_up, w_down_t)
    return widen(*grads)


def solution(mesh):
    return jax.shard_map(
        on_device,
        mesh=mesh,
        in_specs=(
            P("wide", "node"),
            P("wide", "node"),
            P(None, "node"),
            P(),
            P("wide", "node"),
            P("wide", "node"),
            P("wide"),
            P("wide"),
        ),
        out_specs=(P("wide", "node"), P("wide", "node"), P("wide", "node")),
        check_vma=False,
    )
```

```python
import jax
import jax.numpy as jnp
from jax import lax
from jax.experimental import pallas as pl
from jax.experimental.pallas import tpu as pltpu
from jax.sharding import PartitionSpec as P

F32 = jnp.float32
BF16 = jnp.bfloat16
MESH = pl.DeviceIdType.MESH
COEF = 0.7978845608028654


def dot_nn(a, b):
    return jnp.dot(a, b, preferred_element_type=F32)


def dot_nt(a, b):
    return lax.dot_general(a, b, (((1,), (1,)), ((), ())), preferred_element_type=F32)


def dot_tn(a, b):
    return lax.dot_general(a, b, (((0,), (0,)), ((), ())), preferred_element_type=F32)


def gelu_slope(v):
    th = jnp.tanh(COEF * (v + 0.044715 * v * v * v))
    return 0.5 * (1.0 + th) + 0.5 * v * (1.0 - th * th) * COEF * (1.0 + 3 * 0.044715 * v * v)


def tiles(rows, size, body):
    @pl.loop(0, rows // size)
    def _(t):
        body(pl.ds(pl.multiple_of(t * size, size), size))


def make_kernel(rows, feat, depth, hidden, micro, scale):
    seq = rows // micro

    def kernel(
        tok_in, tgt_in, mod_in, adv_in, bins_in, grps_in, wu_in, wd_in,
        gt_out, gu_out, gd_out,
        X, Y, Wu, Wd, pre, dh, hid, dpre, SB, RB, SGD, SIBD, SIBU, RGD, RGU, gain,
        bins, grps, tok, mod, adv, tgt, dpred, gt, gu, gd, ss, rs, ls,
    ):
        SGU = Wd
        wi, ni = lax.axis_index("wide"), lax.axis_index("node")
        xh, z, c = wi // 8, (wi // 2) % 4, wi % 2
        xl, y = ni // 4, ni % 4

        def nd(dx, dy):
            return ((xl + dx) % 2) * 4 + (y + dy + 4) % 4

        def wm(dx, dz):
            return ((xh + dx) % 2) * 4 + (z + dz + 4) % 4

        def dnode(dx, dy):
            return (wi, nd(dx, dy))

        def dwide(dx, dz):
            return (wm(dx, dz) * 2 + c, ni)

        sib = (wm(0, 0) * 2 + 1 - c, ni)

        table = {}
        count = [0]

        def add(name, src, dst, got, dev):
            table[name] = (count[0], src, dst, got, dev)
            count[0] += 1

        def desc(name, received):
            i, src, dst, got, dev = table[name]
            return pltpu.make_async_remote_copy(
                src_ref=got if received else src,
                dst_ref=got if received else dst,
                send_sem=ss.at[i],
                recv_sem=rs.at[i],
                device_id=dev,
                device_id_type=MESH,
            )

        def start(*names):
            for name in names:
                desc(name, False).start()

        def recv(*names):
            for name in names:
                desc(name, True).wait_recv()

        def sent(*names):
            for name in names:
                desc(name, False).wait_send()

        part = depth // 16
        mine, other = pl.multiple_of(c * part, part), pl.multiple_of((1 - c) * part, part)
        PC, PS = pl.ds(mine, part), pl.ds(other, part)
        Q1 = pl.ds(mine, part // 2)
        Q2 = pl.ds(pl.multiple_of(mine + part // 2, part // 2), part // 2)
        W = pl.ds(0, rows)
        half = rows // 2
        H1, H2 = pl.ds(0, half), pl.ds(half, half)
        K = [pl.ds(i * (half // 2), half // 2) for i in range(4)]

        def add_ag(p, B, fewer):
            def one(name, blk, r, got, dev):
                add(p + name, B.at[blk, r], B.at[blk, r], B.at[got, r], dev)

            for i, rp, rm in (("1", K[0], K[2]), ("2", K[1], K[3]), ("3", H2, H1)):
                one("yp" + i, nd(0, 0), rp, nd(0, -1), dnode(0, 1))
                one("ym" + i, nd(0, 0), rm, nd(0, 1), dnode(0, -1))
            for i, r in (("1", H1), ("2", H2)):
                one("x" + i, nd(0, 0), r, nd(1, 0), dnode(1, 0))
                one("bp" + i, nd(1, 0), r, nd(1, -1), dnode(0, 1))
                one("bm" + i, nd(1, 0), r, nd(1, 1), dnode(0, -1))
            for i, rp, rm in (("1", K[0], K[2]), ("2", K[1], K[3])):
                one("cp" + i, nd(0, -1), rp, nd(0, 2), dnode(0, 1))
                one("cm" + i, nd(0, 1), rm, nd(0, 2), dnode(0, -1))
                one("dp" + i, nd(0, 2), rp, nd(1, 2), dnode(1, 0))
                if not fewer:
                    one("dm" + i, nd(0, 2), rm, nd(1, 2), dnode(1, 0))
            if fewer:
                one("ep", nd(1, -1), K[2], nd(1, 2), dnode(0, 1))
                one("em", nd(1, 1), K[3], nd(1, 2), dnode(0, -1))

        def ag_names(p, fewer):
            names = ["yp", "ym", "x", "bp", "bm", "cp", "cm", "dp"] + ([] if fewer else ["dm"])
            last = ["yp3", "ym3"] + (["ep", "em"] if fewer else [])
            return [p + n + i for n in names for i in "12"] + [p + n for n in last]

        def add_wag(p, B, b0):
            def one(name, blk, r, got, dev):
                add(p + name, B.at[blk, r], B.at[blk, r], B.at[got, r], dev)

            one("x", wm(0, 0), PC, wm(1, 0), dwide(1, 0))
            for i, b in ((0, b0), (1, 1 - b0)):
                here, up, down, far = (b * 4 + (z + d) % 4 for d in (0, 1, 3, 2))
                one(f"zp{i}", here, Q1, down, dwide(0, 1))
                one(f"zm{i}", here, Q2, up, dwide(0, -1))
                one(f"yp{i}", here, Q2, down, dwide(0, 1))
                one(f"ym{i}", here, Q1, up, dwide(0, -1))
                one(f"cp{i}", down, Q1, far, dwide(0, 1))
                one(f"cm{i}", up, Q2, far, dwide(0, -1))
            base = count[0]
            count[0] += 8

            def share(b, received=False):
                r = PS if received else PC
                return pltpu.make_async_remote_copy(
                    src_ref=B.at[b, r],
                    dst_ref=B.at[b, r],
                    send_sem=ss.at[base + b],
                    recv_sem=rs.at[base + b],
                    device_id=sib,
                    device_id_type=MESH,
                )

            return share

        WAG = ("x",) + tuple(f"{n}{i}" for i in (0, 1) for n in ("zp", "zm", "yp", "ym", "cp", "cm"))

        def add_rs(p, R):
            def one(name, blk, r, slot, dev):
                add(p + name, SB.at[blk, r], R.at[slot, r], R.at[slot, r], dev)

            for i, r in (("1", H1), ("2", H2)):
                one("x" + i, nd(1, 2), r, 0, dnode(1, 0))
                one("bp" + i, nd(1, 1), r, 2, dnode(0, 1))
                one("bm" + i, nd(1, -1), r, 3, dnode(0, -1))
            one("ax1", nd(1, 0), H1, 4, dnode(1, 0))
            one("ax2", nd(1, 0), H2, 4, dnode(1, 0))
            for i, rp, rm in (("1", K[0], K[2]), ("2", K[1], K[3])):
                one("cp" + i, nd(0, 2), rp, 1, dnode(0, 1))
                one("cm" + i, nd(0, 2), rm, 1, dnode(0, -1))
            for i, rp, rm in (("1", K[0], K[2]), ("2", K[1], K[3]), ("3", H2, H1)):
                one("ap" + i, nd(0, 1), rp, 5, dnode(0, 1))
                one("am" + i, nd(0, -1), rm, 6, dnode(0, -1))

        RSN = [n + i for n in ("x", "ax", "bp", "bm", "cp", "cm", "ap", "am") for i in "12"] + ["ap3", "am3"]
        A1, A2 = pl.ds(0, part // 2), pl.ds(part // 2, part // 2)
        AW = pl.ds(0, part)

        def add_wrs(p, S, R, B, b0):
            def one(name, blk, r, slot, rr, dev):
                add(p + name, S.at[blk, r], R.at[slot, rr], R.at[slot, rr], dev)

            one("xa", wm(1, 0), Q1, 6, A1, dwide(1, 0))
            one("xb", wm(1, 0), Q2, 6, A2, dwide(1, 0))
            for i, b in ((0, b0), (1, 1 - b0)):
                up, down, far = (b * 4 + (z + d) % 4 for d in (1, 3, 2))
                one(f"cp{i}", far, Q1, i, A1, dwide(0, 1))
                one(f"cm{i}", far, Q2, i, A2, dwide(0, -1))
                for h, r, a in (("a", Q1, A1), ("b", Q2, A2)):
                    one(f"ap{i}{h}", up, r, 2 + 2 * i, a, dwide(0, 1))
                    one(f"am{i}{h}", down, r, 3 + 2 * i, a, dwide(0, -1))
            base = count[0]
            count[0] += 8

            def share(b):
                return pltpu.make_async_remote_copy(
                    src_ref=S.at[b, PS],
                    dst_ref=B.at[b],
                    send_sem=ss.at[base + b],
                    recv_sem=rs.at[base + b],
                    device_id=sib,
                    device_id_type=MESH,
                )

            return share

        RSW = ("xa", "xb") + tuple(n.format(i) for i in (0, 1) for n in ("cp{}", "cm{}", "ap{}a", "ap{}b", "am{}a", "am{}b"))
        add_ag("X", X, True)
        add_ag("Y", Y, False)
        share_u = add_wag("U", Wu, xh)
        share_d = add_wag("D", Wd, 1 - xl)
        add_rs("P", RB)
        add_rs("M", RB)
        sib_d = add_wrs("G", SGD, RGD, SIBD, xl)
        sib_u = add_wrs("H", SGU, RGU, SIBU, xl)
        assert count[0] <= TRANSFERS, count[0]

        barrier = pltpu.get_barrier_semaphore()
        for dev in (dnode(1, 0), dnode(0, 1), dnode(0, -1), dwide(1, 0), dwide(0, 1), dwide(0, -1), sib):
            pl.semaphore_signal(barrier, inc=1, device_id=dev, device_id_type=MESH)
        lu = pltpu.make_async_copy(wu_in, Wu.at[wm(0, 0), PC], ls.at[0])
        ld = pltpu.make_async_copy(wd_in, Wd.at[wm(0, 0), PC], ls.at[1])
        lt = pltpu.make_async_copy(tgt_in, tgt, ls.at[2])
        lk = pltpu.make_async_copy(tok_in, tok, ls.at[6])
        lm = pltpu.make_async_copy(mod_in, mod, ls.at[7])
        la = pltpu.make_async_copy(adv_in, adv, ls.at[8])
        lb = pltpu.make_async_copy(bins_in, bins, ls.at[9])
        lg = pltpu.make_async_copy(grps_in, grps, ls.at[10])
        lb.start()
        lg.start()
        lm.start()
        lk.start()
        la.start()
        lu.start()
        ld.start()
        lt.start()

        def back(src, dst, i):
            return pltpu.make_async_copy(src, dst, ls.at[3 + i])

        ng, nb = adv.shape
        lb.wait()
        lg.wait()
        lm.wait()
        lk.wait()
        row_i = lax.broadcasted_iota(jnp.int32, (nb, feat), 0)
        for s in range(micro):
            picked = jnp.sum(jnp.where(row_i == bins[s], mod[...].astype(F32), 0.0), axis=0, keepdims=True)
            gain[s : s + 1, :] = 1.0 + picked

            def modulate(r, s=s):
                q = pl.ds(pl.multiple_of(r.start + s * seq, 32), r.size)
                X[nd(0, 0), q, :] = (tok[q, :].astype(F32) * gain[s : s + 1, :]).astype(BF16)

            tiles(seq, 32, modulate)
        lu.wait()
        ld.wait()
        pl.semaphore_wait(barrier, 7)

        def ring_start(p, i):
            start(f"{p}zp{i}", f"{p}zm{i}", f"{p}yp{i}", f"{p}ym{i}")

        def ring_relay(p, i):
            recv(f"{p}zp{i}")
            start(f"{p}cp{i}")
            recv(f"{p}zm{i}")
            start(f"{p}cm{i}")

        def ring_share(p, i, b, share):
            recv(f"{p}yp{i}")
            share(b * 4 + (z + 3) % 4).start()
            recv(f"{p}ym{i}")
            share(b * 4 + (z + 1) % 4).start()

        def ring_end(p, i, b, share):
            recv(f"{p}cp{i}", f"{p}cm{i}")
            share(b * 4 + (z + 2) % 4).start()

        same = xh == xl
        start("Xyp1", "Xym1", "Xyp2", "Xym2", "Ux")
        ring_start("U", 0)
        start("Xyp3", "Xym3")
        share_u(wm(0, 0)).start()
        share_d(wm(0, 0)).start()

        @pl.when(~same)
        def _():
            start("Dx")

        start("Xx2")

        @pl.when(same)
        def _():
            start("Dx")

        start("Xx1")

        def zero(r):
            pre[r, :] = jnp.zeros((r.size, hidden), F32)
            dh[r, :] = jnp.zeros((r.size, hidden), F32)

        tiles(rows, 32, zero)
        ring_relay("U", 0)
        def far_relay(p):
            for d in ("p1", "m1", "p2", "m2"):
                recv(p + "y" + d)
                start(p + "c" + d)

        far_relay("X")
        recv("Ux")
        ring_start("U", 1)
        share_u(wm(1, 0)).start()
        ring_share("U", 0, xh, share_u)
        ring_end("U", 0, xh, share_u)
        ring_relay("U", 1)

        @pl.when(same)
        def _():
            recv("Dx")
            share_d(wm(1, 0)).start()

        ring_start("D", 0)
        recv("Xx2")
        start("Xbp2", "Xbm2")
        recv("Xcp1", "Xcp2")
        start("Xdp1", "Xdp2")
        recv("Xcm1", "Xcm2")
        ring_share("U", 1, 1 - xh, share_u)
        ring_end("U", 1, 1 - xh, share_u)
        recv("Xyp3", "Xym3")

        @pl.loop(0, 8)
        def _(b):
            share_u(b, True).wait_recv()

        def arrival(k):
            dx = jnp.where((k == 3) | (k >= 5), 1, 0)
            dy = jnp.where((k == 1) | (k == 5), 1, jnp.where((k == 2) | (k == 6), 3, jnp.where((k == 4) | (k == 7), 2, 0)))
            return ((xl + dx) % 2) * 4 + (y + dy) % 4

        @pl.loop(0, 5)
        def _(k):
            @pl.when(k == 1)
            def _():
                recv("Xbp2")
                start("Xep")
                recv("Xbm2")
                start("Xem")
                recv("Xx1")
                start("Xbp1", "Xbm1")

            @pl.when(k == 2)
            def _():
                ring_relay("D", 0)

            n = arrival(k)
            pre[...] += dot_nn(X[n], Wu[n])

        ring_share("D", 0, 1 - xl, share_d)

        @pl.when(~same)
        def _():
            recv("Dx")
            share_d(wm(1, 0)).start()

        ring_start("D", 1)

        def forward(i, r):
            if i == "1":
                recv("Xbp1", "Xbm1", "Xdp1", "Xdp2")
            else:
                recv("Xep", "Xem")

            @pl.loop(5, 8)
            def _(k):
                n = arrival(k)
                pre[r] += dot_nn(X[n, r], Wu[n])

            def activate(t):
                q = pl.ds(pl.multiple_of(t.start + r.start, 32), t.size)
                hid[q, :] = jax.nn.gelu(pre[q, :], approximate=True).astype(BF16)

            if i == "2":
                ring_end("D", 0, 1 - xl, share_d)
            tiles(r.size, 32, activate)
            if i == "2":
                wait_column(1 - xl, share_d)
            products("P", hid, Wd, 0, 3, r)

        def departure(k):
            dx = jnp.where(k <= 3, 1, 0)
            dy = jnp.where((k == 0) | (k == 4), 2, jnp.where((k == 1) | (k == 5), 1, jnp.where((k == 2) | (k == 6), 3, 0)))
            return ((xl + dx) % 2) * 4 + (y + dy) % 4

        def products(p, left, weight, first, last, r=W):
            @pl.loop(first, last)
            def _(k):
                n = departure(k)
                SB[n, r] = dot_nt(left[r], weight[n]).astype(BF16)
                for at, name in ((0, "x"), (1, "bp"), (2, "bm")):
                    if first <= at < last:

                        @pl.when(k == at)
                        def _(name=name):
                            if r.start == 0:
                                start(p + name + "1")
                            if r.start + r.size == rows:
                                start(p + name + "2")

                for at, name in ((5, "ap3"), (6, "am3")):
                    if first <= at < last:

                        @pl.when(k == at)
                        def _(name=name):
                            start(p + name)

        def plus(blk, r0, size, R, *slots):
            def body(r):
                q = pl.ds(pl.multiple_of(r.start + r0, 32), r.size)
                v = SB[blk, q, :].astype(F32)
                for slot in slots:
                    v = v + R[slot, q, :].astype(F32)
                SB[blk, q, :] = v.astype(BF16)

            tiles(size, 32, body)

        def rs_first(p, R, order):
            for i in order:
                recv(p + "x" + i)
                plus(nd(0, 2), half * (int(i) - 1), half, R, 0)
                d = "cp" if i == "1" else "cm"
                start(p + d + "1", p + d + "2")

        def rs_second(p, R, order):
            for i in order:
                recv(p + "bp" + i, p + "bm" + i)
                plus(nd(1, 0), half * (int(i) - 1), half, R, 2, 3)
                start(p + "ax" + i)

        def rs_third(p, R):
            for i, r in ((1, 0), (2, 1)):
                recv(f"{p}cp{i}")
                plus(nd(0, 1), K[r].start, half // 2, R, 1)
                start(f"{p}ap{i}")
                recv(f"{p}cm{i}")
                plus(nd(0, -1), K[r + 2].start, half // 2, R, 1)
                start(f"{p}am{i}")

        def rs_end(p, i):
            if i == 1:
                recv(p + "ax1", p + "ax2", p + "ap3", p + "am3")
            recv(f"{p}ap{i}", f"{p}am{i}")

        def wait_column(b, share):
            for d in range(4):
                share(b * 4 + d, True).wait_recv()

        forward("2", H2)
        ring_relay("D", 1)
        forward("1", H1)
        products("P", hid, Wd, 3, 4)
        ring_share("D", 1, xl, share_d)
        ring_end("D", 1, xl, share_d)
        wait_column(xl, share_d)
        products("P", hid, Wd, 4, 5)
        rs_first("P", RB, "2")
        products("P", hid, Wd, 5, 8)
        rs_first("P", RB, "1")
        rs_second("P", RB, "21")
        rs_third("P", RB)
        rs_end("P", 1)
        lt.wait()
        la.wait()

        def total(R, q):
            v = SB[nd(0, 0), q, :].astype(F32) + R[4, q, :].astype(F32)
            return v + R[5, q, :].astype(F32) + R[6, q, :].astype(F32)

        bin_i = lax.broadcasted_iota(jnp.int32, (ng, nb), 1)
        grp_i = lax.broadcasted_iota(jnp.int32, (ng, nb), 0)
        weight = []
        for s in range(micro):
            chosen = jnp.where((bin_i == bins[s]) & (grp_i == grps[s]), adv[...], 0.0)
            weight.append(jnp.sum(jnp.sum(chosen, axis=1, keepdims=True), axis=0, keepdims=True))

        def error(k):
            begin, end = K[k].start, K[k].start + K[k].size
            for s in range(micro):
                lo, hi = max(begin, s * seq), min(end, (s + 1) * seq)

                def body(r, s=s, lo=lo):
                    q = pl.ds(pl.multiple_of(r.start + lo, 32), r.size)
                    d = weight[s] * (tok[q, :].astype(F32) + total(RB, q) - tgt[q, :].astype(F32))
                    dpred[q, :] = d
                    Y[nd(0, 0), q, :] = d.astype(BF16)

                if lo < hi:
                    tiles(hi - lo, 32, body)

        error(0)
        error(2)
        start("Yyp1", "Yym1")
        rs_end("P", 2)
        error(1)
        error(3)
        start("Yyp2", "Yym2", "Yx1", "Yx2", "Yyp3", "Yym3")
        sent(*["P" + n for n in RSN])

        def stage_down(m):
            SGD[m] = (dot_tn(Y[m], hid[...]) * scale).astype(BF16)
            sib_d(m).start()

        def stage_up(m):
            SGU[m] = (dot_tn(X[m], dpre[...]) * scale).astype(BF16)
            sib_u(m).start()

        def wide_plus(S, blk, slots, r0, size):
            def body(r):
                a = pl.ds(pl.multiple_of(r.start + r0, 32), r.size)
                q = pl.ds(pl.multiple_of(mine + r.start + r0, 32), r.size)
                v = S[blk, q, :].astype(F32)
                for ref, slot in slots:
                    v = v + ref[slot, a, :].astype(F32)
                S[blk, q, :] = v.astype(BF16)

            tiles(size, 32, body)

        quarter = part // 2

        def wide_first(p, i, b, S, B, share):
            m = b * 4 + (z + 2) % 4
            share(m).wait_recv()
            wide_plus(S, m, ((B, m),), 0, part)
            start(f"{p}cp{i}", f"{p}cm{i}")

        def wide_early(p, i, b, S, B, share):
            up, down = b * 4 + (z + 1) % 4, b * 4 + (z + 3) % 4
            share(up).wait_recv()
            wide_plus(S, up, ((B, up),), quarter, quarter)
            start(f"{p}ap{i}b")
            share(down).wait_recv()
            wide_plus(S, down, ((B, down),), 0, quarter)
            start(f"{p}am{i}a")

        def wide_second(p, i, b, S, B, R, share):
            up, down = b * 4 + (z + 1) % 4, b * 4 + (z + 3) % 4
            recv(f"{p}cp{i}")
            wide_plus(S, up, ((B, up), (R, i)), 0, quarter)
            start(f"{p}ap{i}a")
            recv(f"{p}cm{i}")
            wide_plus(S, down, ((B, down), (R, i)), quarter, quarter)
            start(f"{p}am{i}b")
            share(b * 4 + z).wait_recv()

        def wide_step(p, i, b, S, B, R, share):
            up, down = b * 4 + (z + 1) % 4, b * 4 + (z + 3) % 4
            recv(f"{p}cp{i}", f"{p}cm{i}")
            share(up).wait_recv()
            wide_plus(S, up, ((B, up), (R, i)), 0, quarter)
            start(f"{p}ap{i}a")
            share(down).wait_recv()
            wide_plus(S, down, ((B, down),), 0, quarter)
            start(f"{p}am{i}a")
            wide_plus(S, up, ((B, up),), quarter, quarter)
            start(f"{p}ap{i}b")
            wide_plus(S, down, ((B, down), (R, i)), quarter, quarter)
            start(f"{p}am{i}b")
            share(b * 4 + z).wait_recv()

        def wide_third(p, i, b, S, B, R):
            m = b * 4 + z
            for h, r0 in (("a", 0), ("b", quarter)):
                recv(f"{p}ap{i}{h}", f"{p}am{i}{h}")

                @pl.when(xh != b)
                def _(h=h, r0=r0):
                    wide_plus(S, m, ((B, m), (R, 2 + 2 * i), (R, 3 + 2 * i)), r0, quarter)
                    start(p + "x" + h)

        def wide_last(p, b0, S, B, R, out):
            recv(p + "xa", p + "xb")
            m = wm(0, 0)
            slot = jnp.where(xh == b0, 2, 4)

            def body(r):
                q = pl.ds(pl.multiple_of(mine + r.start, 32), r.size)
                v = S[m, q, :].astype(F32) + B[m, r, :].astype(F32)
                v = v + R[slot, r, :].astype(F32) + R[slot + 1, r, :].astype(F32)
                out[r, :] = (v + R[6, r, :].astype(F32)).astype(BF16)

            tiles(part, 32, body)

        G0 = ("G", 0, xl, SGD, SIBD)
        G1 = ("G", 1, 1 - xl, SGD, SIBD)
        U0 = ("H", 0, xl, SGU, SIBU)
        U1 = ("H", 1, 1 - xl, SGU, SIBU)

        @pl.loop(0, 5)
        def _(k):
            @pl.when(k == 1)
            def _():
                far_relay("Y")
                recv("Yx1")
                start("Ybp1", "Ybm1")
                recv("Yx2")
                start("Ybp2", "Ybm2")
                recv("Yyp3", "Yym3")

            @pl.when(k == 4)
            def _():
                for d in ("p1", "p2", "m1", "m2"):
                    recv("Yc" + d)
                    start("Yd" + d)

            n = arrival(k)

            @pl.when(k != 3)
            def _():
                stage_down(n)

            @pl.when(k != 4)
            def _():
                dh[...] += dot_nn(Y[n], Wd[n])

        wide_first(*G0, sib_d)
        wide_early(*G0, sib_d)
        last = arrival(4)
        dh[...] += dot_nn(Y[last], Wd[last])
        wide_second(*G0, RGD, sib_d)
        def backward(i, r):
            recv(*["Y" + n + i for n in ("bp", "bm")], *["Yd" + "pm"[int(i) - 1] + j for j in "12"])
            if i == "2":
                stage_down((1 - xl) * 4 + (z + 2) % 4)

            def more(first, last):
                @pl.loop(first, last)
                def _(k):
                    n = arrival(k)
                    dh[r] += dot_nn(Y[n, r], Wd[n])

            more(5, 7)
            if i == "2":
                wide_first(*G1, sib_d)
            more(7, 8)

            def slope(t):
                q = pl.ds(pl.multiple_of(t.start + r.start, 32), t.size)
                dpre[q, :] = (dh[q, :] * gelu_slope(pre[q, :])).astype(BF16)

            tiles(r.size, 32, slope)
            if i == "2":

                @pl.loop(0, 2)
                def _(k):
                    stage_up(((xl + k) % 2) * 4 + (z + 2) % 4)

            products("M", dpre, Wu, 0, 2, r)
            if i == "2":
                wide_first(*U0, sib_u)
                wide_first(*U1, sib_u)
            products("M", dpre, Wu, 2, 3, r)

        backward("1", H1)
        sent(*["D" + n for n in WAG])

        @pl.loop(0, 8)
        def _(b):
            share_d(b).wait_send()

        backward("2", H2)
        wide_third("G", 0, xl, SGD, SIBD, RGD)
        products("M", dpre, Wu, 3, 5)
        rs_second("M", RB, "1")

        @pl.loop(0, 3)
        def _(k):
            stage_down((1 - xl) * 4 + (z + 3 + k) % 4)

        rs_first("M", RB, "12")
        wide_early(*G1, sib_d)
        wide_second(*G1, RGD, sib_d)

        @pl.loop(0, 3)
        def _(k):
            stage_up(xl * 4 + (z + 3 + k) % 4)

        rs_second("M", RB, "2")
        products("M", dpre, Wu, 5, 8)
        wide_early(*U0, sib_u)
        wide_second(*U0, RGU, sib_u)

        @pl.loop(0, 3)
        def _(k):
            stage_up((1 - xl) * 4 + (z + 3 + k) % 4)

        rs_third("M", RB)
        wide_step(*U1, RGU, sib_u)
        wide_third("G", 1, 1 - xl, SGD, SIBD, RGD)
        wide_third("H", 0, xl, SGU, SIBU, RGU)
        wide_third("H", 1, 1 - xl, SGU, SIBU, RGU)
        rs_end("M", 1)
        rs_end("M", 2)
        for s in range(micro):

            def finish(r, s=s):
                q = pl.ds(pl.multiple_of(r.start + s * seq, 32), r.size)
                gt[q, :] = (dpred[q, :] + gain[s : s + 1, :] * total(RB, q)).astype(BF16)

            tiles(seq, 32, finish)
        back(gt, gt_out, 1).start()
        wide_last("G", xl, SGD, SIBD, RGD, gd)
        back(gd, gd_out, 0).start()
        wide_last("H", xl, SGU, SIBU, RGU, gu)
        back(gu, gu_out, 2).start()

        sent(*ag_names("X", True), *ag_names("Y", False), *["U" + n for n in WAG], *["M" + n for n in RSN])
        sent(*["G" + n for n in RSW], *["H" + n for n in RSW])

        @pl.loop(0, 8)
        def _(b):
            share_u(b).wait_send()
            sib_d(b).wait_send()
            sib_u(b).wait_send()

        back(gd, gd_out, 0).wait()
        back(gt, gt_out, 1).wait()
        back(gu, gu_out, 2).wait()

    return kernel


TRANSFERS = 176


def widen(*arrays):
    pieces = 2

    def kernel(*refs):
        n = len(arrays)
        src, dst, inner, outer, sems = refs[:n], refs[n : 2 * n], refs[2 * n : 3 * n], refs[3 * n : 4 * n], refs[4 * n]

        def copies(i, j):
            size = arrays[i].shape[0] // pieces
            r = pl.ds(j * size, size)
            return (
                pltpu.make_async_copy(src[i].at[r], inner[i].at[r], sems.at[0, i, j]),
                pltpu.make_async_copy(outer[i].at[r], dst[i].at[r], sems.at[1, i, j]),
                r,
            )

        every = [copies(i, j) for i in range(n) for j in range(pieces)]
        for read, _, _ in every:
            read.start()
        for k, (read, write, r) in enumerate(every):
            i = k // pieces
            read.wait()

            def body(t, i=i, r=r):
                q = pl.ds(pl.multiple_of(t.start + r.start, 32), t.size)
                outer[i][q, :] = inner[i][q, :].astype(F32)

            tiles(r.size, 32, body)
            write.start()
        for _, write, _ in every:
            write.wait()

    anys = pl.BlockSpec(memory_space=pl.ANY)
    return pl.pallas_call(
        kernel,
        out_shape=tuple(jax.ShapeDtypeStruct(a.shape, F32) for a in arrays),
        in_specs=[anys] * len(arrays),
        out_specs=(anys,) * len(arrays),
        scratch_shapes=[pltpu.VMEM(a.shape, BF16) for a in arrays]
        + [pltpu.VMEM(a.shape, F32) for a in arrays]
        + [pltpu.SemaphoreType.DMA((2, len(arrays), pieces))],
        compiler_params=pltpu.CompilerParams(vmem_limit_bytes=63 * 2**20),
        cost_estimate=pl.CostEstimate(flops=0, bytes_accessed=6 * sum(a.size for a in arrays), transcendentals=0),
        name="widen",
    )(*arrays)


def on_device(tokens, target, mod_table, adv_table, w_up, w_down_t, bins, groups):
    rows, feat = tokens.shape
    part, hidden = w_up.shape
    depth = part * 16
    micro = bins.shape[0]
    scale = float(16 * rows) ** (-0.5)
    anys = pl.BlockSpec(memory_space=pl.ANY)
    block = (8, rows, feat)
    wblock = (8, depth // 8, hidden)
    V = pltpu.VMEM
    flops = 6 * 2 * rows * depth * hidden
    grads = pl.pallas_call(
        make_kernel(rows, feat, depth, hidden, micro, scale),
        out_shape=(
            jax.ShapeDtypeStruct((rows, feat), BF16),
            jax.ShapeDtypeStruct((part, hidden), BF16),
            jax.ShapeDtypeStruct((part, hidden), BF16),
        ),
        in_specs=[anys] * 8,
        out_specs=(anys, anys, anys),
        scratch_shapes=[
            V(block, BF16), V(block, BF16), V(wblock, BF16), V(wblock, BF16),
            V((rows, hidden), F32), V((rows, hidden), F32), V((rows, hidden), BF16), V((rows, hidden), BF16),
            V(block, BF16), V((7, rows, feat), BF16),
            V(wblock, BF16), V((8, part, hidden), BF16), V((8, part, hidden), BF16),
            V((7, part, hidden), BF16), V((7, part, hidden), BF16),
            V((8, feat), F32),
            pltpu.SMEM(bins.shape, jnp.int32), pltpu.SMEM(groups.shape, jnp.int32),
            V((rows, feat), BF16), V(mod_table.shape, BF16), V(adv_table.shape[::-1], F32),
            V((rows, feat), BF16), V((rows, feat), F32), V((rows, feat), BF16), V((part, hidden), BF16), V((part, hidden), BF16),
            pltpu.SemaphoreType.DMA((TRANSFERS,)),
            pltpu.SemaphoreType.DMA((TRANSFERS,)),
            pltpu.SemaphoreType.DMA((11,)),
        ],
        compiler_params=pltpu.CompilerParams(
            collective_id=0, has_side_effects=True, vmem_limit_bytes=63 * 2**20
        ),
        cost_estimate=pl.CostEstimate(flops=flops, bytes_accessed=8 * 2**20, transcendentals=2 * rows * hidden),
        name="block_gradient",
    )(tokens, target, mod_table, adv_table.T, bins, groups, w_up, w_down_t)
    return widen(*grads)


def solution(mesh):
    return jax.shard_map(
        on_device,
        mesh=mesh,
        in_specs=(
            P("wide", "node"),
            P("wide", "node"),
            P(None, "node"),
            P(),
            P("wide", "node"),
            P("wide", "node"),
            P("wide"),
            P("wide"),
        ),
        out_specs=(P("wide", "node"), P("wide", "node"), P("wide", "node")),
        check_vma=False,
    )
```

```python
import jax
import jax.numpy as jnp
from jax import lax
from jax.experimental import pallas as pl
from jax.experimental.pallas import tpu as pltpu
from jax.sharding import PartitionSpec as P

F32 = jnp.float32
BF16 = jnp.bfloat16
MESH = pl.DeviceIdType.MESH
COEF = 0.7978845608028654


def dot_nn(a, b):
    return jnp.dot(a, b, preferred_element_type=F32)


def dot_nt(a, b):
    return lax.dot_general(a, b, (((1,), (1,)), ((), ())), preferred_element_type=F32)


def dot_tn(a, b):
    return lax.dot_general(a, b, (((0,), (0,)), ((), ())), preferred_element_type=F32)


def gelu_slope(v):
    th = jnp.tanh(COEF * (v + 0.044715 * v * v * v))
    return 0.5 * (1.0 + th) + 0.5 * v * (1.0 - th * th) * COEF * (1.0 + 3 * 0.044715 * v * v)


def tiles(rows, size, body):
    @pl.loop(0, rows // size)
    def _(t):
        body(pl.ds(pl.multiple_of(t * size, size), size))


def make_kernel(rows, feat, depth, hidden, micro, scale):
    seq = rows // micro

    def kernel(
        tok_in, tgt_in, mod_in, adv_in, bins_in, grps_in, wu_in, wd_in,
        gt_out, gu_out, gd_out,
        X, Y, Wu, Wd, pre, dh, hid, dpre, SB, RB, SGD, SIBD, SIBU, RGD, RGU, gain,
        bins, grps, tok, mod, adv, tgt, dpred, gt, gu, gd, ss, rs, cs, ls,
    ):
        SGU = Wd
        wi, ni = lax.axis_index("wide"), lax.axis_index("node")
        xh, z, c = wi // 8, (wi // 2) % 4, wi % 2
        xl, y = ni // 4, ni % 4

        def nd(dx, dy):
            return ((xl + dx) % 2) * 4 + (y + dy + 4) % 4

        def wm(dx, dz):
            return ((xh + dx) % 2) * 4 + (z + dz + 4) % 4

        def dnode(dx, dy):
            return (wi, nd(dx, dy))

        def dwide(dx, dz):
            return (wm(dx, dz) * 2 + c, ni)

        sib = (wm(0, 0) * 2 + 1 - c, ni)

        table = {}
        slots = {}

        def slot(key):
            return slots.setdefault(key, len(slots))

        def add(name, src, dst, got, dev):
            table[name] = (src, dst, got, dev)

        def start(*names):
            for name in names:
                src, dst, _, dev = table[name]
                pltpu.make_async_remote_copy(
                    src_ref=src,
                    dst_ref=dst,
                    send_sem=ss.at[SENDS.index(name[0])],
                    recv_sem=rs.at[slot(together(name))],
                    device_id=dev,
                    device_id_type=MESH,
                ).start()

        def bytes_of(ref, send, receive):
            return pltpu.make_async_remote_copy(
                src_ref=ref, dst_ref=ref, send_sem=ss.at[send], recv_sem=rs.at[receive], device_id=sib, device_id_type=MESH
            )

        def recv(*names):
            groups = {}
            for name in names:
                groups.setdefault(together(name), []).append(name)
            for key, members in groups.items():
                assert len(members) == sum(together(name) == key for name in table), key
                got = table[members[0]][2]
                if len(members) > 1:
                    n = sum(table[name][2].shape[0] for name in members)
                    if members[0][0] in "UDGH":
                        got = RGD.at[0]
                        assert n == part
                    elif n <= rows:
                        got = RB.at[0, pl.ds(0, n)]
                    else:
                        got = RB.at[pl.ds(0, n // half), H1]
                bytes_of(got, 0, slot(key)).wait_recv()

        def sent(*prefixes):
            for p in prefixes:
                bytes_of(RGD if p in "UDGH" else RB, SENDS.index(p), 0).wait_send()

        def shared(*prefixes):
            for p in prefixes:
                bytes_of(SIBD, SENDS.index(p.lower()), 0).wait_send()

        part = depth // 16
        mine, other = pl.multiple_of(c * part, part), pl.multiple_of((1 - c) * part, part)
        PC, PS = pl.ds(mine, part), pl.ds(other, part)
        Q1 = pl.ds(mine, part // 2)
        Q2 = pl.ds(pl.multiple_of(mine + part // 2, part // 2), part // 2)
        W = pl.ds(0, rows)
        half = rows // 2
        H1, H2 = pl.ds(0, half), pl.ds(half, half)
        K = [pl.ds(i * (half // 2), half // 2) for i in range(4)]
        eighth = half // 4
        T1, T2 = pl.ds(half - eighth, eighth), pl.ds(rows - eighth, eighth)
        L1, L2 = pl.ds(0, half - eighth), pl.ds(half, half - eighth)

        def add_ag(p, B, fewer):
            def one(name, blk, r, got, dev):
                add(p + name, B.at[blk, r], B.at[blk, r], B.at[got, r], dev)

            for i, rp, rm in (("1", K[0], K[2]), ("2", K[1], K[3]), ("3", H2, H1)):
                one("yp" + i, nd(0, 0), rp, nd(0, -1), dnode(0, 1))
                one("ym" + i, nd(0, 0), rm, nd(0, 1), dnode(0, -1))
            for i, r in (("1", H1), ("2", H2)):
                one("x" + i, nd(0, 0), r, nd(1, 0), dnode(1, 0))
                b = L2 if i == "2" and not fewer else r
                one("bp" + i, nd(1, 0), b, nd(1, -1), dnode(0, 1))
                one("bm" + i, nd(1, 0), b, nd(1, 1), dnode(0, -1))
            if not fewer:
                one("tp", nd(0, -1), T2, nd(1, -1), dnode(1, 0))
                one("tm", nd(0, 1), T2, nd(1, 1), dnode(1, 0))
            for i, rp, rm in (("1", K[0], K[2]), ("2", K[1], K[3])):
                one("cp" + i, nd(0, -1), rp, nd(0, 2), dnode(0, 1))
                one("cm" + i, nd(0, 1), rm, nd(0, 2), dnode(0, -1))
                one("dp" + i, nd(0, 2), rp, nd(1, 2), dnode(1, 0))
                if not fewer:
                    one("dm" + i, nd(0, 2), rm, nd(1, 2), dnode(1, 0))
            if fewer:
                one("ep", nd(1, -1), K[2], nd(1, 2), dnode(0, 1))
                one("em", nd(1, 1), K[3], nd(1, 2), dnode(0, -1))

        def add_wag(p, B, b0):
            def one(name, blk, r, got, dev):
                add(p + name, B.at[blk, r], B.at[blk, r], B.at[got, r], dev)

            one("x", wm(0, 0), PC, wm(1, 0), dwide(1, 0))
            for i, b in ((0, b0), (1, 1 - b0)):
                here, up, down, far = (b * 4 + (z + d) % 4 for d in (0, 1, 3, 2))
                one(f"zp{i}", here, Q1, down, dwide(0, 1))
                one(f"zm{i}", here, Q2, up, dwide(0, -1))
                one(f"yp{i}", here, Q2, down, dwide(0, 1))
                one(f"ym{i}", here, Q1, up, dwide(0, -1))
                one(f"cp{i}", down, Q1, far, dwide(0, 1))
                one(f"cm{i}", up, Q2, far, dwide(0, -1))
            def share(b):
                column = jnp.where(b // 4 == b0, 0, 1)
                return pltpu.make_async_remote_copy(
                    src_ref=B.at[b, PC],
                    dst_ref=B.at[b, PC],
                    send_sem=ss.at[SENDS.index(p.lower())],
                    recv_sem=cs.at[(0 if p == "U" else 2) + column],
                    device_id=sib,
                    device_id_type=MESH,
                )

            def column_shared(i):
                ref = SIBD.at[pl.ds(0, 4)]
                pltpu.make_async_remote_copy(
                    src_ref=ref,
                    dst_ref=ref,
                    send_sem=ss.at[0],
                    recv_sem=cs.at[(0 if p == "U" else 2) + i],
                    device_id=sib,
                    device_id_type=MESH,
                ).wait_recv()

            return share, column_shared

        def add_rs(p, R):
            def one(name, blk, r, slot, dev):
                add(p + name, SB.at[blk, r], R.at[slot, r], R.at[slot, r], dev)

            for i, r in (("1", H1), ("2", H2)):
                one("x" + i, nd(1, 2), r, 0, dnode(1, 0))
                one("bp" + i, nd(1, 1), L1 if i == "1" and p == "P" else r, 2, dnode(0, 1))
                one("bm" + i, nd(1, -1), L2 if i == "2" and p == "P" else r, 3, dnode(0, -1))
            if p == "P":
                one("tp", nd(1, 1), T1, 2, dnode(1, 0))
                one("tm", nd(1, -1), T2, 3, dnode(1, 0))
            one("ax1", nd(1, 0), H1, 4, dnode(1, 0))
            one("ax2", nd(1, 0), H2, 4, dnode(1, 0))
            for i, rp, rm in (("1", K[0], K[2]), ("2", K[1], K[3])):
                one("cp" + i, nd(0, 2), rp, 1, dnode(0, 1))
                one("cm" + i, nd(0, 2), rm, 1, dnode(0, -1))
            for i, rp, rm in (("1", K[0], K[2]), ("2", K[1], K[3]), ("3", H2, H1)):
                one("ap" + i, nd(0, 1), rp, 5, dnode(0, 1))
                one("am" + i, nd(0, -1), rm, 6, dnode(0, -1))

        A1, A2 = pl.ds(0, part // 2), pl.ds(part // 2, part // 2)
        AW = pl.ds(0, part)

        def add_wrs(p, S, R, B, b0):
            def one(name, blk, r, slot, rr, dev):
                add(p + name, S.at[blk, r], R.at[slot, rr], R.at[slot, rr], dev)

            one("xa", wm(1, 0), Q1, 6, A1, dwide(1, 0))
            one("xb", wm(1, 0), Q2, 6, A2, dwide(1, 0))
            for i, b in ((0, b0), (1, 1 - b0)):
                up, down, far = (b * 4 + (z + d) % 4 for d in (1, 3, 2))
                one(f"cp{i}", far, Q1, i, A1, dwide(0, 1))
                one(f"cm{i}", far, Q2, i, A2, dwide(0, -1))
                for h, r, a in (("a", Q1, A1), ("b", Q2, A2)):
                    one(f"ap{i}{h}", up, r, 2 + 2 * i, a, dwide(0, 1))
                    one(f"am{i}{h}", down, r, 3 + 2 * i, a, dwide(0, -1))
            base = 4 if p == "G" else 12

            def share(b):
                return pltpu.make_async_remote_copy(
                    src_ref=S.at[b, PS],
                    dst_ref=B.at[b],
                    send_sem=ss.at[SENDS.index(p.lower())],
                    recv_sem=cs.at[base + b],
                    device_id=sib,
                    device_id_type=MESH,
                )

            return share

        add_ag("X", X, True)
        add_ag("Y", Y, False)
        share_u, column_u = add_wag("U", Wu, xh)
        share_d, column_d = add_wag("D", Wd, 1 - xl)
        add_rs("P", RB)
        add_rs("M", RB)
        sib_d = add_wrs("G", SGD, RGD, SIBD, xl)
        sib_u = add_wrs("H", SGU, RGU, SIBU, xl)

        barrier = pltpu.get_barrier_semaphore()
        for dev in (dnode(1, 0), dnode(0, 1), dnode(0, -1), dwide(1, 0), dwide(0, 1), dwide(0, -1), sib):
            pl.semaphore_signal(barrier, inc=1, device_id=dev, device_id_type=MESH)
        lu = pltpu.make_async_copy(wu_in, Wu.at[wm(0, 0), PC], ls.at[0])
        ld = pltpu.make_async_copy(wd_in, Wd.at[wm(0, 0), PC], ls.at[1])
        lt = pltpu.make_async_copy(tgt_in, tgt, ls.at[2])
        lk = pltpu.make_async_copy(tok_in, tok, ls.at[6])
        lm = pltpu.make_async_copy(mod_in, mod, ls.at[7])
        la = pltpu.make_async_copy(adv_in, adv, ls.at[8])
        lb = pltpu.make_async_copy(bins_in, bins, ls.at[9])
        lg = pltpu.make_async_copy(grps_in, grps, ls.at[10])
        lb.start()
        lg.start()
        lm.start()
        lk.start()
        la.start()
        lu.start()
        ld.start()
        lt.start()

        def back(src, dst, i):
            return pltpu.make_async_copy(src, dst, ls.at[3 + i])

        ng, nb = adv.shape
        lb.wait()
        lg.wait()
        lm.wait()
        lk.wait()
        row_i = lax.broadcasted_iota(jnp.int32, (nb, feat), 0)
        for s in range(micro):
            picked = jnp.sum(jnp.where(row_i == bins[s], mod[...].astype(F32), 0.0), axis=0, keepdims=True)
            gain[s : s + 1, :] = 1.0 + picked

            def modulate(r, s=s):
                q = pl.ds(pl.multiple_of(r.start + s * seq, 32), r.size)
                X[nd(0, 0), q, :] = (tok[q, :].astype(F32) * gain[s : s + 1, :]).astype(BF16)

            tiles(seq, 32, modulate)
        lu.wait()
        ld.wait()
        pl.semaphore_wait(barrier, 7)

        def ring_start(p, i):
            start(f"{p}zp{i}", f"{p}zm{i}", f"{p}yp{i}", f"{p}ym{i}")

        def ring_relay(p, i):
            recv(f"{p}zp{i}")
            start(f"{p}cp{i}")
            recv(f"{p}zm{i}")
            start(f"{p}cm{i}")

        def ring_share(p, i, b, share):
            recv(f"{p}yp{i}")
            share(b * 4 + (z + 3) % 4).start()
            recv(f"{p}ym{i}")
            share(b * 4 + (z + 1) % 4).start()

        def ring_end(p, i, b, share):
            recv(f"{p}cp{i}", f"{p}cm{i}")
            share(b * 4 + (z + 2) % 4).start()

        same = xh == xl
        start("Xyp1", "Xym1", "Xyp2", "Xym2", "Ux")
        ring_start("U", 0)
        start("Xyp3", "Xym3")
        share_u(wm(0, 0)).start()
        share_d(wm(0, 0)).start()

        @pl.when(~same)
        def _():
            start("Dx")

        start("Xx2")

        @pl.when(same)
        def _():
            start("Dx")

        start("Xx1")

        def zero(r):
            pre[r, :] = jnp.zeros((r.size, hidden), F32)
            dh[r, :] = jnp.zeros((r.size, hidden), F32)

        tiles(rows, 32, zero)
        ring_relay("U", 0)
        def far_relay(p):
            for d in ("p1", "m1", "p2", "m2"):
                recv(p + "y" + d)
                start(p + "c" + d)

        far_relay("X")
        recv("Ux")
        ring_start("U", 1)
        share_u(wm(1, 0)).start()
        ring_share("U", 0, xh, share_u)
        ring_end("U", 0, xh, share_u)
        ring_relay("U", 1)

        @pl.when(same)
        def _():
            recv("Dx")
            share_d(wm(1, 0)).start()

        ring_start("D", 0)
        recv("Xx2")
        start("Xbp2", "Xbm2")
        recv("Xcp1", "Xcp2")
        start("Xdp1", "Xdp2")
        recv("Xcm1", "Xcm2")
        ring_share("U", 1, 1 - xh, share_u)
        ring_end("U", 1, 1 - xh, share_u)
        recv("Xyp3", "Xym3")

        column_u(0)
        column_u(1)

        def arrival(k):
            dx = jnp.where((k == 3) | (k >= 5), 1, 0)
            dy = jnp.where((k == 1) | (k == 5), 1, jnp.where((k == 2) | (k == 6), 3, jnp.where((k == 4) | (k == 7), 2, 0)))
            return ((xl + dx) % 2) * 4 + (y + dy) % 4

        @pl.loop(0, 5)
        def _(k):
            @pl.when(k == 1)
            def _():
                recv("Xbp2")
                start("Xep")
                recv("Xbm2")
                start("Xem")
                recv("Xx1")
                start("Xbp1", "Xbm1")

            @pl.when(k == 2)
            def _():
                ring_relay("D", 0)

            n = arrival(k)
            pre[...] += dot_nn(X[n], Wu[n])

        ring_share("D", 0, 1 - xl, share_d)

        @pl.when(~same)
        def _():
            recv("Dx")
            share_d(wm(1, 0)).start()

        ring_start("D", 1)

        def forward(i, r):
            if i == "1":
                recv("Xbp1", "Xbm1", "Xdp1", "Xdp2")
            else:
                recv("Xep", "Xem")

            @pl.loop(5, 8)
            def _(k):
                n = arrival(k)
                pre[r] += dot_nn(X[n, r], Wu[n])

            def activate(t):
                q = pl.ds(pl.multiple_of(t.start + r.start, 32), t.size)
                hid[q, :] = jax.nn.gelu(pre[q, :], approximate=True).astype(BF16)

            if i == "2":
                ring_end("D", 0, 1 - xl, share_d)
            tiles(r.size, 32, activate)
            if i == "2":
                column_d(0)
            products("P", hid, Wd, 0, 3, r)

        def departure(k):
            dx = jnp.where(k <= 3, 1, 0)
            dy = jnp.where((k == 0) | (k == 4), 2, jnp.where((k == 1) | (k == 5), 1, jnp.where((k == 2) | (k == 6), 3, 0)))
            return ((xl + dx) % 2) * 4 + (y + dy) % 4

        def products(p, left, weight, first, last, r=W):
            @pl.loop(first, last)
            def _(k):
                n = departure(k)
                SB[n, r] = dot_nt(left[r], weight[n]).astype(BF16)
                for at, name in ((0, "x"), (1, "bp"), (2, "bm")):
                    if first <= at < last:

                        @pl.when(k == at)
                        def _(name=name):
                            if r.start == 0:
                                start(p + name + "1")
                                if p == "P" and name != "x":
                                    start(p + "t" + name[1])
                            if r.start + r.size == rows:
                                start(p + name + "2")

                for at, name in ((5, "ap3"), (6, "am3")):
                    if first <= at < last:

                        @pl.when(k == at)
                        def _(name=name):
                            start(p + name)

        def plus(blk, r0, size, R, *slots):
            def body(r):
                q = pl.ds(pl.multiple_of(r.start + r0, 32), r.size)
                v = SB[blk, q, :].astype(F32)
                for slot in slots:
                    v = v + R[slot, q, :].astype(F32)
                SB[blk, q, :] = v.astype(BF16)

            tiles(size, 32, body)

        def rs_first(p, R, order):
            for i in order:
                recv(p + "x" + i)
                plus(nd(0, 2), half * (int(i) - 1), half, R, 0)
                d = "cp" if i == "1" else "cm"
                start(p + d + "1", p + d + "2")

        def rs_second(p, R, order):
            for i in order:
                recv(p + "bp" + i, p + "bm" + i)
                if p == "P":
                    low, last = (L1, T1) if i == "1" else (L2, T2)
                    plus(nd(1, 0), low.start, low.size, R, 2, 3)
                    plus(nd(1, 0), last.start, last.size, R, 3 if i == "1" else 2)
                else:
                    plus(nd(1, 0), half * (int(i) - 1), half, R, 2, 3)
                start(p + "ax" + i)

        def rs_third(p, R):
            for i, r in ((1, 0), (2, 1)):
                recv(f"{p}cp{i}")
                plus(nd(0, 1), K[r].start, half // 2, R, 1)
                if p == "P" and i == 2:
                    recv("Ptp")
                    plus(nd(0, 1), T1.start, eighth, R, 2)
                start(f"{p}ap{i}")
                recv(f"{p}cm{i}")
                plus(nd(0, -1), K[r + 2].start, half // 2, R, 1)
                if p == "P" and i == 2:
                    recv("Ptm")
                    plus(nd(0, -1), T2.start, eighth, R, 3)
                start(f"{p}am{i}")

        def rs_end(p, i):
            if i == 1:
                recv(p + "ax1", p + "ax2", p + "ap3", p + "am3")
            recv(f"{p}ap{i}", f"{p}am{i}")

        forward("2", H2)
        ring_relay("D", 1)
        forward("1", H1)
        products("P", hid, Wd, 3, 4)
        ring_share("D", 1, xl, share_d)
        ring_end("D", 1, xl, share_d)
        column_d(1)
        products("P", hid, Wd, 4, 5)
        rs_first("P", RB, "2")
        products("P", hid, Wd, 5, 8)
        rs_first("P", RB, "1")
        rs_second("P", RB, "21")
        rs_third("P", RB)
        rs_end("P", 1)
        lt.wait()
        la.wait()

        def total(R, q):
            v = SB[nd(0, 0), q, :].astype(F32) + R[4, q, :].astype(F32)
            return v + R[5, q, :].astype(F32) + R[6, q, :].astype(F32)

        bin_i = lax.broadcasted_iota(jnp.int32, (ng, nb), 1)
        grp_i = lax.broadcasted_iota(jnp.int32, (ng, nb), 0)
        weight = []
        for s in range(micro):
            chosen = jnp.where((bin_i == bins[s]) & (grp_i == grps[s]), adv[...], 0.0)
            weight.append(jnp.sum(jnp.sum(chosen, axis=1, keepdims=True), axis=0, keepdims=True))

        def error(k):
            begin, end = K[k].start, K[k].start + K[k].size
            for s in range(micro):
                lo, hi = max(begin, s * seq), min(end, (s + 1) * seq)

                def body(r, s=s, lo=lo):
                    q = pl.ds(pl.multiple_of(r.start + lo, 32), r.size)
                    d = weight[s] * (tok[q, :].astype(F32) + total(RB, q) - tgt[q, :].astype(F32))
                    dpred[q, :] = d
                    Y[nd(0, 0), q, :] = d.astype(BF16)

                if lo < hi:
                    tiles(hi - lo, 32, body)

        error(0)
        error(2)
        start("Yyp1", "Yym1")
        rs_end("P", 2)
        error(1)
        error(3)
        start("Yyp2", "Yym2", "Yx1", "Yx2", "Yyp3", "Yym3")
        sent("P")

        def stage_down(m):
            SGD[m] = (dot_tn(Y[m], hid[...]) * scale).astype(BF16)
            sib_d(m).start()

        def stage_up(m):
            SGU[m] = (dot_tn(X[m], dpre[...]) * scale).astype(BF16)
            sib_u(m).start()

        def wide_plus(S, blk, slots, r0, size):
            def body(r):
                a = pl.ds(pl.multiple_of(r.start + r0, 32), r.size)
                q = pl.ds(pl.multiple_of(mine + r.start + r0, 32), r.size)
                v = S[blk, q, :].astype(F32)
                for ref, slot in slots:
                    v = v + ref[slot, a, :].astype(F32)
                S[blk, q, :] = v.astype(BF16)

            tiles(size, 32, body)

        quarter = part // 2

        def wide_first(p, i, b, S, B, share):
            m = b * 4 + (z + 2) % 4
            share(m).wait_recv()
            wide_plus(S, m, ((B, m),), 0, part)
            start(f"{p}cp{i}", f"{p}cm{i}")

        def wide_early(p, i, b, S, B, share):
            up, down = b * 4 + (z + 1) % 4, b * 4 + (z + 3) % 4
            share(up).wait_recv()
            wide_plus(S, up, ((B, up),), quarter, quarter)
            start(f"{p}ap{i}b")
            share(down).wait_recv()
            wide_plus(S, down, ((B, down),), 0, quarter)
            start(f"{p}am{i}a")

        def wide_second(p, i, b, S, B, R, share):
            up, down = b * 4 + (z + 1) % 4, b * 4 + (z + 3) % 4
            recv(f"{p}cp{i}")
            wide_plus(S, up, ((B, up), (R, i)), 0, quarter)
            start(f"{p}ap{i}a")
            recv(f"{p}cm{i}")
            wide_plus(S, down, ((B, down), (R, i)), quarter, quarter)
            start(f"{p}am{i}b")
            share(b * 4 + z).wait_recv()

        def wide_step(p, i, b, S, B, R, share):
            up, down = b * 4 + (z + 1) % 4, b * 4 + (z + 3) % 4
            recv(f"{p}cp{i}", f"{p}cm{i}")
            share(up).wait_recv()
            wide_plus(S, up, ((B, up), (R, i)), 0, quarter)
            start(f"{p}ap{i}a")
            share(down).wait_recv()
            wide_plus(S, down, ((B, down),), 0, quarter)
            start(f"{p}am{i}a")
            wide_plus(S, up, ((B, up),), quarter, quarter)
            start(f"{p}ap{i}b")
            wide_plus(S, down, ((B, down), (R, i)), quarter, quarter)
            start(f"{p}am{i}b")
            share(b * 4 + z).wait_recv()

        def wide_third(p, i, b, S, B, R):
            m = b * 4 + z
            for h, r0 in (("a", 0), ("b", quarter)):
                recv(f"{p}ap{i}{h}", f"{p}am{i}{h}")

                @pl.when(xh != b)
                def _(h=h, r0=r0):
                    wide_plus(S, m, ((B, m), (R, 2 + 2 * i), (R, 3 + 2 * i)), r0, quarter)
                    start(p + "x" + h)

        def wide_last(p, b0, S, B, R, out):
            recv(p + "xa", p + "xb")
            m = wm(0, 0)
            slot = jnp.where(xh == b0, 2, 4)

            def body(r):
                q = pl.ds(pl.multiple_of(mine + r.start, 32), r.size)
                v = S[m, q, :].astype(F32) + B[m, r, :].astype(F32)
                v = v + R[slot, r, :].astype(F32) + R[slot + 1, r, :].astype(F32)
                out[r, :] = (v + R[6, r, :].astype(F32)).astype(BF16)

            tiles(part, 32, body)

        G0 = ("G", 0, xl, SGD, SIBD)
        G1 = ("G", 1, 1 - xl, SGD, SIBD)
        U0 = ("H", 0, xl, SGU, SIBU)
        U1 = ("H", 1, 1 - xl, SGU, SIBU)

        @pl.loop(0, 5)
        def _(k):
            @pl.when(k == 1)
            def _():
                far_relay("Y")
                recv("Yx1")
                start("Ybp1", "Ybm1")
                recv("Yx2")
                start("Ybp2", "Ybm2")
                recv("Yyp3", "Yym3")
                start("Ytp", "Ytm")

            @pl.when(k == 4)
            def _():
                for d in ("p1", "p2", "m1", "m2"):
                    recv("Yc" + d)
                    start("Yd" + d)

            n = arrival(k)

            @pl.when(k != 3)
            def _():
                stage_down(n)

            @pl.when(k != 4)
            def _():
                dh[...] += dot_nn(Y[n], Wd[n])

        wide_first(*G0, sib_d)
        wide_early(*G0, sib_d)
        last = arrival(4)
        dh[...] += dot_nn(Y[last], Wd[last])
        wide_second(*G0, RGD, sib_d)
        def backward(i, r):
            late = ["Ytp", "Ytm"] if i == "2" else []
            recv(*["Y" + n + i for n in ("bp", "bm")], *["Yd" + "pm"[int(i) - 1] + j for j in "12"], *late)
            if i == "2":
                stage_down((1 - xl) * 4 + (z + 2) % 4)

            def more(first, last):
                @pl.loop(first, last)
                def _(k):
                    n = arrival(k)
                    dh[r] += dot_nn(Y[n, r], Wd[n])

            more(5, 7)
            if i == "2":
                wide_first(*G1, sib_d)
            more(7, 8)

            def slope(t):
                q = pl.ds(pl.multiple_of(t.start + r.start, 32), t.size)
                dpre[q, :] = (dh[q, :] * gelu_slope(pre[q, :])).astype(BF16)

            tiles(r.size, 32, slope)
            if i == "2":

                @pl.loop(0, 2)
                def _(k):
                    stage_up(((xl + k) % 2) * 4 + (z + 2) % 4)

            products("M", dpre, Wu, 0, 2, r)
            if i == "2":
                wide_first(*U0, sib_u)
                wide_first(*U1, sib_u)
            products("M", dpre, Wu, 2, 3, r)

        backward("1", H1)
        sent("D")
        shared("D")

        backward("2", H2)
        wide_third("G", 0, xl, SGD, SIBD, RGD)
        products("M", dpre, Wu, 3, 5)
        rs_second("M", RB, "1")

        @pl.loop(0, 3)
        def _(k):
            stage_down((1 - xl) * 4 + (z + 3 + k) % 4)

        rs_first("M", RB, "12")
        wide_early(*G1, sib_d)
        wide_second(*G1, RGD, sib_d)

        @pl.loop(0, 3)
        def _(k):
            stage_up(xl * 4 + (z + 3 + k) % 4)

        rs_second("M", RB, "2")
        products("M", dpre, Wu, 5, 8)
        wide_early(*U0, sib_u)
        wide_second(*U0, RGU, sib_u)

        @pl.loop(0, 3)
        def _(k):
            stage_up((1 - xl) * 4 + (z + 3 + k) % 4)

        rs_third("M", RB)
        wide_step(*U1, RGU, sib_u)
        wide_third("G", 1, 1 - xl, SGD, SIBD, RGD)
        wide_third("H", 0, xl, SGU, SIBU, RGU)
        wide_third("H", 1, 1 - xl, SGU, SIBU, RGU)
        rs_end("M", 1)
        rs_end("M", 2)
        for s in range(micro):

            def finish(r, s=s):
                q = pl.ds(pl.multiple_of(r.start + s * seq, 32), r.size)
                gt[q, :] = (dpred[q, :] + gain[s : s + 1, :] * total(RB, q)).astype(BF16)

            tiles(seq, 32, finish)
        back(gt, gt_out, 1).start()
        wide_last("G", xl, SGD, SIBD, RGD, gd)
        back(gd, gd_out, 0).start()
        wide_last("H", xl, SGU, SIBU, RGU, gu)
        back(gu, gu_out, 2).start()

        sent("X", "Y", "U", "M", "G", "H")
        shared("U", "G", "H")
        assert len(slots) == RECEIVES, len(slots)
        back(gd, gd_out, 0).wait()
        back(gt, gt_out, 1).wait()
        back(gu, gu_out, 2).wait()

    return kernel


SENDS = "XYUDPMGHudgh"


def together(name):
    p, n = name[0], name[1:]
    if n in ("yp3", "ym3"):
        return p + "y3"
    if p in "XY" and n in ("bp1", "bm1", "dp1", "dp2"):
        return p + "n1"
    if (p == "Y" and n in ("bp2", "bm2", "dm1", "dm2", "tp", "tm")) or (p == "X" and n in ("ep", "em")):
        return p + "n2"
    if p == "X" and n in ("cm1", "cm2"):
        return "Xcm"
    if p in "PM":
        if n in ("ax1", "ax2", "ap3", "am3"):
            return p + "n"
        if n[:2] in ("bp", "bm"):
            return p + "b" + n[2]
    if p in "UD" and n[:2] in ("cp", "cm"):
        return p + "c" + n[2]
    if p in "GH":
        if n[0] == "x":
            return p + "x"
        if n[0] == "a":
            return p + "a" + n[2:]
    return name


RECEIVES = 95


def widen(*arrays):
    pieces = 2

    def kernel(*refs):
        n = len(arrays)
        src, dst, inner, outer, sems = refs[:n], refs[n : 2 * n], refs[2 * n : 3 * n], refs[3 * n : 4 * n], refs[4 * n]

        def copies(i, j):
            size = arrays[i].shape[0] // pieces
            r = pl.ds(j * size, size)
            return (
                pltpu.make_async_copy(src[i].at[r], inner[i].at[r], sems.at[0, i, j]),
                pltpu.make_async_copy(outer[i].at[r], dst[i].at[r], sems.at[1, i, j]),
                r,
            )

        every = [copies(i, j) for i in range(n) for j in range(pieces)]
        for read, _, _ in every:
            read.start()
        for k, (read, write, r) in enumerate(every):
            i = k // pieces
            read.wait()

            def body(t, i=i, r=r):
                q = pl.ds(pl.multiple_of(t.start + r.start, 32), t.size)
                outer[i][q, :] = inner[i][q, :].astype(F32)

            tiles(r.size, 32, body)
            write.start()
        for _, write, _ in every:
            write.wait()

    anys = pl.BlockSpec(memory_space=pl.ANY)
    return pl.pallas_call(
        kernel,
        out_shape=tuple(jax.ShapeDtypeStruct(a.shape, F32) for a in arrays),
        in_specs=[anys] * len(arrays),
        out_specs=(anys,) * len(arrays),
        scratch_shapes=[pltpu.VMEM(a.shape, BF16) for a in arrays]
        + [pltpu.VMEM(a.shape, F32) for a in arrays]
        + [pltpu.SemaphoreType.DMA((2, len(arrays), pieces))],
        compiler_params=pltpu.CompilerParams(vmem_limit_bytes=63 * 2**20),
        cost_estimate=pl.CostEstimate(flops=0, bytes_accessed=6 * sum(a.size for a in arrays), transcendentals=0),
        name="widen",
    )(*arrays)


def on_device(tokens, target, mod_table, adv_table, w_up, w_down_t, bins, groups):
    rows, feat = tokens.shape
    part, hidden = w_up.shape
    depth = part * 16
    micro = bins.shape[0]
    scale = float(16 * rows) ** (-0.5)
    anys = pl.BlockSpec(memory_space=pl.ANY)
    block = (8, rows, feat)
    wblock = (8, depth // 8, hidden)
    V = pltpu.VMEM
    flops = 6 * 2 * rows * depth * hidden
    grads = pl.pallas_call(
        make_kernel(rows, feat, depth, hidden, micro, scale),
        out_shape=(
            jax.ShapeDtypeStruct((rows, feat), BF16),
            jax.ShapeDtypeStruct((part, hidden), BF16),
            jax.ShapeDtypeStruct((part, hidden), BF16),
        ),
        in_specs=[anys] * 8,
        out_specs=(anys, anys, anys),
        scratch_shapes=[
            V(block, BF16), V(block, BF16), V(wblock, BF16), V(wblock, BF16),
            V((rows, hidden), F32), V((rows, hidden), F32), V((rows, hidden), BF16), V((rows, hidden), BF16),
            V(block, BF16), V((7, rows, feat), BF16),
            V(wblock, BF16), V((8, part, hidden), BF16), V((8, part, hidden), BF16),
            V((7, part, hidden), BF16), V((7, part, hidden), BF16),
            V((8, feat), F32),
            pltpu.SMEM(bins.shape, jnp.int32), pltpu.SMEM(groups.shape, jnp.int32),
            V((rows, feat), BF16), V(mod_table.shape, BF16), V(adv_table.shape[::-1], F32),
            V((rows, feat), BF16), V((rows, feat), F32), V((rows, feat), BF16), V((part, hidden), BF16), V((part, hidden), BF16),
            pltpu.SemaphoreType.DMA((len(SENDS),)),
            pltpu.SemaphoreType.DMA((RECEIVES,)),
            pltpu.SemaphoreType.DMA((20,)),
            pltpu.SemaphoreType.DMA((11,)),
        ],
        compiler_params=pltpu.CompilerParams(
            collective_id=0, has_side_effects=True, vmem_limit_bytes=63 * 2**20
        ),
        cost_estimate=pl.CostEstimate(flops=flops, bytes_accessed=8 * 2**20, transcendentals=2 * rows * hidden),
        name="block_gradient",
    )(tokens, target, mod_table, adv_table.T, bins, groups, w_up, w_down_t)
    return widen(*grads)


def solution(mesh):
    return jax.shard_map(
        on_device,
        mesh=mesh,
        in_specs=(
            P("wide", "node"),
            P("wide", "node"),
            P(None, "node"),
            P(),
            P("wide", "node"),
            P("wide", "node"),
            P("wide"),
            P("wide"),
        ),
        out_specs=(P("wide", "node"), P("wide", "node"), P("wide", "node")),
        check_vma=False,
    )
```

```python
import jax
import jax.numpy as jnp
from jax import lax
from jax.experimental import pallas as pl
from jax.experimental.pallas import tpu as pltpu
from jax.sharding import PartitionSpec as P

F32 = jnp.float32
BF16 = jnp.bfloat16
MESH = pl.DeviceIdType.MESH
COEF = 0.7978845608028654


def dot_nn(a, b):
    return jnp.dot(a, b, preferred_element_type=F32)


def dot_nt(a, b):
    return lax.dot_general(a, b, (((1,), (1,)), ((), ())), preferred_element_type=F32)


def dot_tn(a, b):
    return lax.dot_general(a, b, (((0,), (0,)), ((), ())), preferred_element_type=F32)


def gelu_slope(v):
    th = jnp.tanh(COEF * (v + 0.044715 * v * v * v))
    return 0.5 * (1.0 + th) + 0.5 * v * (1.0 - th * th) * COEF * (1.0 + 3 * 0.044715 * v * v)


def tiles(rows, size, body):
    @pl.loop(0, rows // size)
    def _(t):
        body(pl.ds(pl.multiple_of(t * size, size), size))


def make_kernel(rows, feat, depth, hidden, micro, scale):
    seq = rows // micro

    def kernel(
        tok_in, tgt_in, mod_in, adv_in, bins_in, grps_in, wu_in, wd_in,
        gt_out, gu_out, gd_out,
        X, Y, Wu, Wd, pre, dh, hid, dpre, SB, RB, SGD, SIBD, SIBU, RGD, RGU, gain,
        bins, grps, tok, mod, adv, tgt, dpred, gt, gu, gd, ss, rs, cs, ls,
    ):
        SGU = Wd
        wi, ni = lax.axis_index("wide"), lax.axis_index("node")
        xh, z, c = wi // 8, (wi // 2) % 4, wi % 2
        xl, y = ni // 4, ni % 4

        def nd(dx, dy):
            return ((xl + dx) % 2) * 4 + (y + dy + 4) % 4

        def wm(dx, dz):
            return ((xh + dx) % 2) * 4 + (z + dz + 4) % 4

        def dnode(dx, dy):
            return (wi, nd(dx, dy))

        def dwide(dx, dz):
            return (wm(dx, dz) * 2 + c, ni)

        sib = (wm(0, 0) * 2 + 1 - c, ni)

        table = {}
        slots = {}

        def slot(key):
            return slots.setdefault(key, len(slots))

        def add(name, src, dst, got, dev):
            table[name] = (src, dst, got, dev)

        def start(*names):
            for name in names:
                src, dst, _, dev = table[name]
                pltpu.make_async_remote_copy(
                    src_ref=src,
                    dst_ref=dst,
                    send_sem=ss.at[SENDS.index(name[0])],
                    recv_sem=rs.at[slot(together(name))],
                    device_id=dev,
                    device_id_type=MESH,
                ).start()

        def bytes_of(ref, send, receive):
            return pltpu.make_async_remote_copy(
                src_ref=ref, dst_ref=ref, send_sem=ss.at[send], recv_sem=rs.at[receive], device_id=sib, device_id_type=MESH
            )

        def recv(*names):
            groups = {}
            for name in names:
                groups.setdefault(together(name), []).append(name)
            for key, members in groups.items():
                assert len(members) == sum(together(name) == key for name in table), key
                got = table[members[0]][2]
                if len(members) > 1:
                    n = sum(table[name][2].shape[0] for name in members)
                    if members[0][0] in "UDGH":
                        got = RGD.at[0]
                        assert n == part
                    elif n <= rows:
                        got = RB.at[0, pl.ds(0, n)]
                    else:
                        got = RB.at[pl.ds(0, n // half), H1]
                bytes_of(got, 0, slot(key)).wait_recv()

        def sent(*prefixes):
            for p in prefixes:
                bytes_of(RGD if p in "UDGH" else RB, SENDS.index(p), 0).wait_send()

        def shared(*prefixes):
            for p in prefixes:
                bytes_of(SIBD, SENDS.index(p.lower()), 0).wait_send()

        part = depth // 16
        mine, other = pl.multiple_of(c * part, part), pl.multiple_of((1 - c) * part, part)
        PC, PS = pl.ds(mine, part), pl.ds(other, part)
        Q1 = pl.ds(mine, part // 2)
        Q2 = pl.ds(pl.multiple_of(mine + part // 2, part // 2), part // 2)
        W = pl.ds(0, rows)
        half = rows // 2
        H1, H2 = pl.ds(0, half), pl.ds(half, half)
        K = [pl.ds(i * (half // 2), half // 2) for i in range(4)]
        eighth = half // 4
        T1, T2 = pl.ds(half - eighth, eighth), pl.ds(rows - eighth, eighth)
        L1, L2 = pl.ds(0, half - eighth), pl.ds(half, half - eighth)

        def add_ag(p, B, fewer):
            def one(name, blk, r, got, dev):
                add(p + name, B.at[blk, r], B.at[blk, r], B.at[got, r], dev)

            for i, rp, rm in (("1", K[0], K[2]), ("2", K[1], K[3]), ("3", H2, H1)):
                one("yp" + i, nd(0, 0), rp, nd(0, -1), dnode(0, 1))
                one("ym" + i, nd(0, 0), rm, nd(0, 1), dnode(0, -1))
            for i, r in (("1", H1), ("2", H2)):
                if fewer:
                    one("x" + i, nd(0, 0), r, nd(1, 0), dnode(1, 0))
                b = L2 if i == "2" and not fewer else r
                one("bp" + i, nd(1, 0), b, nd(1, -1), dnode(0, 1))
                one("bm" + i, nd(1, 0), b, nd(1, 1), dnode(0, -1))
            if not fewer:
                for i, r in (("1", K[0]), ("2", K[2]), ("3", K[1]), ("4", K[3])):
                    one("x" + i, nd(0, 0), r, nd(1, 0), dnode(1, 0))
                one("tp", nd(0, -1), T2, nd(1, -1), dnode(1, 0))
                one("tm", nd(0, 1), T2, nd(1, 1), dnode(1, 0))
            for i, rp, rm in (("1", K[0], K[2]), ("2", K[1], K[3])):
                one("cp" + i, nd(0, -1), rp, nd(0, 2), dnode(0, 1))
                one("cm" + i, nd(0, 1), rm, nd(0, 2), dnode(0, -1))
                one("dp" + i, nd(0, 2), rp, nd(1, 2), dnode(1, 0))
                if not fewer:
                    one("dm" + i, nd(0, 2), rm, nd(1, 2), dnode(1, 0))
            if fewer:
                one("ep", nd(1, -1), K[2], nd(1, 2), dnode(0, 1))
                one("em", nd(1, 1), K[3], nd(1, 2), dnode(0, -1))

        def add_wag(p, B, b0):
            def one(name, blk, r, got, dev):
                add(p + name, B.at[blk, r], B.at[blk, r], B.at[got, r], dev)

            one("x", wm(0, 0), PC, wm(1, 0), dwide(1, 0))
            for i, b in ((0, b0), (1, 1 - b0)):
                here, up, down, far = (b * 4 + (z + d) % 4 for d in (0, 1, 3, 2))
                one(f"zp{i}", here, Q1, down, dwide(0, 1))
                one(f"zm{i}", here, Q2, up, dwide(0, -1))
                one(f"yp{i}", here, Q2, down, dwide(0, 1))
                one(f"ym{i}", here, Q1, up, dwide(0, -1))
                one(f"cp{i}", down, Q1, far, dwide(0, 1))
                one(f"cm{i}", up, Q2, far, dwide(0, -1))
            def share(b):
                column = jnp.where(b // 4 == b0, 0, 1)
                return pltpu.make_async_remote_copy(
                    src_ref=B.at[b, PC],
                    dst_ref=B.at[b, PC],
                    send_sem=ss.at[SENDS.index(p.lower())],
                    recv_sem=cs.at[(0 if p == "U" else 2) + column],
                    device_id=sib,
                    device_id_type=MESH,
                )

            def column_shared(i):
                ref = SIBD.at[pl.ds(0, 4)]
                pltpu.make_async_remote_copy(
                    src_ref=ref,
                    dst_ref=ref,
                    send_sem=ss.at[0],
                    recv_sem=cs.at[(0 if p == "U" else 2) + i],
                    device_id=sib,
                    device_id_type=MESH,
                ).wait_recv()

            return share, column_shared

        def add_rs(p, R):
            def one(name, blk, r, slot, dev):
                add(p + name, SB.at[blk, r], R.at[slot, r], R.at[slot, r], dev)

            for i, r in (("1", H1), ("2", H2)):
                one("x" + i, nd(1, 2), r, 0, dnode(1, 0))
                one("bp" + i, nd(1, 1), L1 if i == "1" and p == "P" else r, 2, dnode(0, 1))
                one("bm" + i, nd(1, -1), L2 if i == "2" and p == "P" else r, 3, dnode(0, -1))
            if p == "P":
                one("tp", nd(1, 1), T1, 2, dnode(1, 0))
                one("tm", nd(1, -1), T2, 3, dnode(1, 0))
            one("ax1", nd(1, 0), H1, 4, dnode(1, 0))
            one("ax2", nd(1, 0), H2, 4, dnode(1, 0))
            for i, rp, rm in (("1", K[0], K[2]), ("2", K[1], K[3])):
                one("cp" + i, nd(0, 2), rp, 1, dnode(0, 1))
                one("cm" + i, nd(0, 2), rm, 1, dnode(0, -1))
            for i, rp, rm in (("1", K[0], K[2]), ("2", K[1], K[3]), ("3", H2, H1)):
                one("ap" + i, nd(0, 1), rp, 5, dnode(0, 1))
                one("am" + i, nd(0, -1), rm, 6, dnode(0, -1))

        A1, A2 = pl.ds(0, part // 2), pl.ds(part // 2, part // 2)
        AW = pl.ds(0, part)

        def add_wrs(p, S, R, B, b0):
            def one(name, blk, r, slot, rr, dev):
                add(p + name, S.at[blk, r], R.at[slot, rr], R.at[slot, rr], dev)

            one("xa", wm(1, 0), Q1, 6, A1, dwide(1, 0))
            one("xb", wm(1, 0), Q2, 6, A2, dwide(1, 0))
            for i, b in ((0, b0), (1, 1 - b0)):
                up, down, far = (b * 4 + (z + d) % 4 for d in (1, 3, 2))
                one(f"cp{i}", far, Q1, i, A1, dwide(0, 1))
                one(f"cm{i}", far, Q2, i, A2, dwide(0, -1))
                for h, r, a in (("a", Q1, A1), ("b", Q2, A2)):
                    one(f"ap{i}{h}", up, r, 2 + 2 * i, a, dwide(0, 1))
                    one(f"am{i}{h}", down, r, 3 + 2 * i, a, dwide(0, -1))
            base = 4 if p == "G" else 12

            def share(b):
                return pltpu.make_async_remote_copy(
                    src_ref=S.at[b, PS],
                    dst_ref=B.at[b],
                    send_sem=ss.at[SENDS.index(p.lower())],
                    recv_sem=cs.at[base + b],
                    device_id=sib,
                    device_id_type=MESH,
                )

            return share

        add_ag("X", X, True)
        add_ag("Y", Y, False)
        share_u, column_u = add_wag("U", Wu, xh)
        share_d, column_d = add_wag("D", Wd, 1 - xl)
        add_rs("P", RB)
        add_rs("M", RB)
        sib_d = add_wrs("G", SGD, RGD, SIBD, xl)
        sib_u = add_wrs("H", SGU, RGU, SIBU, xl)

        barrier = pltpu.get_barrier_semaphore()
        for dev in (dnode(1, 0), dnode(0, 1), dnode(0, -1), dwide(1, 0), dwide(0, 1), dwide(0, -1), sib):
            pl.semaphore_signal(barrier, inc=1, device_id=dev, device_id_type=MESH)
        lu = pltpu.make_async_copy(wu_in, Wu.at[wm(0, 0), PC], ls.at[0])
        ld = pltpu.make_async_copy(wd_in, Wd.at[wm(0, 0), PC], ls.at[1])
        lt = pltpu.make_async_copy(tgt_in, tgt, ls.at[2])
        lk = pltpu.make_async_copy(tok_in, tok, ls.at[6])
        lm = pltpu.make_async_copy(mod_in, mod, ls.at[7])
        la = pltpu.make_async_copy(adv_in, adv, ls.at[8])
        lb = pltpu.make_async_copy(bins_in, bins, ls.at[9])
        lg = pltpu.make_async_copy(grps_in, grps, ls.at[10])
        lb.start()
        lg.start()
        lm.start()
        lk.start()
        la.start()
        lu.start()
        ld.start()
        lt.start()

        def back(src, dst, i):
            return pltpu.make_async_copy(src, dst, ls.at[3 + i])

        ng, nb = adv.shape
        lb.wait()
        lg.wait()
        lm.wait()
        lk.wait()
        row_i = lax.broadcasted_iota(jnp.int32, (nb, feat), 0)
        for s in range(micro):
            picked = jnp.sum(jnp.where(row_i == bins[s], mod[...].astype(F32), 0.0), axis=0, keepdims=True)
            gain[s : s + 1, :] = 1.0 + picked

            def modulate(r, s=s):
                q = pl.ds(pl.multiple_of(r.start + s * seq, 32), r.size)
                X[nd(0, 0), q, :] = (tok[q, :].astype(F32) * gain[s : s + 1, :]).astype(BF16)

            tiles(seq, 32, modulate)
        lu.wait()
        ld.wait()
        pl.semaphore_wait(barrier, 7)

        def ring_start(p, i):
            start(f"{p}zp{i}", f"{p}zm{i}", f"{p}yp{i}", f"{p}ym{i}")

        def ring_relay(p, i):
            recv(f"{p}zp{i}")
            start(f"{p}cp{i}")
            recv(f"{p}zm{i}")
            start(f"{p}cm{i}")

        def ring_share(p, i, b, share):
            recv(f"{p}yp{i}")
            share(b * 4 + (z + 3) % 4).start()
            recv(f"{p}ym{i}")
            share(b * 4 + (z + 1) % 4).start()

        def ring_end(p, i, b, share):
            recv(f"{p}cp{i}", f"{p}cm{i}")
            share(b * 4 + (z + 2) % 4).start()

        same = xh == xl
        start("Xyp1", "Xym1", "Xyp2", "Xym2", "Ux")
        ring_start("U", 0)
        start("Xyp3", "Xym3")
        share_u(wm(0, 0)).start()
        share_d(wm(0, 0)).start()

        @pl.when(~same)
        def _():
            start("Dx")

        start("Xx2")

        @pl.when(same)
        def _():
            start("Dx")

        start("Xx1")

        def zero(r):
            pre[r, :] = jnp.zeros((r.size, hidden), F32)
            dh[r, :] = jnp.zeros((r.size, hidden), F32)

        tiles(rows, 32, zero)
        ring_relay("U", 0)
        def far_relay(p):
            for d in ("p1", "m1", "p2", "m2"):
                recv(p + "y" + d)
                start(p + "c" + d)

        far_relay("X")
        recv("Ux")
        ring_start("U", 1)
        share_u(wm(1, 0)).start()
        ring_share("U", 0, xh, share_u)
        ring_end("U", 0, xh, share_u)
        ring_relay("U", 1)

        @pl.when(same)
        def _():
            recv("Dx")
            share_d(wm(1, 0)).start()

        ring_start("D", 0)
        recv("Xx2")
        start("Xbp2", "Xbm2")
        recv("Xcp1", "Xcp2")
        start("Xdp1", "Xdp2")
        recv("Xcm1", "Xcm2")
        ring_share("U", 1, 1 - xh, share_u)
        ring_end("U", 1, 1 - xh, share_u)
        recv("Xyp3", "Xym3")

        column_u(0)
        column_u(1)

        def arrival(k):
            dx = jnp.where((k == 3) | (k >= 5), 1, 0)
            dy = jnp.where((k == 1) | (k == 5), 1, jnp.where((k == 2) | (k == 6), 3, jnp.where((k == 4) | (k == 7), 2, 0)))
            return ((xl + dx) % 2) * 4 + (y + dy) % 4

        @pl.loop(0, 5)
        def _(k):
            @pl.when(k == 1)
            def _():
                recv("Xbp2")
                start("Xep")
                recv("Xbm2")
                start("Xem")
                recv("Xx1")
                start("Xbp1", "Xbm1")

            @pl.when(k == 2)
            def _():
                ring_relay("D", 0)

            n = arrival(k)
            pre[...] += dot_nn(X[n], Wu[n])

        ring_share("D", 0, 1 - xl, share_d)

        @pl.when(~same)
        def _():
            recv("Dx")
            share_d(wm(1, 0)).start()

        ring_start("D", 1)

        def forward(i, r):
            if i == "1":
                recv("Xbp1", "Xbm1", "Xdp1", "Xdp2")
            else:
                recv("Xep", "Xem")

            @pl.loop(5, 8)
            def _(k):
                n = arrival(k)
                pre[r] += dot_nn(X[n, r], Wu[n])

            def activate(t):
                q = pl.ds(pl.multiple_of(t.start + r.start, 32), t.size)
                hid[q, :] = jax.nn.gelu(pre[q, :], approximate=True).astype(BF16)

            if i == "2":
                ring_end("D", 0, 1 - xl, share_d)
            tiles(r.size, 32, activate)
            if i == "2":
                column_d(0)
            products("P", hid, Wd, 0, 3, r)

        def departure(k):
            dx = jnp.where(k <= 3, 1, 0)
            dy = jnp.where((k == 0) | (k == 4), 2, jnp.where((k == 1) | (k == 5), 1, jnp.where((k == 2) | (k == 6), 3, 0)))
            return ((xl + dx) % 2) * 4 + (y + dy) % 4

        def products(p, left, weight, first, last, r=W):
            @pl.loop(first, last)
            def _(k):
                n = departure(k)
                SB[n, r] = dot_nt(left[r], weight[n]).astype(BF16)
                for at, name in ((0, "x"), (1, "bp"), (2, "bm")):
                    if first <= at < last:

                        @pl.when(k == at)
                        def _(name=name):
                            if r.start == 0:
                                start(p + name + "1")
                                if p == "P" and name != "x":
                                    start(p + "t" + name[1])
                            if r.start + r.size == rows:
                                start(p + name + "2")

                for at, name in ((5, "ap3"), (6, "am3")):
                    if first <= at < last:

                        @pl.when(k == at)
                        def _(name=name):
                            start(p + name)

        def plus(blk, r0, size, R, *slots):
            def body(r):
                q = pl.ds(pl.multiple_of(r.start + r0, 32), r.size)
                v = SB[blk, q, :].astype(F32)
                for slot in slots:
                    v = v + R[slot, q, :].astype(F32)
                SB[blk, q, :] = v.astype(BF16)

            tiles(size, 32, body)

        def rs_first(p, R, order):
            for i in order:
                recv(p + "x" + i)
                plus(nd(0, 2), half * (int(i) - 1), half, R, 0)
                d = "cp" if i == "1" else "cm"
                start(p + d + "1", p + d + "2")

        def rs_second(p, R, order):
            for i in order:
                recv(p + "bp" + i, p + "bm" + i)
                if p == "P":
                    low, last = (L1, T1) if i == "1" else (L2, T2)
                    plus(nd(1, 0), low.start, low.size, R, 2, 3)
                    plus(nd(1, 0), last.start, last.size, R, 3 if i == "1" else 2)
                else:
                    plus(nd(1, 0), half * (int(i) - 1), half, R, 2, 3)
                start(p + "ax" + i)

        def rs_third(p, R):
            for i, r in ((1, 0), (2, 1)):
                recv(f"{p}cp{i}")
                plus(nd(0, 1), K[r].start, half // 2, R, 1)
                if p == "P" and i == 2:
                    recv("Ptp")
                    plus(nd(0, 1), T1.start, eighth, R, 2)
                start(f"{p}ap{i}")
                recv(f"{p}cm{i}")
                plus(nd(0, -1), K[r + 2].start, half // 2, R, 1)
                if p == "P" and i == 2:
                    recv("Ptm")
                    plus(nd(0, -1), T2.start, eighth, R, 3)
                start(f"{p}am{i}")

        def rs_end(p, i):
            if i == 1:
                recv(p + "ax1", p + "ax2", p + "ap3", p + "am3")
            recv(f"{p}ap{i}", f"{p}am{i}")

        forward("2", H2)
        ring_relay("D", 1)
        forward("1", H1)
        products("P", hid, Wd, 3, 4)
        ring_share("D", 1, xl, share_d)
        ring_end("D", 1, xl, share_d)
        column_d(1)
        products("P", hid, Wd, 4, 5)
        rs_first("P", RB, "2")
        products("P", hid, Wd, 5, 8)
        rs_first("P", RB, "1")
        rs_second("P", RB, "21")
        rs_third("P", RB)
        rs_end("P", 1)
        lt.wait()
        la.wait()

        def total(R, q):
            v = SB[nd(0, 0), q, :].astype(F32) + R[4, q, :].astype(F32)
            return v + R[5, q, :].astype(F32) + R[6, q, :].astype(F32)

        bin_i = lax.broadcasted_iota(jnp.int32, (ng, nb), 1)
        grp_i = lax.broadcasted_iota(jnp.int32, (ng, nb), 0)
        weight = []
        for s in range(micro):
            chosen = jnp.where((bin_i == bins[s]) & (grp_i == grps[s]), adv[...], 0.0)
            weight.append(jnp.sum(jnp.sum(chosen, axis=1, keepdims=True), axis=0, keepdims=True))

        def error(k):
            begin, end = K[k].start, K[k].start + K[k].size
            for s in range(micro):
                lo, hi = max(begin, s * seq), min(end, (s + 1) * seq)

                def body(r, s=s, lo=lo):
                    q = pl.ds(pl.multiple_of(r.start + lo, 32), r.size)
                    d = weight[s] * (tok[q, :].astype(F32) + total(RB, q) - tgt[q, :].astype(F32))
                    dpred[q, :] = d
                    Y[nd(0, 0), q, :] = d.astype(BF16)

                if lo < hi:
                    tiles(hi - lo, 32, body)

        error(0)
        error(2)
        start("Yyp1", "Yym1", "Yx1", "Yx2")
        rs_end("P", 2)
        error(1)
        error(3)
        start("Yyp2", "Yym2", "Yx3", "Yx4", "Yyp3", "Yym3")
        sent("P")

        def stage_down(m):
            SGD[m] = (dot_tn(Y[m], hid[...]) * scale).astype(BF16)
            sib_d(m).start()

        def stage_up(m):
            SGU[m] = (dot_tn(X[m], dpre[...]) * scale).astype(BF16)
            sib_u(m).start()

        def wide_plus(S, blk, slots, r0, size):
            def body(r):
                a = pl.ds(pl.multiple_of(r.start + r0, 32), r.size)
                q = pl.ds(pl.multiple_of(mine + r.start + r0, 32), r.size)
                v = S[blk, q, :].astype(F32)
                for ref, slot in slots:
                    v = v + ref[slot, a, :].astype(F32)
                S[blk, q, :] = v.astype(BF16)

            tiles(size, 32, body)

        quarter = part // 2

        def wide_first(p, i, b, S, B, share):
            m = b * 4 + (z + 2) % 4
            share(m).wait_recv()
            wide_plus(S, m, ((B, m),), 0, part)
            start(f"{p}cp{i}", f"{p}cm{i}")

        def wide_early(p, i, b, S, B, share):
            up, down = b * 4 + (z + 1) % 4, b * 4 + (z + 3) % 4
            share(up).wait_recv()
            wide_plus(S, up, ((B, up),), quarter, quarter)
            start(f"{p}ap{i}b")
            share(down).wait_recv()
            wide_plus(S, down, ((B, down),), 0, quarter)
            start(f"{p}am{i}a")

        def wide_second(p, i, b, S, B, R, share):
            up, down = b * 4 + (z + 1) % 4, b * 4 + (z + 3) % 4
            recv(f"{p}cp{i}")
            wide_plus(S, up, ((B, up), (R, i)), 0, quarter)
            start(f"{p}ap{i}a")
            recv(f"{p}cm{i}")
            wide_plus(S, down, ((B, down), (R, i)), quarter, quarter)
            start(f"{p}am{i}b")
            share(b * 4 + z).wait_recv()

        def wide_step(p, i, b, S, B, R, share):
            up, down = b * 4 + (z + 1) % 4, b * 4 + (z + 3) % 4
            recv(f"{p}cp{i}", f"{p}cm{i}")
            share(up).wait_recv()
            wide_plus(S, up, ((B, up), (R, i)), 0, quarter)
            start(f"{p}ap{i}a")
            share(down).wait_recv()
            wide_plus(S, down, ((B, down),), 0, quarter)
            start(f"{p}am{i}a")
            wide_plus(S, up, ((B, up),), quarter, quarter)
            start(f"{p}ap{i}b")
            wide_plus(S, down, ((B, down), (R, i)), quarter, quarter)
            start(f"{p}am{i}b")
            share(b * 4 + z).wait_recv()

        def wide_third(p, i, b, S, B, R):
            m = b * 4 + z
            for h, r0 in (("a", 0), ("b", quarter)):
                recv(f"{p}ap{i}{h}", f"{p}am{i}{h}")

                @pl.when(xh != b)
                def _(h=h, r0=r0):
                    wide_plus(S, m, ((B, m), (R, 2 + 2 * i), (R, 3 + 2 * i)), r0, quarter)
                    start(p + "x" + h)

        def wide_last(p, b0, S, B, R, out):
            recv(p + "xa", p + "xb")
            m = wm(0, 0)
            slot = jnp.where(xh == b0, 2, 4)

            def body(r):
                q = pl.ds(pl.multiple_of(mine + r.start, 32), r.size)
                v = S[m, q, :].astype(F32) + B[m, r, :].astype(F32)
                v = v + R[slot, r, :].astype(F32) + R[slot + 1, r, :].astype(F32)
                out[r, :] = (v + R[6, r, :].astype(F32)).astype(BF16)

            tiles(part, 32, body)

        G0 = ("G", 0, xl, SGD, SIBD)
        G1 = ("G", 1, 1 - xl, SGD, SIBD)
        U0 = ("H", 0, xl, SGU, SIBU)
        U1 = ("H", 1, 1 - xl, SGU, SIBU)

        @pl.loop(0, 5)
        def _(k):
            @pl.when(k == 1)
            def _():
                far_relay("Y")
                recv("Yx1", "Yx2", "Yx3")
                start("Ybp1", "Ybm1")
                recv("Yx4")
                start("Ybp2", "Ybm2")
                recv("Yyp3", "Yym3")
                start("Ytp", "Ytm")

            for at, ds in ((2, ("p1",)), (3, ("p2", "m1", "m2"))):

                @pl.when(k == at)
                def _(ds=ds):
                    for d in ds:
                        recv("Yc" + d)
                        start("Yd" + d)

            n = arrival(k)

            @pl.when(k != 3)
            def _():
                stage_down(n)

            @pl.when(k != 4)
            def _():
                dh[...] += dot_nn(Y[n], Wd[n])

        wide_first(*G0, sib_d)
        wide_early(*G0, sib_d)
        last = arrival(4)
        dh[...] += dot_nn(Y[last], Wd[last])
        def backward(i, r):
            late = ["Ytp", "Ytm"] if i == "2" else []
            recv(*["Y" + n + i for n in ("bp", "bm")], *["Yd" + "pm"[int(i) - 1] + j for j in "12"], *late)
            if i == "2":
                stage_down((1 - xl) * 4 + (z + 2) % 4)

            def more(first, last):
                @pl.loop(first, last)
                def _(k):
                    n = arrival(k)
                    dh[r] += dot_nn(Y[n, r], Wd[n])

            more(5, 7)
            if i == "2":
                wide_first(*G1, sib_d)
            more(7, 8)

            def slope(t):
                q = pl.ds(pl.multiple_of(t.start + r.start, 32), t.size)
                dpre[q, :] = (dh[q, :] * gelu_slope(pre[q, :])).astype(BF16)

            tiles(r.size, 32, slope)
            if i == "2":

                @pl.loop(0, 2)
                def _(k):
                    stage_up(((xl + k) % 2) * 4 + (z + 2) % 4)

            if i == "2":
                wide_first(*U0, sib_u)
                products("M", dpre, Wu, 0, 1, r)
                wide_first(*U1, sib_u)
                products("M", dpre, Wu, 1, 3, r)
            else:
                products("M", dpre, Wu, 0, 3, r)

        backward("1", H1)
        wide_second(*G0, RGD, sib_d)
        sent("D")
        shared("D")

        backward("2", H2)
        wide_third("G", 0, xl, SGD, SIBD, RGD)

        @pl.loop(0, 3)
        def _(k):
            stage_down((1 - xl) * 4 + (z + 3 + k) % 4)

        products("M", dpre, Wu, 3, 5)
        wide_early(*G1, sib_d)
        rs_second("M", RB, "1")
        rs_first("M", RB, "12")
        wide_second(*G1, RGD, sib_d)

        @pl.loop(0, 3)
        def _(k):
            stage_up(xl * 4 + (z + 3 + k) % 4)

        rs_second("M", RB, "2")
        products("M", dpre, Wu, 5, 8)
        wide_early(*U0, sib_u)
        wide_second(*U0, RGU, sib_u)

        @pl.loop(0, 3)
        def _(k):
            stage_up((1 - xl) * 4 + (z + 3 + k) % 4)

        rs_third("M", RB)
        wide_step(*U1, RGU, sib_u)
        wide_third("G", 1, 1 - xl, SGD, SIBD, RGD)
        wide_third("H", 0, xl, SGU, SIBU, RGU)
        wide_third("H", 1, 1 - xl, SGU, SIBU, RGU)
        rs_end("M", 1)
        rs_end("M", 2)
        for s in range(micro):

            def finish(r, s=s):
                q = pl.ds(pl.multiple_of(r.start + s * seq, 32), r.size)
                gt[q, :] = (dpred[q, :] + gain[s : s + 1, :] * total(RB, q)).astype(BF16)

            tiles(seq, 32, finish)
        back(gt, gt_out, 1).start()
        wide_last("G", xl, SGD, SIBD, RGD, gd)
        back(gd, gd_out, 0).start()
        wide_last("H", xl, SGU, SIBU, RGU, gu)
        back(gu, gu_out, 2).start()

        sent("X", "Y", "U", "M", "G", "H")
        shared("U", "G", "H")
        assert len(slots) == RECEIVES, len(slots)
        back(gd, gd_out, 0).wait()
        back(gt, gt_out, 1).wait()
        back(gu, gu_out, 2).wait()

    return kernel


SENDS = "XYUDPMGHudgh"


def together(name):
    p, n = name[0], name[1:]
    if n in ("yp3", "ym3"):
        return p + "y3"
    if p in "XY" and n in ("bp1", "bm1", "dp1", "dp2"):
        return p + "n1"
    if (p == "Y" and n in ("bp2", "bm2", "dm1", "dm2", "tp", "tm")) or (p == "X" and n in ("ep", "em")):
        return p + "n2"
    if p == "X" and n in ("cm1", "cm2"):
        return "Xcm"
    if p in "PM":
        if n in ("ax1", "ax2", "ap3", "am3"):
            return p + "n"
        if n[:2] in ("bp", "bm"):
            return p + "b" + n[2]
    if p in "UD" and n[:2] in ("cp", "cm"):
        return p + "c" + n[2]
    if p in "GH":
        if n[0] == "x":
            return p + "x"
        if n[0] == "a":
            return p + "a" + n[2:]
    return name


RECEIVES = 97


def widen(*arrays):
    pieces = 3

    def kernel(*refs):
        n = len(arrays)
        src, dst, inner, outer, sems = refs[:n], refs[n : 2 * n], refs[2 * n : 3 * n], refs[3 * n : 4 * n], refs[4 * n]

        def copies(i, j):
            size = arrays[i].shape[0] // pieces
            r = pl.ds(j * size, size)
            return (
                pltpu.make_async_copy(src[i].at[r], inner[i].at[r], sems.at[0, i, j]),
                pltpu.make_async_copy(outer[i].at[r], dst[i].at[r], sems.at[1, i, j]),
                r,
            )

        every = [copies(i, j) for i in range(n) for j in range(pieces)]
        for read, _, _ in every:
            read.start()
        for k, (read, write, r) in enumerate(every):
            i = k // pieces
            read.wait()

            def body(t, i=i, r=r):
                q = pl.ds(pl.multiple_of(t.start + r.start, 32), t.size)
                outer[i][q, :] = inner[i][q, :].astype(F32)

            tiles(r.size, 32, body)
            write.start()
        for _, write, _ in every:
            write.wait()

    anys = pl.BlockSpec(memory_space=pl.ANY)
    return pl.pallas_call(
        kernel,
        out_shape=tuple(jax.ShapeDtypeStruct(a.shape, F32) for a in arrays),
        in_specs=[anys] * len(arrays),
        out_specs=(anys,) * len(arrays),
        scratch_shapes=[pltpu.VMEM(a.shape, BF16) for a in arrays]
        + [pltpu.VMEM(a.shape, F32) for a in arrays]
        + [pltpu.SemaphoreType.DMA((2, len(arrays), pieces))],
        compiler_params=pltpu.CompilerParams(vmem_limit_bytes=63 * 2**20),
        cost_estimate=pl.CostEstimate(flops=0, bytes_accessed=6 * sum(a.size for a in arrays), transcendentals=0),
        name="widen",
    )(*arrays)


def on_device(tokens, target, mod_table, adv_table, w_up, w_down_t, bins, groups):
    rows, feat = tokens.shape
    part, hidden = w_up.shape
    depth = part * 16
    micro = bins.shape[0]
    scale = float(16 * rows) ** (-0.5)
    anys = pl.BlockSpec(memory_space=pl.ANY)
    block = (8, rows, feat)
    wblock = (8, depth // 8, hidden)
    V = pltpu.VMEM
    flops = 6 * 2 * rows * depth * hidden
    grads = pl.pallas_call(
        make_kernel(rows, feat, depth, hidden, micro, scale),
        out_shape=(
            jax.ShapeDtypeStruct((rows, feat), BF16),
            jax.ShapeDtypeStruct((part, hidden), BF16),
            jax.ShapeDtypeStruct((part, hidden), BF16),
        ),
        in_specs=[anys] * 8,
        out_specs=(anys, anys, anys),
        scratch_shapes=[
            V(block, BF16), V(block, BF16), V(wblock, BF16), V(wblock, BF16),
            V((rows, hidden), F32), V((rows, hidden), F32), V((rows, hidden), BF16), V((rows, hidden), BF16),
            V(block, BF16), V((7, rows, feat), BF16),
            V(wblock, BF16), V((8, part, hidden), BF16), V((8, part, hidden), BF16),
            V((7, part, hidden), BF16), V((7, part, hidden), BF16),
            V((8, feat), F32),
            pltpu.SMEM(bins.shape, jnp.int32), pltpu.SMEM(groups.shape, jnp.int32),
            V((rows, feat), BF16), V(mod_table.shape, BF16), V(adv_table.shape[::-1], F32),
            V((rows, feat), BF16), V((rows, feat), F32), V((rows, feat), BF16), V((part, hidden), BF16), V((part, hidden), BF16),
            pltpu.SemaphoreType.DMA((len(SENDS),)),
            pltpu.SemaphoreType.DMA((RECEIVES,)),
            pltpu.SemaphoreType.DMA((20,)),
            pltpu.SemaphoreType.DMA((11,)),
        ],
        compiler_params=pltpu.CompilerParams(
            collective_id=0, has_side_effects=True, vmem_limit_bytes=63 * 2**20
        ),
        cost_estimate=pl.CostEstimate(flops=flops, bytes_accessed=8 * 2**20, transcendentals=2 * rows * hidden),
        name="block_gradient",
    )(tokens, target, mod_table, adv_table.T, bins, groups, w_up, w_down_t)
    return widen(*grads)


def solution(mesh):
    return jax.shard_map(
        on_device,
        mesh=mesh,
        in_specs=(
            P("wide", "node"),
            P("wide", "node"),
            P(None, "node"),
            P(),
            P("wide", "node"),
            P("wide", "node"),
            P("wide"),
            P("wide"),
        ),
        out_specs=(P("wide", "node"), P("wide", "node"), P("wide", "node")),
        check_vma=False,
    )
```

```python
import jax
import jax.numpy as jnp
from jax import lax
from jax.experimental import pallas as pl
from jax.experimental.pallas import tpu as pltpu
from jax.sharding import PartitionSpec as P

F32 = jnp.float32
BF16 = jnp.bfloat16
MESH = pl.DeviceIdType.MESH
COEF = 0.7978845608028654


def dot_nn(a, b):
    return jnp.dot(a, b, preferred_element_type=F32)


def dot_nt(a, b):
    return lax.dot_general(a, b, (((1,), (1,)), ((), ())), preferred_element_type=F32)


def dot_tn(a, b):
    return lax.dot_general(a, b, (((0,), (0,)), ((), ())), preferred_element_type=F32)


def gelu_slope(v):
    th = jnp.tanh(COEF * (v + 0.044715 * v * v * v))
    return 0.5 * (1.0 + th) + 0.5 * v * (1.0 - th * th) * COEF * (1.0 + 3 * 0.044715 * v * v)


def tiles(rows, size, body):
    @pl.loop(0, rows // size)
    def _(t):
        body(pl.ds(pl.multiple_of(t * size, size), size))


def make_kernel(rows, feat, depth, hidden, micro, scale):
    seq = rows // micro

    def kernel(
        tok_in, tgt_in, mod_in, adv_in, bins_in, grps_in, wu_in, wd_in,
        gt_out, gu_out, gd_out,
        X, Y, Wu, Wd, pre, dh, hid, dpre, SB, RB, SGD, SIBD, SIBU, RGD, RGU, gain,
        bins, grps, tok, mod, adv, tgt, dpred, gt, gu, gd, ss, rs, cs, ls,
    ):
        SGU = Wd
        wi, ni = lax.axis_index("wide"), lax.axis_index("node")
        xh, z, c = wi // 8, (wi // 2) % 4, wi % 2
        xl, y = ni // 4, ni % 4

        def nd(dx, dy):
            return ((xl + dx) % 2) * 4 + (y + dy + 4) % 4

        def wm(dx, dz):
            return ((xh + dx) % 2) * 4 + (z + dz + 4) % 4

        def dnode(dx, dy):
            return (wi, nd(dx, dy))

        def dwide(dx, dz):
            return (wm(dx, dz) * 2 + c, ni)

        sib = (wm(0, 0) * 2 + 1 - c, ni)

        table = {}
        slots = {}

        def slot(key):
            return slots.setdefault(key, len(slots))

        def add(name, src, dst, got, dev):
            table[name] = (src, dst, got, dev)

        def start(*names):
            for name in names:
                src, dst, _, dev = table[name]
                pltpu.make_async_remote_copy(
                    src_ref=src,
                    dst_ref=dst,
                    send_sem=ss.at[SENDS.index(name[0])],
                    recv_sem=rs.at[slot(together(name))],
                    device_id=dev,
                    device_id_type=MESH,
                ).start()

        def bytes_of(ref, send, receive):
            return pltpu.make_async_remote_copy(
                src_ref=ref, dst_ref=ref, send_sem=ss.at[send], recv_sem=rs.at[receive], device_id=sib, device_id_type=MESH
            )

        def recv(*names):
            groups = {}
            for name in names:
                groups.setdefault(together(name), []).append(name)
            for key, members in groups.items():
                assert len(members) == sum(together(name) == key for name in table), key
                got = table[members[0]][2]
                if len(members) > 1:
                    n = sum(table[name][2].shape[0] for name in members)
                    if members[0][0] in "UDGH":
                        got = RGD.at[0]
                        assert n == part
                    elif n <= rows:
                        got = RB.at[0, pl.ds(0, n)]
                    else:
                        got = RB.at[pl.ds(0, n // half), H1]
                bytes_of(got, 0, slot(key)).wait_recv()

        def sent(*prefixes):
            for p in prefixes:
                bytes_of(RGD if p in "UDGH" else RB, SENDS.index(p), 0).wait_send()

        def shared(*prefixes):
            for p in prefixes:
                bytes_of(SIBD, SENDS.index(p.lower()), 0).wait_send()

        part = depth // 16
        mine, other = pl.multiple_of(c * part, part), pl.multiple_of((1 - c) * part, part)
        PC, PS = pl.ds(mine, part), pl.ds(other, part)
        Q1 = pl.ds(mine, part // 2)
        Q2 = pl.ds(pl.multiple_of(mine + part // 2, part // 2), part // 2)
        W = pl.ds(0, rows)
        half = rows // 2
        H1, H2 = pl.ds(0, half), pl.ds(half, half)
        K = [pl.ds(i * (half // 2), half // 2) for i in range(4)]
        eighth = half // 4
        T1, T2 = pl.ds(half - eighth, eighth), pl.ds(rows - eighth, eighth)
        L1, L2 = pl.ds(0, half - eighth), pl.ds(half, half - eighth)

        def add_ag(p, B, fewer):
            def one(name, blk, r, got, dev):
                add(p + name, B.at[blk, r], B.at[blk, r], B.at[got, r], dev)

            for i, rp, rm in (("1", K[0], K[2]), ("2", K[1], K[3]), ("3", H2, H1)):
                one("yp" + i, nd(0, 0), rp, nd(0, -1), dnode(0, 1))
                one("ym" + i, nd(0, 0), rm, nd(0, 1), dnode(0, -1))
            for i, r in (("1", H1), ("2", H2)):
                if fewer:
                    one("x" + i, nd(0, 0), r, nd(1, 0), dnode(1, 0))
                b = L2 if i == "2" and not fewer else r
                one("bp" + i, nd(1, 0), b, nd(1, -1), dnode(0, 1))
                one("bm" + i, nd(1, 0), b, nd(1, 1), dnode(0, -1))
            if not fewer:
                for i, r in (("1", K[0]), ("2", K[2]), ("3", K[1]), ("4", K[3])):
                    one("x" + i, nd(0, 0), r, nd(1, 0), dnode(1, 0))
                one("tp", nd(0, -1), T2, nd(1, -1), dnode(1, 0))
                one("tm", nd(0, 1), T2, nd(1, 1), dnode(1, 0))
            for i, rp, rm in (("1", K[0], K[2]), ("2", K[1], K[3])):
                one("cp" + i, nd(0, -1), rp, nd(0, 2), dnode(0, 1))
                one("cm" + i, nd(0, 1), rm, nd(0, 2), dnode(0, -1))
                one("dp" + i, nd(0, 2), rp, nd(1, 2), dnode(1, 0))
                if not fewer:
                    one("dm" + i, nd(0, 2), rm, nd(1, 2), dnode(1, 0))
            if fewer:
                one("ep", nd(1, -1), K[2], nd(1, 2), dnode(0, 1))
                one("em", nd(1, 1), K[3], nd(1, 2), dnode(0, -1))

        def add_wag(p, B, b0):
            def one(name, blk, r, got, dev):
                add(p + name, B.at[blk, r], B.at[blk, r], B.at[got, r], dev)

            one("x", wm(0, 0), PC, wm(1, 0), dwide(1, 0))
            for i, b in ((0, b0), (1, 1 - b0)):
                here, up, down, far = (b * 4 + (z + d) % 4 for d in (0, 1, 3, 2))
                one(f"zp{i}", here, Q1, down, dwide(0, 1))
                one(f"zm{i}", here, Q2, up, dwide(0, -1))
                one(f"yp{i}", here, Q2, down, dwide(0, 1))
                one(f"ym{i}", here, Q1, up, dwide(0, -1))
                one(f"cp{i}", down, Q1, far, dwide(0, 1))
                one(f"cm{i}", up, Q2, far, dwide(0, -1))
            def share(b):
                column = jnp.where(b // 4 == b0, 0, 1)
                return pltpu.make_async_remote_copy(
                    src_ref=B.at[b, PC],
                    dst_ref=B.at[b, PC],
                    send_sem=ss.at[SENDS.index(p.lower())],
                    recv_sem=cs.at[(0 if p == "U" else 2) + column],
                    device_id=sib,
                    device_id_type=MESH,
                )

            def column_shared(i):
                ref = SIBD.at[pl.ds(0, 4)]
                pltpu.make_async_remote_copy(
                    src_ref=ref,
                    dst_ref=ref,
                    send_sem=ss.at[0],
                    recv_sem=cs.at[(0 if p == "U" else 2) + i],
                    device_id=sib,
                    device_id_type=MESH,
                ).wait_recv()

            return share, column_shared

        def add_rs(p, R):
            def one(name, blk, r, slot, dev):
                add(p + name, SB.at[blk, r], R.at[slot, r], R.at[slot, r], dev)

            for i, r in (("1", H1), ("2", H2)):
                low = L1 if i == "1" else L2
                one("x" + i, nd(1, 2), low if p == "M" else r, 0, dnode(1, 0))
                one("bp" + i, nd(1, 1), low if i == "1" else r, 2, dnode(0, 1))
                one("bm" + i, nd(1, -1), low if i == "2" else r, 3, dnode(0, -1))
            if p == "M":
                one("ep", nd(1, 2), T1, 0, dnode(0, 1))
                one("em", nd(1, 2), T2, 0, dnode(0, -1))
                one("fp", nd(1, 1), T1, 2, dnode(0, 1))
                one("fm", nd(1, -1), T2, 3, dnode(0, -1))
            if p == "P":
                one("tp", nd(1, 1), T1, 2, dnode(1, 0))
                one("tm", nd(1, -1), T2, 3, dnode(1, 0))
            one("ax1", nd(1, 0), H1, 4, dnode(1, 0))
            one("ax2", nd(1, 0), H2, 4, dnode(1, 0))
            for i, rp, rm in (("1", K[0], K[2]), ("2", K[1], K[3])):
                one("cp" + i, nd(0, 2), rp, 1, dnode(0, 1))
                one("cm" + i, nd(0, 2), rm, 1, dnode(0, -1))
            for i, rp, rm in (("1", K[0], K[2]), ("2", K[1], K[3]), ("3", H2, H1)):
                one("ap" + i, nd(0, 1), rp, 5, dnode(0, 1))
                one("am" + i, nd(0, -1), rm, 6, dnode(0, -1))

        A1, A2 = pl.ds(0, part // 2), pl.ds(part // 2, part // 2)
        AW = pl.ds(0, part)

        def add_wrs(p, S, R, B, b0):
            def one(name, blk, r, slot, rr, dev):
                add(p + name, S.at[blk, r], R.at[slot, rr], R.at[slot, rr], dev)

            one("xa", wm(1, 0), Q1, 6, A1, dwide(1, 0))
            one("xb", wm(1, 0), Q2, 6, A2, dwide(1, 0))
            for i, b in ((0, b0), (1, 1 - b0)):
                up, down, far = (b * 4 + (z + d) % 4 for d in (1, 3, 2))
                one(f"cp{i}", far, Q1, i, A1, dwide(0, 1))
                one(f"cm{i}", far, Q2, i, A2, dwide(0, -1))
                for h, r, a in (("a", Q1, A1), ("b", Q2, A2)):
                    one(f"ap{i}{h}", up, r, 2 + 2 * i, a, dwide(0, 1))
                    one(f"am{i}{h}", down, r, 3 + 2 * i, a, dwide(0, -1))
            base = 4 if p == "G" else 12

            def share(b):
                return pltpu.make_async_remote_copy(
                    src_ref=S.at[b, PS],
                    dst_ref=B.at[b],
                    send_sem=ss.at[SENDS.index(p.lower())],
                    recv_sem=cs.at[base + b],
                    device_id=sib,
                    device_id_type=MESH,
                )

            return share

        add_ag("X", X, True)
        add_ag("Y", Y, False)
        share_u, column_u = add_wag("U", Wu, xh)
        share_d, column_d = add_wag("D", Wd, 1 - xl)
        add_rs("P", RB)
        add_rs("M", RB)
        sib_d = add_wrs("G", SGD, RGD, SIBD, xl)
        sib_u = add_wrs("H", SGU, RGU, SIBU, xl)

        barrier = pltpu.get_barrier_semaphore()
        for dev in (dnode(1, 0), dnode(0, 1), dnode(0, -1), dwide(1, 0), dwide(0, 1), dwide(0, -1), sib):
            pl.semaphore_signal(barrier, inc=1, device_id=dev, device_id_type=MESH)
        lu = pltpu.make_async_copy(wu_in, Wu.at[wm(0, 0), PC], ls.at[0])
        ld = pltpu.make_async_copy(wd_in, Wd.at[wm(0, 0), PC], ls.at[1])
        lt = pltpu.make_async_copy(tgt_in, tgt, ls.at[2])
        lk = pltpu.make_async_copy(tok_in, tok, ls.at[6])
        lm = pltpu.make_async_copy(mod_in, mod, ls.at[7])
        la = pltpu.make_async_copy(adv_in, adv, ls.at[8])
        lb = pltpu.make_async_copy(bins_in, bins, ls.at[9])
        lg = pltpu.make_async_copy(grps_in, grps, ls.at[10])
        lb.start()
        lg.start()
        lm.start()
        lk.start()
        la.start()
        lu.start()
        ld.start()
        lt.start()

        def back(src, dst, i):
            return pltpu.make_async_copy(src, dst, ls.at[3 + i])

        ng, nb = adv.shape
        lb.wait()
        lg.wait()
        lm.wait()
        lk.wait()
        row_i = lax.broadcasted_iota(jnp.int32, (nb, feat), 0)
        for s in range(micro):
            picked = jnp.sum(jnp.where(row_i == bins[s], mod[...].astype(F32), 0.0), axis=0, keepdims=True)
            gain[s : s + 1, :] = 1.0 + picked

            def modulate(r, s=s):
                q = pl.ds(pl.multiple_of(r.start + s * seq, 32), r.size)
                X[nd(0, 0), q, :] = (tok[q, :].astype(F32) * gain[s : s + 1, :]).astype(BF16)

            tiles(seq, 32, modulate)
        lu.wait()
        ld.wait()
        pl.semaphore_wait(barrier, 7)

        def ring_start(p, i):
            start(f"{p}zp{i}", f"{p}zm{i}", f"{p}yp{i}", f"{p}ym{i}")

        def ring_relay(p, i):
            recv(f"{p}zp{i}")
            start(f"{p}cp{i}")
            recv(f"{p}zm{i}")
            start(f"{p}cm{i}")

        def ring_share(p, i, b, share):
            recv(f"{p}yp{i}")
            share(b * 4 + (z + 3) % 4).start()
            recv(f"{p}ym{i}")
            share(b * 4 + (z + 1) % 4).start()

        def ring_end(p, i, b, share):
            recv(f"{p}cp{i}", f"{p}cm{i}")
            share(b * 4 + (z + 2) % 4).start()

        same = xh == xl
        start("Xyp1", "Xym1", "Xyp2", "Xym2", "Ux")
        ring_start("U", 0)
        start("Xyp3", "Xym3")
        share_u(wm(0, 0)).start()
        share_d(wm(0, 0)).start()

        @pl.when(~same)
        def _():
            start("Dx")

        start("Xx2")

        @pl.when(same)
        def _():
            start("Dx")

        start("Xx1")

        def zero(r):
            pre[r, :] = jnp.zeros((r.size, hidden), F32)
            dh[r, :] = jnp.zeros((r.size, hidden), F32)

        tiles(rows, 32, zero)
        ring_relay("U", 0)
        def far_relay(p):
            for d in ("p1", "m1", "p2", "m2"):
                recv(p + "y" + d)
                start(p + "c" + d)

        far_relay("X")
        recv("Ux")
        ring_start("U", 1)
        share_u(wm(1, 0)).start()
        ring_share("U", 0, xh, share_u)
        ring_end("U", 0, xh, share_u)
        ring_relay("U", 1)

        @pl.when(same)
        def _():
            recv("Dx")
            share_d(wm(1, 0)).start()

        ring_start("D", 0)
        recv("Xx2")
        start("Xbp2", "Xbm2")
        recv("Xcp1", "Xcp2")
        start("Xdp1", "Xdp2")
        recv("Xcm1", "Xcm2")
        ring_share("U", 1, 1 - xh, share_u)
        ring_end("U", 1, 1 - xh, share_u)
        recv("Xyp3", "Xym3")

        column_u(0)
        column_u(1)

        def arrival(k):
            dx = jnp.where((k == 3) | (k >= 5), 1, 0)
            dy = jnp.where((k == 1) | (k == 5), 1, jnp.where((k == 2) | (k == 6), 3, jnp.where((k == 4) | (k == 7), 2, 0)))
            return ((xl + dx) % 2) * 4 + (y + dy) % 4

        @pl.loop(0, 5)
        def _(k):
            @pl.when(k == 1)
            def _():
                recv("Xbp2")
                start("Xep")
                recv("Xbm2")
                start("Xem")
                ring_relay("D", 0)
                recv("Xx1")
                start("Xbp1", "Xbm1")

            n = arrival(k)
            pre[...] += dot_nn(X[n], Wu[n])

        ring_share("D", 0, 1 - xl, share_d)

        @pl.when(~same)
        def _():
            recv("Dx")
            share_d(wm(1, 0)).start()

        ring_start("D", 1)

        def forward(i, r):
            if i == "1":
                recv("Xbp1", "Xbm1", "Xdp1", "Xdp2")
            else:
                recv("Xep", "Xem")

            @pl.loop(5, 8)
            def _(k):
                n = arrival(k)
                pre[r] += dot_nn(X[n, r], Wu[n])

            def activate(t):
                q = pl.ds(pl.multiple_of(t.start + r.start, 32), t.size)
                hid[q, :] = jax.nn.gelu(pre[q, :], approximate=True).astype(BF16)

            if i == "2":
                ring_end("D", 0, 1 - xl, share_d)
            tiles(r.size, 32, activate)
            if i == "2":
                column_d(0)
            products("P", hid, Wd, 0, 3, r)

        def departure(k):
            dx = jnp.where(k <= 3, 1, 0)
            dy = jnp.where((k == 0) | (k == 4), 2, jnp.where((k == 1) | (k == 5), 1, jnp.where((k == 2) | (k == 6), 3, 0)))
            return ((xl + dx) % 2) * 4 + (y + dy) % 4

        def products(p, left, weight, first, last, r=W):
            @pl.loop(first, last)
            def _(k):
                n = departure(k)
                SB[n, r] = dot_nt(left[r], weight[n]).astype(BF16)
                for at, name in ((0, "x"), (1, "bp"), (2, "bm")):
                    if first <= at < last:

                        @pl.when(k == at)
                        def _(name=name):
                            if r.start == 0:
                                start(p + name + "1")
                                if p == "P" and name != "x":
                                    start(p + "t" + name[1])
                                if p == "M" and name == "x":
                                    start("Mep")
                            if r.start + r.size == rows:
                                start(p + name + "2")
                                if p == "M" and name == "x":
                                    start("Mem")

                for at, name in ((5, "ap3"), (6, "am3")):
                    if first <= at < last:

                        @pl.when(k == at)
                        def _(name=name):
                            start(p + name)

        def plus(blk, r0, size, R, *slots):
            def body(r):
                q = pl.ds(pl.multiple_of(r.start + r0, 32), r.size)
                v = SB[blk, q, :].astype(F32)
                for slot in slots:
                    v = v + R[slot, q, :].astype(F32)
                SB[blk, q, :] = v.astype(BF16)

            tiles(size, 32, body)

        def rs_first(p, R, order):
            for i in order:
                recv(p + "x" + i)
                plus(nd(0, 2), half * (int(i) - 1), half if p == "P" else half - eighth, R, 0)
                d = "cp" if i == "1" else "cm"
                start(p + d + "1", p + d + "2")

        def rs_second(p, R, order):
            for i in order:
                recv(p + "bp" + i, p + "bm" + i, *(["Mfp" if i == "1" else "Mfm"] if p == "M" else []))
                if p == "P":
                    low, last = (L1, T1) if i == "1" else (L2, T2)
                    plus(nd(1, 0), low.start, low.size, R, 2, 3)
                    plus(nd(1, 0), last.start, last.size, R, 3 if i == "1" else 2)
                else:
                    plus(nd(1, 0), half * (int(i) - 1), half, R, 2, 3)
                start(p + "ax" + i)

        def pass_on(i):
            recv("Mep" if i == "1" else "Mem")
            blk, r = (nd(1, 1), T1) if i == "1" else (nd(1, -1), T2)
            plus(blk, r.start, r.size, RB, 0)
            start("Mfp" if i == "1" else "Mfm")

        def rs_third(p, R):
            for i, r in ((1, 0), (2, 1)):
                recv(f"{p}cp{i}")
                plus(nd(0, 1), K[r].start, half // 2, R, 1)
                if p == "P" and i == 2:
                    recv("Ptp")
                    plus(nd(0, 1), T1.start, eighth, R, 2)
                start(f"{p}ap{i}")
                recv(f"{p}cm{i}")
                plus(nd(0, -1), K[r + 2].start, half // 2, R, 1)
                if p == "P" and i == 2:
                    recv("Ptm")
                    plus(nd(0, -1), T2.start, eighth, R, 3)
                start(f"{p}am{i}")

        def rs_end(p, i):
            if i == 1:
                recv(p + "ax1", p + "ax2", p + "ap3", p + "am3")
            recv(f"{p}ap{i}", f"{p}am{i}")

        forward("2", H2)
        ring_relay("D", 1)
        forward("1", H1)
        products("P", hid, Wd, 3, 4)
        ring_share("D", 1, xl, share_d)
        ring_end("D", 1, xl, share_d)
        column_d(1)
        products("P", hid, Wd, 4, 5)
        rs_first("P", RB, "2")
        products("P", hid, Wd, 5, 8)
        rs_first("P", RB, "1")
        rs_second("P", RB, "21")
        rs_third("P", RB)
        rs_end("P", 1)
        lt.wait()
        la.wait()

        def total(R, q):
            v = SB[nd(0, 0), q, :].astype(F32) + R[4, q, :].astype(F32)
            return v + R[5, q, :].astype(F32) + R[6, q, :].astype(F32)

        bin_i = lax.broadcasted_iota(jnp.int32, (ng, nb), 1)
        grp_i = lax.broadcasted_iota(jnp.int32, (ng, nb), 0)
        weight = []
        for s in range(micro):
            chosen = jnp.where((bin_i == bins[s]) & (grp_i == grps[s]), adv[...], 0.0)
            weight.append(jnp.sum(jnp.sum(chosen, axis=1, keepdims=True), axis=0, keepdims=True))

        def error(k):
            begin, end = K[k].start, K[k].start + K[k].size
            for s in range(micro):
                lo, hi = max(begin, s * seq), min(end, (s + 1) * seq)

                def body(r, s=s, lo=lo):
                    q = pl.ds(pl.multiple_of(r.start + lo, 32), r.size)
                    d = weight[s] * (tok[q, :].astype(F32) + total(RB, q) - tgt[q, :].astype(F32))
                    dpred[q, :] = d
                    Y[nd(0, 0), q, :] = d.astype(BF16)

                if lo < hi:
                    tiles(hi - lo, 32, body)

        error(0)
        error(2)
        start("Yyp1", "Yym1", "Yx1", "Yx2")
        rs_end("P", 2)
        error(1)
        error(3)
        start("Yyp2", "Yym2", "Yx3", "Yx4", "Yyp3", "Yym3")
        sent("P")

        def stage_down(m):
            SGD[m] = (dot_tn(Y[m], hid[...]) * scale).astype(BF16)
            sib_d(m).start()

        def stage_up(m):
            SGU[m] = (dot_tn(X[m], dpre[...]) * scale).astype(BF16)
            sib_u(m).start()

        def wide_plus(S, blk, slots, r0, size):
            def body(r):
                a = pl.ds(pl.multiple_of(r.start + r0, 32), r.size)
                q = pl.ds(pl.multiple_of(mine + r.start + r0, 32), r.size)
                v = S[blk, q, :].astype(F32)
                for ref, slot in slots:
                    v = v + ref[slot, a, :].astype(F32)
                S[blk, q, :] = v.astype(BF16)

            tiles(size, 32, body)

        quarter = part // 2

        def wide_first(p, i, b, S, B, share):
            m = b * 4 + (z + 2) % 4
            share(m).wait_recv()
            wide_plus(S, m, ((B, m),), 0, part)
            start(f"{p}cp{i}", f"{p}cm{i}")

        def wide_early(p, i, b, S, B, share):
            up, down = b * 4 + (z + 1) % 4, b * 4 + (z + 3) % 4
            share(up).wait_recv()
            wide_plus(S, up, ((B, up),), quarter, quarter)
            start(f"{p}ap{i}b")
            share(down).wait_recv()
            wide_plus(S, down, ((B, down),), 0, quarter)
            start(f"{p}am{i}a")

        def wide_second(p, i, b, S, B, R, share):
            up, down = b * 4 + (z + 1) % 4, b * 4 + (z + 3) % 4
            recv(f"{p}cp{i}")
            wide_plus(S, up, ((B, up), (R, i)), 0, quarter)
            start(f"{p}ap{i}a")
            recv(f"{p}cm{i}")
            wide_plus(S, down, ((B, down), (R, i)), quarter, quarter)
            start(f"{p}am{i}b")
            share(b * 4 + z).wait_recv()

        def wide_step(p, i, b, S, B, R, share):
            up, down = b * 4 + (z + 1) % 4, b * 4 + (z + 3) % 4
            recv(f"{p}cp{i}", f"{p}cm{i}")
            share(up).wait_recv()
            wide_plus(S, up, ((B, up), (R, i)), 0, quarter)
            start(f"{p}ap{i}a")
            share(down).wait_recv()
            wide_plus(S, down, ((B, down),), 0, quarter)
            start(f"{p}am{i}a")
            wide_plus(S, up, ((B, up),), quarter, quarter)
            start(f"{p}ap{i}b")
            wide_plus(S, down, ((B, down), (R, i)), quarter, quarter)
            start(f"{p}am{i}b")
            share(b * 4 + z).wait_recv()

        def wide_third(p, i, b, S, B, R):
            m = b * 4 + z
            for h, r0 in (("a", 0), ("b", quarter)):
                recv(f"{p}ap{i}{h}", f"{p}am{i}{h}")

                @pl.when(xh != b)
                def _(h=h, r0=r0):
                    wide_plus(S, m, ((B, m), (R, 2 + 2 * i), (R, 3 + 2 * i)), r0, quarter)
                    start(p + "x" + h)

        def wide_last(p, b0, S, B, R, out):
            recv(p + "xa", p + "xb")
            m = wm(0, 0)
            slot = jnp.where(xh == b0, 2, 4)

            def body(r):
                q = pl.ds(pl.multiple_of(mine + r.start, 32), r.size)
                v = S[m, q, :].astype(F32) + B[m, r, :].astype(F32)
                v = v + R[slot, r, :].astype(F32) + R[slot + 1, r, :].astype(F32)
                out[r, :] = (v + R[6, r, :].astype(F32)).astype(BF16)

            tiles(part, 32, body)

        G0 = ("G", 0, xl, SGD, SIBD)
        G1 = ("G", 1, 1 - xl, SGD, SIBD)
        U0 = ("H", 0, xl, SGU, SIBU)
        U1 = ("H", 1, 1 - xl, SGU, SIBU)

        @pl.loop(0, 5)
        def _(k):
            @pl.when(k == 1)
            def _():
                far_relay("Y")
                recv("Yx1", "Yx2", "Yx3")
                start("Ybp1", "Ybm1")
                recv("Yx4")
                start("Ybp2", "Ybm2")
                recv("Yyp3", "Yym3")
                start("Ytp", "Ytm")

            for at, ds in ((2, ("p1",)), (3, ("p2", "m1", "m2"))):

                @pl.when(k == at)
                def _(ds=ds):
                    for d in ds:
                        recv("Yc" + d)
                        start("Yd" + d)

            n = arrival(k)

            @pl.when(k != 3)
            def _():
                stage_down(n)

            @pl.when(k < 3)
            def _():
                dh[...] += dot_nn(Y[n], Wd[n])

        wide_first(*G0, sib_d)
        wide_early(*G0, sib_d)

        @pl.loop(3, 5)
        def _(k):
            n = arrival(k)
            dh[...] += dot_nn(Y[n], Wd[n])

        def backward(i, r):
            late = ["Ytp", "Ytm"] if i == "2" else []
            recv(*["Y" + n + i for n in ("bp", "bm")], *["Yd" + "pm"[int(i) - 1] + j for j in "12"], *late)
            if i == "2":
                stage_down((1 - xl) * 4 + (z + 2) % 4)

            def more(first, last):
                @pl.loop(first, last)
                def _(k):
                    n = arrival(k)
                    dh[r] += dot_nn(Y[n, r], Wd[n])

            more(5, 6)
            if i == "2":
                wide_first(*G1, sib_d)
            more(6, 8)

            def slope(t):
                q = pl.ds(pl.multiple_of(t.start + r.start, 32), t.size)
                dpre[q, :] = (dh[q, :] * gelu_slope(pre[q, :])).astype(BF16)

            tiles(r.size, 32, slope)
            if i == "2":

                @pl.loop(0, 2)
                def _(k):
                    stage_up(((xl + k) % 2) * 4 + (z + 2) % 4)

            if i == "2":
                wide_first(*U0, sib_u)
                pass_on("1")
                products("M", dpre, Wu, 0, 1, r)
                wide_first(*U1, sib_u)
                products("M", dpre, Wu, 1, 3, r)
            else:
                products("M", dpre, Wu, 0, 1, r)
                wide_second(*G0, RGD, sib_d)
                products("M", dpre, Wu, 1, 3, r)

        backward("1", H1)
        sent("D")
        shared("D")

        backward("2", H2)
        wide_third("G", 0, xl, SGD, SIBD, RGD)

        @pl.loop(0, 3)
        def _(k):
            stage_down((1 - xl) * 4 + (z + 3 + k) % 4)

        pass_on("2")
        products("M", dpre, Wu, 3, 5)
        wide_early(*G1, sib_d)
        rs_second("M", RB, "1")
        rs_first("M", RB, "12")
        wide_second(*G1, RGD, sib_d)

        @pl.loop(0, 3)
        def _(k):
            stage_up(xl * 4 + (z + 3 + k) % 4)

        rs_second("M", RB, "2")
        products("M", dpre, Wu, 5, 8)
        wide_early(*U0, sib_u)
        wide_second(*U0, RGU, sib_u)

        @pl.loop(0, 3)
        def _(k):
            stage_up((1 - xl) * 4 + (z + 3 + k) % 4)

        rs_third("M", RB)
        wide_step(*U1, RGU, sib_u)
        wide_third("G", 1, 1 - xl, SGD, SIBD, RGD)
        wide_third("H", 0, xl, SGU, SIBU, RGU)
        wide_third("H", 1, 1 - xl, SGU, SIBU, RGU)
        rs_end("M", 1)
        rs_end("M", 2)
        for s in range(micro):

            def finish(r, s=s):
                q = pl.ds(pl.multiple_of(r.start + s * seq, 32), r.size)
                gt[q, :] = (dpred[q, :] + gain[s : s + 1, :] * total(RB, q)).astype(BF16)

            tiles(seq, 32, finish)
        back(gt, gt_out, 1).start()
        wide_last("G", xl, SGD, SIBD, RGD, gd)
        back(gd, gd_out, 0).start()
        wide_last("H", xl, SGU, SIBU, RGU, gu)
        back(gu, gu_out, 2).start()

        sent("X", "Y", "U", "M", "G", "H")
        shared("U", "G", "H")
        assert len(slots) == RECEIVES, len(slots)
        back(gd, gd_out, 0).wait()
        back(gt, gt_out, 1).wait()
        back(gu, gu_out, 2).wait()

    return kernel


SENDS = "XYUDPMGHudgh"


def together(name):
    p, n = name[0], name[1:]
    if n in ("yp3", "ym3"):
        return p + "y3"
    if p in "XY" and n in ("bp1", "bm1", "dp1", "dp2"):
        return p + "n1"
    if (p == "Y" and n in ("bp2", "bm2", "dm1", "dm2", "tp", "tm")) or (p == "X" and n in ("ep", "em")):
        return p + "n2"
    if p == "X" and n in ("cm1", "cm2"):
        return "Xcm"
    if p in "PM":
        if n in ("ax1", "ax2", "ap3", "am3"):
            return p + "n"
        if n[:2] in ("bp", "bm"):
            return p + "b" + n[2]
        if n in ("fp", "fm"):
            return p + ("b1" if n == "fp" else "b2")
    if p in "UD" and n[:2] in ("cp", "cm"):
        return p + "c" + n[2]
    if p in "GH":
        if n[0] == "x":
            return p + "x"
        if n[0] == "a":
            return p + "a" + n[2:]
    return name


RECEIVES = 99


def widen(*arrays):
    pieces = 3

    def kernel(*refs):
        n = len(arrays)
        src, dst, inner, outer, sems = refs[:n], refs[n : 2 * n], refs[2 * n : 3 * n], refs[3 * n : 4 * n], refs[4 * n]

        def copies(i, j):
            size = arrays[i].shape[0] // pieces
            r = pl.ds(j * size, size)
            return (
                pltpu.make_async_copy(src[i].at[r], inner[i].at[r], sems.at[0, i, j]),
                pltpu.make_async_copy(outer[i].at[r], dst[i].at[r], sems.at[1, i, j]),
                r,
            )

        every = [copies(i, j) for i in range(n) for j in range(pieces)]
        for read, _, _ in every:
            read.start()
        for k, (read, write, r) in enumerate(every):
            i = k // pieces
            read.wait()

            def body(t, i=i, r=r):
                q = pl.ds(pl.multiple_of(t.start + r.start, 32), t.size)
                outer[i][q, :] = inner[i][q, :].astype(F32)

            tiles(r.size, 32, body)
            write.start()
        for _, write, _ in every:
            write.wait()

    anys = pl.BlockSpec(memory_space=pl.ANY)
    return pl.pallas_call(
        kernel,
        out_shape=tuple(jax.ShapeDtypeStruct(a.shape, F32) for a in arrays),
        in_specs=[anys] * len(arrays),
        out_specs=(anys,) * len(arrays),
        scratch_shapes=[pltpu.VMEM(a.shape, BF16) for a in arrays]
        + [pltpu.VMEM(a.shape, F32) for a in arrays]
        + [pltpu.SemaphoreType.DMA((2, len(arrays), pieces))],
        compiler_params=pltpu.CompilerParams(vmem_limit_bytes=63 * 2**20),
        cost_estimate=pl.CostEstimate(flops=0, bytes_accessed=6 * sum(a.size for a in arrays), transcendentals=0),
        name="widen",
    )(*arrays)


def on_device(tokens, target, mod_table, adv_table, w_up, w_down_t, bins, groups):
    rows, feat = tokens.shape
    part, hidden = w_up.shape
    depth = part * 16
    micro = bins.shape[0]
    scale = float(16 * rows) ** (-0.5)
    anys = pl.BlockSpec(memory_space=pl.ANY)
    block = (8, rows, feat)
    wblock = (8, depth // 8, hidden)
    V = pltpu.VMEM
    flops = 6 * 2 * rows * depth * hidden
    grads = pl.pallas_call(
        make_kernel(rows, feat, depth, hidden, micro, scale),
        out_shape=(
            jax.ShapeDtypeStruct((rows, feat), BF16),
            jax.ShapeDtypeStruct((part, hidden), BF16),
            jax.ShapeDtypeStruct((part, hidden), BF16),
        ),
        in_specs=[anys] * 8,
        out_specs=(anys, anys, anys),
        scratch_shapes=[
            V(block, BF16), V(block, BF16), V(wblock, BF16), V(wblock, BF16),
            V((rows, hidden), F32), V((rows, hidden), F32), V((rows, hidden), BF16), V((rows, hidden), BF16),
            V(block, BF16), V((7, rows, feat), BF16),
            V(wblock, BF16), V((8, part, hidden), BF16), V((8, part, hidden), BF16),
            V((7, part, hidden), BF16), V((7, part, hidden), BF16),
            V((8, feat), F32),
            pltpu.SMEM(bins.shape, jnp.int32), pltpu.SMEM(groups.shape, jnp.int32),
            V((rows, feat), BF16), V(mod_table.shape, BF16), V(adv_table.shape[::-1], F32),
            V((rows, feat), BF16), V((rows, feat), F32), V((rows, feat), BF16), V((part, hidden), BF16), V((part, hidden), BF16),
            pltpu.SemaphoreType.DMA((len(SENDS),)),
            pltpu.SemaphoreType.DMA((RECEIVES,)),
            pltpu.SemaphoreType.DMA((20,)),
            pltpu.SemaphoreType.DMA((11,)),
        ],
        compiler_params=pltpu.CompilerParams(
            collective_id=0, has_side_effects=True, vmem_limit_bytes=63 * 2**20
        ),
        cost_estimate=pl.CostEstimate(flops=flops, bytes_accessed=8 * 2**20, transcendentals=2 * rows * hidden),
        name="block_gradient",
    )(tokens, target, mod_table, adv_table.T, bins, groups, w_up, w_down_t)
    return widen(*grads)


def solution(mesh):
    return jax.shard_map(
        on_device,
        mesh=mesh,
        in_specs=(
            P("wide", "node"),
            P("wide", "node"),
            P(None, "node"),
            P(),
            P("wide", "node"),
            P("wide", "node"),
            P("wide"),
            P("wide"),
        ),
        out_specs=(P("wide", "node"), P("wide", "node"), P("wide", "node")),
        check_vma=False,
    )
```

```python
import jax
import jax.numpy as jnp
from jax import lax
from jax.experimental import pallas as pl
from jax.experimental.pallas import tpu as pltpu
from jax.sharding import PartitionSpec as P

F32 = jnp.float32
BF16 = jnp.bfloat16
MESH = pl.DeviceIdType.MESH
COEF = 0.7978845608028654


def dot_nn(a, b):
    return jnp.dot(a, b, preferred_element_type=F32)


def dot_nt(a, b):
    return lax.dot_general(a, b, (((1,), (1,)), ((), ())), preferred_element_type=F32)


def dot_tn(a, b):
    return lax.dot_general(a, b, (((0,), (0,)), ((), ())), preferred_element_type=F32)


def gelu_slope(v):
    th = jnp.tanh(COEF * (v + 0.044715 * v * v * v))
    return 0.5 * (1.0 + th) + 0.5 * v * (1.0 - th * th) * COEF * (1.0 + 3 * 0.044715 * v * v)


def tiles(rows, size, body):
    @pl.loop(0, rows // size)
    def _(t):
        body(pl.ds(pl.multiple_of(t * size, size), size))


def make_kernel(rows, feat, depth, hidden, micro, scale):
    seq = rows // micro

    def kernel(
        tok_in, tgt_in, mod_in, adv_in, bins_in, grps_in, wu_in, wd_in,
        gt_out, gu_out, gd_out,
        X, Y, Wu, Wd, pre, dh, hid, dpre, SB, RB, SGD, SIBD, SIBU, RGD, RGU, gain,
        bins, grps, tok, mod, adv, tgt, dpred, gt, gu, gd, ss, rs, cs, ls,
    ):
        SGU = Wd
        wi, ni = lax.axis_index("wide"), lax.axis_index("node")
        xh, z, c = wi // 8, (wi // 2) % 4, wi % 2
        xl, y = ni // 4, ni % 4

        def nd(dx, dy):
            return ((xl + dx) % 2) * 4 + (y + dy + 4) % 4

        def wm(dx, dz):
            return ((xh + dx) % 2) * 4 + (z + dz + 4) % 4

        def dnode(dx, dy):
            return (wi, nd(dx, dy))

        def dwide(dx, dz):
            return (wm(dx, dz) * 2 + c, ni)

        sib = (wm(0, 0) * 2 + 1 - c, ni)

        table = {}
        slots = {}

        def slot(key):
            return slots.setdefault(key, len(slots))

        def add(name, src, dst, got, dev):
            table[name] = (src, dst, got, dev)

        def start(*names):
            for name in names:
                src, dst, _, dev = table[name]
                pltpu.make_async_remote_copy(
                    src_ref=src,
                    dst_ref=dst,
                    send_sem=ss.at[SENDS.index(name[0])],
                    recv_sem=rs.at[slot(together(name))],
                    device_id=dev,
                    device_id_type=MESH,
                ).start()

        def bytes_of(ref, send, receive):
            return pltpu.make_async_remote_copy(
                src_ref=ref, dst_ref=ref, send_sem=ss.at[send], recv_sem=rs.at[receive], device_id=sib, device_id_type=MESH
            )

        def recv(*names):
            groups = {}
            for name in names:
                groups.setdefault(together(name), []).append(name)
            for key, members in groups.items():
                assert len(members) == sum(together(name) == key for name in table), key
                got = table[members[0]][2]
                if len(members) > 1:
                    n = sum(table[name][2].shape[0] for name in members)
                    if members[0][0] in "UDGH":
                        got = RGD.at[0]
                        assert n == part
                    elif n <= rows:
                        got = RB.at[0, pl.ds(0, n)]
                    else:
                        got = RB.at[pl.ds(0, n // half), H1]
                bytes_of(got, 0, slot(key)).wait_recv()

        def sent(*prefixes):
            for p in prefixes:
                bytes_of(RGD if p in "UDGH" else RB, SENDS.index(p), 0).wait_send()

        def shared(*prefixes):
            for p in prefixes:
                bytes_of(SIBD, SENDS.index(p.lower()), 0).wait_send()

        part = depth // 16
        mine, other = pl.multiple_of(c * part, part), pl.multiple_of((1 - c) * part, part)
        PC, PS = pl.ds(mine, part), pl.ds(other, part)
        Q1 = pl.ds(mine, part // 2)
        Q2 = pl.ds(pl.multiple_of(mine + part // 2, part // 2), part // 2)
        W = pl.ds(0, rows)
        half = rows // 2
        H1, H2 = pl.ds(0, half), pl.ds(half, half)
        K = [pl.ds(i * (half // 2), half // 2) for i in range(4)]
        eighth = half // 4
        T1, T2 = pl.ds(half - eighth, eighth), pl.ds(rows - eighth, eighth)
        L1, L2 = pl.ds(0, half - eighth), pl.ds(half, half - eighth)

        def add_ag(p, B, fewer):
            def one(name, blk, r, got, dev):
                add(p + name, B.at[blk, r], B.at[blk, r], B.at[got, r], dev)

            for i, rp, rm in (("1", K[0], K[2]), ("2", K[1], K[3]), ("3", H2, H1)):
                one("yp" + i, nd(0, 0), rp, nd(0, -1), dnode(0, 1))
                one("ym" + i, nd(0, 0), rm, nd(0, 1), dnode(0, -1))
            for i, r in (("1", H1), ("2", H2)):
                if fewer:
                    one("x" + i, nd(0, 0), r, nd(1, 0), dnode(1, 0))
                b = L2 if i == "2" and not fewer else r
                one("bp" + i, nd(1, 0), b, nd(1, -1), dnode(0, 1))
                one("bm" + i, nd(1, 0), b, nd(1, 1), dnode(0, -1))
            if not fewer:
                for i, r in (("1", K[0]), ("2", K[2]), ("3", K[1]), ("4", K[3])):
                    one("x" + i, nd(0, 0), r, nd(1, 0), dnode(1, 0))
                one("tp", nd(0, -1), T2, nd(1, -1), dnode(1, 0))
                one("tm", nd(0, 1), T2, nd(1, 1), dnode(1, 0))
            for i, rp, rm in (("1", K[0], K[2]), ("2", K[1], K[3])):
                one("cp" + i, nd(0, -1), rp, nd(0, 2), dnode(0, 1))
                one("cm" + i, nd(0, 1), rm, nd(0, 2), dnode(0, -1))
                one("dp" + i, nd(0, 2), rp, nd(1, 2), dnode(1, 0))
                if not fewer:
                    one("dm" + i, nd(0, 2), rm, nd(1, 2), dnode(1, 0))
            if fewer:
                one("ep", nd(1, -1), K[2], nd(1, 2), dnode(0, 1))
                one("em", nd(1, 1), K[3], nd(1, 2), dnode(0, -1))

        def add_wag(p, B, b0):
            def one(name, blk, r, got, dev):
                add(p + name, B.at[blk, r], B.at[blk, r], B.at[got, r], dev)

            one("x", wm(0, 0), PC, wm(1, 0), dwide(1, 0))
            for i, b in ((0, b0), (1, 1 - b0)):
                here, up, down, far = (b * 4 + (z + d) % 4 for d in (0, 1, 3, 2))
                one(f"zp{i}", here, Q1, down, dwide(0, 1))
                one(f"zm{i}", here, Q2, up, dwide(0, -1))
                one(f"yp{i}", here, Q2, down, dwide(0, 1))
                one(f"ym{i}", here, Q1, up, dwide(0, -1))
                one(f"cp{i}", down, Q1, far, dwide(0, 1))
                one(f"cm{i}", up, Q2, far, dwide(0, -1))
            def share(b):
                column = jnp.where(b // 4 == b0, 0, 1)
                return pltpu.make_async_remote_copy(
                    src_ref=B.at[b, PC],
                    dst_ref=B.at[b, PC],
                    send_sem=ss.at[SENDS.index(p.lower())],
                    recv_sem=cs.at[(0 if p == "U" else 2) + column],
                    device_id=sib,
                    device_id_type=MESH,
                )

            def column_shared(i):
                ref = SIBD.at[pl.ds(0, 4)]
                pltpu.make_async_remote_copy(
                    src_ref=ref,
                    dst_ref=ref,
                    send_sem=ss.at[0],
                    recv_sem=cs.at[(0 if p == "U" else 2) + i],
                    device_id=sib,
                    device_id_type=MESH,
                ).wait_recv()

            return share, column_shared

        def add_rs(p, R):
            def one(name, blk, r, slot, dev):
                add(p + name, SB.at[blk, r], R.at[slot, r], R.at[slot, r], dev)

            for i, r in (("1", H1), ("2", H2)):
                low = L1 if i == "1" else L2
                one("x" + i, nd(1, 2), low if p == "M" else r, 0, dnode(1, 0))
                one("bp" + i, nd(1, 1), low if i == "1" else r, 2, dnode(0, 1))
                one("bm" + i, nd(1, -1), low if i == "2" else r, 3, dnode(0, -1))
            if p == "M":
                one("ep", nd(1, 2), T1, 0, dnode(0, 1))
                one("em", nd(1, 2), T2, 0, dnode(0, -1))
                one("fp", nd(1, 1), T1, 2, dnode(0, 1))
                one("fm", nd(1, -1), T2, 3, dnode(0, -1))
            if p == "P":
                one("tp", nd(1, 1), T1, 2, dnode(1, 0))
                one("tm", nd(1, -1), T2, 3, dnode(1, 0))
            one("ax1", nd(1, 0), H1, 4, dnode(1, 0))
            one("ax2", nd(1, 0), H2, 4, dnode(1, 0))
            for i, rp, rm in (("1", K[0], K[2]), ("2", K[1], K[3])):
                one("cp" + i, nd(0, 2), rp, 1, dnode(0, 1))
                one("cm" + i, nd(0, 2), rm, 1, dnode(0, -1))
            for i, rp, rm in (("1", K[0], K[2]), ("2", K[1], K[3]), ("3", H2, H1)):
                one("ap" + i, nd(0, 1), rp, 5, dnode(0, 1))
                one("am" + i, nd(0, -1), rm, 6, dnode(0, -1))

        A1, A2 = pl.ds(0, part // 2), pl.ds(part // 2, part // 2)
        AW = pl.ds(0, part)

        def add_wrs(p, S, R, B, b0):
            def one(name, blk, r, slot, rr, dev):
                add(p + name, S.at[blk, r], R.at[slot, rr], R.at[slot, rr], dev)

            one("xa", wm(1, 0), Q1, 6, A1, dwide(1, 0))
            one("xb", wm(1, 0), Q2, 6, A2, dwide(1, 0))
            for i, b in ((0, b0), (1, 1 - b0)):
                up, down, far = (b * 4 + (z + d) % 4 for d in (1, 3, 2))
                one(f"cp{i}", far, Q1, i, A1, dwide(0, 1))
                one(f"cm{i}", far, Q2, i, A2, dwide(0, -1))
                for h, r, a in (("a", Q1, A1), ("b", Q2, A2)):
                    one(f"ap{i}{h}", up, r, 2 + 2 * i, a, dwide(0, 1))
                    one(f"am{i}{h}", down, r, 3 + 2 * i, a, dwide(0, -1))
            base = 4 if p == "G" else 12

            def share(b):
                return pltpu.make_async_remote_copy(
                    src_ref=S.at[b, PS],
                    dst_ref=B.at[b],
                    send_sem=ss.at[SENDS.index(p.lower())],
                    recv_sem=cs.at[base + b],
                    device_id=sib,
                    device_id_type=MESH,
                )

            return share

        add_ag("X", X, True)
        add_ag("Y", Y, False)
        share_u, column_u = add_wag("U", Wu, xh)
        share_d, column_d = add_wag("D", Wd, 1 - xl)
        add_rs("P", RB)
        add_rs("M", RB)
        sib_d = add_wrs("G", SGD, RGD, SIBD, xl)
        sib_u = add_wrs("H", SGU, RGU, SIBU, xl)

        barrier = pltpu.get_barrier_semaphore()
        for dev in (dnode(1, 0), dnode(0, 1), dnode(0, -1), dwide(1, 0), dwide(0, 1), dwide(0, -1), sib):
            pl.semaphore_signal(barrier, inc=1, device_id=dev, device_id_type=MESH)
        lu = pltpu.make_async_copy(wu_in, Wu.at[wm(0, 0), PC], ls.at[0])
        ld = pltpu.make_async_copy(wd_in, Wd.at[wm(0, 0), PC], ls.at[1])
        lt = pltpu.make_async_copy(tgt_in, tgt, ls.at[2])
        lk = pltpu.make_async_copy(tok_in, tok, ls.at[6])
        lm = pltpu.make_async_copy(mod_in, mod, ls.at[7])
        la = pltpu.make_async_copy(adv_in, adv, ls.at[8])
        lb = pltpu.make_async_copy(bins_in, bins, ls.at[9])
        lg = pltpu.make_async_copy(grps_in, grps, ls.at[10])
        lb.start()
        lg.start()
        lm.start()
        lk.start()
        la.start()
        lu.start()
        ld.start()
        lt.start()

        def back(src, dst, i):
            return pltpu.make_async_copy(src, dst, ls.at[3 + i])

        ng, nb = adv.shape
        lb.wait()
        lg.wait()
        lm.wait()
        lk.wait()
        row_i = lax.broadcasted_iota(jnp.int32, (nb, feat), 0)
        for s in range(micro):
            picked = jnp.sum(jnp.where(row_i == bins[s], mod[...].astype(F32), 0.0), axis=0, keepdims=True)
            gain[s : s + 1, :] = 1.0 + picked

            def modulate(r, s=s):
                q = pl.ds(pl.multiple_of(r.start + s * seq, 32), r.size)
                X[nd(0, 0), q, :] = (tok[q, :].astype(F32) * gain[s : s + 1, :]).astype(BF16)

            tiles(seq, 32, modulate)
        lu.wait()
        ld.wait()
        pl.semaphore_wait(barrier, 7)

        def ring_start(p, i):
            start(f"{p}zp{i}", f"{p}zm{i}", f"{p}yp{i}", f"{p}ym{i}")

        def ring_relay(p, i):
            recv(f"{p}zp{i}")
            start(f"{p}cp{i}")
            recv(f"{p}zm{i}")
            start(f"{p}cm{i}")

        def ring_share(p, i, b, share):
            recv(f"{p}yp{i}")
            share(b * 4 + (z + 3) % 4).start()
            recv(f"{p}ym{i}")
            share(b * 4 + (z + 1) % 4).start()

        def ring_end(p, i, b, share):
            recv(f"{p}cp{i}", f"{p}cm{i}")
            share(b * 4 + (z + 2) % 4).start()

        same = xh == xl
        start("Xyp1", "Xym1", "Xyp2", "Xym2", "Ux")
        ring_start("U", 0)
        start("Xyp3", "Xym3")
        share_u(wm(0, 0)).start()
        share_d(wm(0, 0)).start()

        @pl.when(~same)
        def _():
            start("Dx")

        start("Xx2")

        @pl.when(same)
        def _():
            start("Dx")

        start("Xx1")

        def zero(r):
            pre[r, :] = jnp.zeros((r.size, hidden), F32)
            dh[r, :] = jnp.zeros((r.size, hidden), F32)

        tiles(rows, 32, zero)
        ring_relay("U", 0)
        def far_relay(p):
            for d in ("p1", "m1", "p2", "m2"):
                recv(p + "y" + d)
                start(p + "c" + d)

        far_relay("X")
        recv("Ux")
        ring_start("U", 1)
        share_u(wm(1, 0)).start()
        ring_share("U", 0, xh, share_u)
        ring_end("U", 0, xh, share_u)
        ring_relay("U", 1)

        @pl.when(same)
        def _():
            recv("Dx")
            share_d(wm(1, 0)).start()

        ring_start("D", 0)
        recv("Xx2")
        start("Xbp2", "Xbm2")
        recv("Xcp1", "Xcp2")
        start("Xdp1", "Xdp2")
        recv("Xcm1", "Xcm2")
        ring_share("U", 1, 1 - xh, share_u)
        ring_end("U", 1, 1 - xh, share_u)
        recv("Xyp3", "Xym3")

        column_u(0)
        column_u(1)

        def arrival(k):
            dx = jnp.where((k == 3) | (k >= 5), 1, 0)
            dy = jnp.where((k == 1) | (k == 5), 1, jnp.where((k == 2) | (k == 6), 3, jnp.where((k == 4) | (k == 7), 2, 0)))
            return ((xl + dx) % 2) * 4 + (y + dy) % 4

        @pl.loop(0, 5)
        def _(k):
            @pl.when(k == 1)
            def _():
                recv("Xbp2")
                start("Xep")
                recv("Xbm2")
                start("Xem")
                ring_relay("D", 0)
                recv("Xx1")
                start("Xbp1", "Xbm1")

            n = arrival(k)
            pre[...] += dot_nn(X[n], Wu[n])

        ring_share("D", 0, 1 - xl, share_d)

        @pl.when(~same)
        def _():
            recv("Dx")
            share_d(wm(1, 0)).start()

        ring_start("D", 1)

        def forward(i, r):
            if i == "1":
                recv("Xbp1", "Xbm1", "Xdp1", "Xdp2")
            else:
                recv("Xep", "Xem")

            @pl.loop(5, 8)
            def _(k):
                n = arrival(k)
                pre[r] += dot_nn(X[n, r], Wu[n])

            def activate(t):
                q = pl.ds(pl.multiple_of(t.start + r.start, 32), t.size)
                hid[q, :] = jax.nn.gelu(pre[q, :], approximate=True).astype(BF16)

            if i == "2":
                ring_end("D", 0, 1 - xl, share_d)
            tiles(r.size, 32, activate)
            if i == "2":
                column_d(0)
            products("P", hid, Wd, 0, 3, r)

        def departure(k):
            dx = jnp.where(k <= 3, 1, 0)
            dy = jnp.where((k == 0) | (k == 4), 2, jnp.where((k == 1) | (k == 5), 1, jnp.where((k == 2) | (k == 6), 3, 0)))
            return ((xl + dx) % 2) * 4 + (y + dy) % 4

        def products(p, left, weight, first, last, r=W):
            @pl.loop(first, last)
            def _(k):
                n = departure(k)
                SB[n, r] = dot_nt(left[r], weight[n]).astype(BF16)
                for at, name in ((0, "x"), (1, "bp"), (2, "bm")):
                    if first <= at < last:

                        @pl.when(k == at)
                        def _(name=name):
                            if r.start == 0:
                                start(p + name + "1")
                                if p == "P" and name != "x":
                                    start(p + "t" + name[1])
                                if p == "M" and name == "x":
                                    start("Mep")
                            if r.start + r.size == rows:
                                start(p + name + "2")
                                if p == "M" and name == "x":
                                    start("Mem")

                for at, name in ((5, "ap3"), (6, "am3")):
                    if first <= at < last:

                        @pl.when(k == at)
                        def _(name=name):
                            start(p + name)

        def plus(blk, r0, size, R, *slots):
            def body(r):
                q = pl.ds(pl.multiple_of(r.start + r0, 32), r.size)
                v = SB[blk, q, :].astype(F32)
                for slot in slots:
                    v = v + R[slot, q, :].astype(F32)
                SB[blk, q, :] = v.astype(BF16)

            tiles(size, 32, body)

        def rs_first(p, R, order):
            for i in order:
                recv(p + "x" + i)
                plus(nd(0, 2), half * (int(i) - 1), half if p == "P" else half - eighth, R, 0)
                d = "cp" if i == "1" else "cm"
                start(p + d + "1", p + d + "2")

        def rs_second(p, R, order):
            for i in order:
                recv(p + "bp" + i, p + "bm" + i, *(["Mfp" if i == "1" else "Mfm"] if p == "M" else []))
                if p == "P":
                    low, last = (L1, T1) if i == "1" else (L2, T2)
                    plus(nd(1, 0), low.start, low.size, R, 2, 3)
                    plus(nd(1, 0), last.start, last.size, R, 3 if i == "1" else 2)
                else:
                    plus(nd(1, 0), half * (int(i) - 1), half, R, 2, 3)
                start(p + "ax" + i)

        def pass_on(i):
            recv("Mep" if i == "1" else "Mem")
            blk, r = (nd(1, 1), T1) if i == "1" else (nd(1, -1), T2)
            plus(blk, r.start, r.size, RB, 0)
            start("Mfp" if i == "1" else "Mfm")

        def rs_third(p, R):
            for i, r in ((1, 0), (2, 1)):
                recv(f"{p}cp{i}")
                plus(nd(0, 1), K[r].start, half // 2, R, 1)
                if p == "P" and i == 2:
                    recv("Ptp")
                    plus(nd(0, 1), T1.start, eighth, R, 2)
                start(f"{p}ap{i}")
                recv(f"{p}cm{i}")
                plus(nd(0, -1), K[r + 2].start, half // 2, R, 1)
                if p == "P" and i == 2:
                    recv("Ptm")
                    plus(nd(0, -1), T2.start, eighth, R, 3)
                start(f"{p}am{i}")

        def rs_end(p, i):
            if i == 1:
                recv(p + "ax1", p + "ax2", p + "ap3", p + "am3")
            recv(f"{p}ap{i}", f"{p}am{i}")

        forward("2", H2)
        ring_relay("D", 1)
        forward("1", H1)
        products("P", hid, Wd, 3, 4)
        ring_share("D", 1, xl, share_d)
        ring_end("D", 1, xl, share_d)
        column_d(1)
        products("P", hid, Wd, 4, 5)
        rs_first("P", RB, "2")
        products("P", hid, Wd, 5, 8)
        rs_first("P", RB, "1")
        rs_second("P", RB, "21")
        rs_third("P", RB)
        rs_end("P", 1)
        lt.wait()
        la.wait()

        def total(R, q):
            v = SB[nd(0, 0), q, :].astype(F32) + R[4, q, :].astype(F32)
            return v + R[5, q, :].astype(F32) + R[6, q, :].astype(F32)

        bin_i = lax.broadcasted_iota(jnp.int32, (ng, nb), 1)
        grp_i = lax.broadcasted_iota(jnp.int32, (ng, nb), 0)
        weight = []
        for s in range(micro):
            chosen = jnp.where((bin_i == bins[s]) & (grp_i == grps[s]), adv[...], 0.0)
            weight.append(jnp.sum(jnp.sum(chosen, axis=1, keepdims=True), axis=0, keepdims=True))

        def error(k):
            begin, end = K[k].start, K[k].start + K[k].size
            for s in range(micro):
                lo, hi = max(begin, s * seq), min(end, (s + 1) * seq)

                def body(r, s=s, lo=lo):
                    q = pl.ds(pl.multiple_of(r.start + lo, 32), r.size)
                    d = weight[s] * (tok[q, :].astype(F32) + total(RB, q) - tgt[q, :].astype(F32))
                    dpred[q, :] = d
                    Y[nd(0, 0), q, :] = d.astype(BF16)

                if lo < hi:
                    tiles(hi - lo, 32, body)

        error(0)
        error(2)
        start("Yyp1", "Yym1", "Yx1", "Yx2")
        rs_end("P", 2)
        error(1)
        error(3)
        start("Yyp2", "Yym2", "Yx3", "Yx4", "Yyp3", "Yym3")
        sent("P")

        def stage_down(m):
            SGD[m] = (dot_tn(Y[m], hid[...]) * scale).astype(BF16)
            sib_d(m).start()

        def stage_up(m):
            SGU[m] = (dot_tn(X[m], dpre[...]) * scale).astype(BF16)
            sib_u(m).start()

        def wide_plus(S, blk, slots, r0, size):
            def body(r):
                a = pl.ds(pl.multiple_of(r.start + r0, 32), r.size)
                q = pl.ds(pl.multiple_of(mine + r.start + r0, 32), r.size)
                v = S[blk, q, :].astype(F32)
                for ref, slot in slots:
                    v = v + ref[slot, a, :].astype(F32)
                S[blk, q, :] = v.astype(BF16)

            tiles(size, 32, body)

        quarter = part // 2

        def wide_first(p, i, b, S, B, share):
            m = b * 4 + (z + 2) % 4
            share(m).wait_recv()
            wide_plus(S, m, ((B, m),), 0, part)
            start(f"{p}cp{i}", f"{p}cm{i}")

        def wide_early(p, i, b, S, B, share):
            up, down = b * 4 + (z + 1) % 4, b * 4 + (z + 3) % 4
            share(up).wait_recv()
            wide_plus(S, up, ((B, up),), quarter, quarter)
            start(f"{p}ap{i}b")
            share(down).wait_recv()
            wide_plus(S, down, ((B, down),), 0, quarter)
            start(f"{p}am{i}a")

        def wide_second(p, i, b, S, B, R, share):
            up, down = b * 4 + (z + 1) % 4, b * 4 + (z + 3) % 4
            recv(f"{p}cp{i}")
            wide_plus(S, up, ((B, up), (R, i)), 0, quarter)
            start(f"{p}ap{i}a")
            recv(f"{p}cm{i}")
            wide_plus(S, down, ((B, down), (R, i)), quarter, quarter)
            start(f"{p}am{i}b")
            share(b * 4 + z).wait_recv()

        def wide_step(p, i, b, S, B, R, share):
            up, down = b * 4 + (z + 1) % 4, b * 4 + (z + 3) % 4
            recv(f"{p}cp{i}", f"{p}cm{i}")
            share(up).wait_recv()
            wide_plus(S, up, ((B, up), (R, i)), 0, quarter)
            start(f"{p}ap{i}a")
            share(down).wait_recv()
            wide_plus(S, down, ((B, down),), 0, quarter)
            start(f"{p}am{i}a")
            wide_plus(S, up, ((B, up),), quarter, quarter)
            start(f"{p}ap{i}b")
            wide_plus(S, down, ((B, down), (R, i)), quarter, quarter)
            start(f"{p}am{i}b")
            share(b * 4 + z).wait_recv()

        def wide_third(p, i, b, S, B, R):
            m = b * 4 + z
            for h, r0 in (("a", 0), ("b", quarter)):
                recv(f"{p}ap{i}{h}", f"{p}am{i}{h}")

                @pl.when(xh != b)
                def _(h=h, r0=r0):
                    wide_plus(S, m, ((B, m), (R, 2 + 2 * i), (R, 3 + 2 * i)), r0, quarter)
                    start(p + "x" + h)

        def wide_last(p, b0, S, B, R, out, leave):
            m = wm(0, 0)
            first = jnp.where(xh == b0, 2, 4)
            for h, r0 in (("a", 0), ("b", quarter)):
                recv(p + "x" + h)

                def body(r, r0=r0):
                    a = pl.ds(pl.multiple_of(r.start + r0, 32), r.size)
                    q = pl.ds(pl.multiple_of(mine + r.start + r0, 32), r.size)
                    v = S[m, q, :].astype(F32) + B[m, a, :].astype(F32)
                    v = v + R[first, a, :].astype(F32) + R[first + 1, a, :].astype(F32)
                    out[a, :] = (v + R[6, a, :].astype(F32)).astype(BF16)

                tiles(quarter, 32, body)
                leave[h].start()

        def leaving(src, dst, i):
            return {h: back(src.at[r], dst.at[r], i + (h == "b")) for h, r in (("a", A1), ("b", A2))}

        leave_d, leave_u = leaving(gd, gd_out, 8), leaving(gu, gu_out, 10)
        G0 = ("G", 0, xl, SGD, SIBD)
        G1 = ("G", 1, 1 - xl, SGD, SIBD)
        U0 = ("H", 0, xl, SGU, SIBU)
        U1 = ("H", 1, 1 - xl, SGU, SIBU)

        @pl.loop(0, 5)
        def _(k):
            @pl.when(k == 1)
            def _():
                far_relay("Y")
                recv("Yx1", "Yx2", "Yx3")
                start("Ybp1", "Ybm1")
                recv("Yx4")
                start("Ybp2", "Ybm2")
                recv("Yyp3", "Yym3")
                start("Ytp", "Ytm")

            for at, ds in ((2, ("p1",)), (3, ("p2", "m1", "m2"))):

                @pl.when(k == at)
                def _(ds=ds):
                    for d in ds:
                        recv("Yc" + d)
                        start("Yd" + d)

            n = arrival(k)

            @pl.when(k != 3)
            def _():
                stage_down(n)

            @pl.when(k < 3)
            def _():
                dh[...] += dot_nn(Y[n], Wd[n])

        wide_first(*G0, sib_d)
        wide_early(*G0, sib_d)

        @pl.loop(3, 5)
        def _(k):
            n = arrival(k)
            dh[...] += dot_nn(Y[n], Wd[n])

        def backward(i, r):
            late = ["Ytp", "Ytm"] if i == "2" else []
            recv(*["Y" + n + i for n in ("bp", "bm")], *["Yd" + "pm"[int(i) - 1] + j for j in "12"], *late)
            if i == "2":
                stage_down((1 - xl) * 4 + (z + 2) % 4)

            def more(first, last):
                @pl.loop(first, last)
                def _(k):
                    n = arrival(k)
                    dh[r] += dot_nn(Y[n, r], Wd[n])

            more(5, 6)
            if i == "2":
                wide_first(*G1, sib_d)
            more(6, 8)

            def slope(t):
                q = pl.ds(pl.multiple_of(t.start + r.start, 32), t.size)
                dpre[q, :] = (dh[q, :] * gelu_slope(pre[q, :])).astype(BF16)

            tiles(r.size, 32, slope)
            if i == "2":

                @pl.loop(0, 2)
                def _(k):
                    stage_up(((xl + k) % 2) * 4 + (z + 2) % 4)

            if i == "2":
                wide_first(*U0, sib_u)
                pass_on("1")
                products("M", dpre, Wu, 0, 1, r)
                wide_first(*U1, sib_u)
                products("M", dpre, Wu, 1, 3, r)
            else:
                products("M", dpre, Wu, 0, 1, r)
                wide_second(*G0, RGD, sib_d)
                products("M", dpre, Wu, 1, 3, r)

        backward("1", H1)
        sent("D")
        shared("D")

        backward("2", H2)
        wide_third("G", 0, xl, SGD, SIBD, RGD)

        @pl.loop(0, 3)
        def _(k):
            stage_down((1 - xl) * 4 + (z + 3 + k) % 4)

        pass_on("2")
        products("M", dpre, Wu, 3, 5)
        wide_early(*G1, sib_d)
        rs_second("M", RB, "1")
        rs_first("M", RB, "12")
        wide_second(*G1, RGD, sib_d)

        @pl.loop(0, 3)
        def _(k):
            stage_up(xl * 4 + (z + 3 + k) % 4)

        rs_second("M", RB, "2")
        products("M", dpre, Wu, 5, 8)
        wide_early(*U0, sib_u)
        wide_second(*U0, RGU, sib_u)

        @pl.loop(0, 3)
        def _(k):
            stage_up((1 - xl) * 4 + (z + 3 + k) % 4)

        rs_third("M", RB)
        wide_step(*U1, RGU, sib_u)
        wide_third("G", 1, 1 - xl, SGD, SIBD, RGD)
        wide_third("H", 0, xl, SGU, SIBU, RGU)
        wide_third("H", 1, 1 - xl, SGU, SIBU, RGU)
        rs_end("M", 1)
        rs_end("M", 2)
        for s in range(micro):

            def finish(r, s=s):
                q = pl.ds(pl.multiple_of(r.start + s * seq, 32), r.size)
                gt[q, :] = (dpred[q, :] + gain[s : s + 1, :] * total(RB, q)).astype(BF16)

            tiles(seq, 32, finish)
        back(gt, gt_out, 1).start()
        wide_last("G", xl, SGD, SIBD, RGD, gd, leave_d)
        wide_last("H", xl, SGU, SIBU, RGU, gu, leave_u)

        sent("X", "Y", "U", "M", "G", "H")
        shared("U", "G", "H")
        assert len(slots) == RECEIVES, len(slots)
        back(gt, gt_out, 1).wait()
        for h in "ab":
            leave_d[h].wait()
            leave_u[h].wait()

    return kernel


SENDS = "XYUDPMGHudgh"


def together(name):
    p, n = name[0], name[1:]
    if n in ("yp3", "ym3"):
        return p + "y3"
    if p in "XY" and n in ("bp1", "bm1", "dp1", "dp2"):
        return p + "n1"
    if (p == "Y" and n in ("bp2", "bm2", "dm1", "dm2", "tp", "tm")) or (p == "X" and n in ("ep", "em")):
        return p + "n2"
    if p == "X" and n in ("cm1", "cm2"):
        return "Xcm"
    if p in "PM":
        if n in ("ax1", "ax2", "ap3", "am3"):
            return p + "n"
        if n[:2] in ("bp", "bm"):
            return p + "b" + n[2]
        if n in ("fp", "fm"):
            return p + ("b1" if n == "fp" else "b2")
    if p in "UD" and n[:2] in ("cp", "cm"):
        return p + "c" + n[2]
    if p in "GH":
        if n[0] == "a":
            return p + "a" + n[2:]
    return name


RECEIVES = 101


def widen(*arrays):
    pieces = 3

    def kernel(*refs):
        n = len(arrays)
        src, dst, inner, outer, sems = refs[:n], refs[n : 2 * n], refs[2 * n : 3 * n], refs[3 * n : 4 * n], refs[4 * n]

        def copies(i, j):
            size = arrays[i].shape[0] // pieces
            r = pl.ds(j * size, size)
            return (
                pltpu.make_async_copy(src[i].at[r], inner[i].at[r], sems.at[0, i, j]),
                pltpu.make_async_copy(outer[i].at[r], dst[i].at[r], sems.at[1, i, j]),
                r,
            )

        every = [copies(i, j) for i in range(n) for j in range(pieces)]
        for read, _, _ in every:
            read.start()
        for k, (read, write, r) in enumerate(every):
            i = k // pieces
            read.wait()

            def body(t, i=i, r=r):
                q = pl.ds(pl.multiple_of(t.start + r.start, 32), t.size)
                outer[i][q, :] = inner[i][q, :].astype(F32)

            tiles(r.size, 32, body)
            write.start()
        for _, write, _ in every:
            write.wait()

    anys = pl.BlockSpec(memory_space=pl.ANY)
    return pl.pallas_call(
        kernel,
        out_shape=tuple(jax.ShapeDtypeStruct(a.shape, F32) for a in arrays),
        in_specs=[anys] * len(arrays),
        out_specs=(anys,) * len(arrays),
        scratch_shapes=[pltpu.VMEM(a.shape, BF16) for a in arrays]
        + [pltpu.VMEM(a.shape, F32) for a in arrays]
        + [pltpu.SemaphoreType.DMA((2, len(arrays), pieces))],
        compiler_params=pltpu.CompilerParams(vmem_limit_bytes=63 * 2**20),
        cost_estimate=pl.CostEstimate(flops=0, bytes_accessed=6 * sum(a.size for a in arrays), transcendentals=0),
        name="widen",
    )(*arrays)


def on_device(tokens, target, mod_table, adv_table, w_up, w_down_t, bins, groups):
    rows, feat = tokens.shape
    part, hidden = w_up.shape
    depth = part * 16
    micro = bins.shape[0]
    scale = float(16 * rows) ** (-0.5)
    anys = pl.BlockSpec(memory_space=pl.ANY)
    block = (8, rows, feat)
    wblock = (8, depth // 8, hidden)
    V = pltpu.VMEM
    flops = 6 * 2 * rows * depth * hidden
    grads = pl.pallas_call(
        make_kernel(rows, feat, depth, hidden, micro, scale),
        out_shape=(
            jax.ShapeDtypeStruct((rows, feat), BF16),
            jax.ShapeDtypeStruct((part, hidden), BF16),
            jax.ShapeDtypeStruct((part, hidden), BF16),
        ),
        in_specs=[anys] * 8,
        out_specs=(anys, anys, anys),
        scratch_shapes=[
            V(block, BF16), V(block, BF16), V(wblock, BF16), V(wblock, BF16),
            V((rows, hidden), F32), V((rows, hidden), F32), V((rows, hidden), BF16), V((rows, hidden), BF16),
            V(block, BF16), V((7, rows, feat), BF16),
            V(wblock, BF16), V((8, part, hidden), BF16), V((8, part, hidden), BF16),
            V((7, part, hidden), BF16), V((7, part, hidden), BF16),
            V((8, feat), F32),
            pltpu.SMEM(bins.shape, jnp.int32), pltpu.SMEM(groups.shape, jnp.int32),
            V((rows, feat), BF16), V(mod_table.shape, BF16), V(adv_table.shape[::-1], F32),
            V((rows, feat), BF16), V((rows, feat), F32), V((rows, feat), BF16), V((part, hidden), BF16), V((part, hidden), BF16),
            pltpu.SemaphoreType.DMA((len(SENDS),)),
            pltpu.SemaphoreType.DMA((RECEIVES,)),
            pltpu.SemaphoreType.DMA((20,)),
            pltpu.SemaphoreType.DMA((15,)),
        ],
        compiler_params=pltpu.CompilerParams(
            collective_id=0, has_side_effects=True, vmem_limit_bytes=63 * 2**20
        ),
        cost_estimate=pl.CostEstimate(flops=flops, bytes_accessed=8 * 2**20, transcendentals=2 * rows * hidden),
        name="block_gradient",
    )(tokens, target, mod_table, adv_table.T, bins, groups, w_up, w_down_t)
    return widen(*grads)


def solution(mesh):
    return jax.shard_map(
        on_device,
        mesh=mesh,
        in_specs=(
            P("wide", "node"),
            P("wide", "node"),
            P(None, "node"),
            P(),
            P("wide", "node"),
            P("wide", "node"),
            P("wide"),
            P("wide"),
        ),
        out_specs=(P("wide", "node"), P("wide", "node"), P("wide", "node")),
        check_vma=False,
    )
```
